32 devices in a mesh: row: 8 (over z, y), col: 4 (over x, core).
Axes of the slice: x: 2, y: 2, z: 4, core: 2. Of those that a mesh axis runs over, the one named last changes fastest.
Arguments:
- hidden_in: bfloat16 [8192, 2048], P('row', 'col'), may hold values from -32 to 32
- seq_lengths: int32 [8, 4], P('row'), may hold values from 1 to 512, 1024 in all within a row
- attn_norm: float32 [2048], P('col'), may hold values from 0.5 to 1.5
- w_query: bfloat16 [2048, 2048], P('row', 'col'), may hold values from -0.125 to 0.125
- key_weight: bfloat16 [2048, 1024], P('row', 'col'), may hold values from -0.125 to 0.125
- value_weight: bfloat16 [2048, 1024], P('row', 'col'), may hold values from -0.125 to 0.125
- query_norm: float32 [128], replicated, may hold values from 0.8 to 2
- key_norm: float32 [128], replicated, may hold values from 0.8 to 2
- w_output: bfloat16 [2048, 2048], P('col', 'row'), may hold values from -0.5 to 0.5
- ffwd_norm: float32 [2048], P('col'), may hold values from 0.5 to 1.5
- w_gate: bfloat16 [2048, 6144], P('row', 'col'), may hold values from -0.125 to 0.125
- w_up: bfloat16 [2048, 6144], P('row', 'col'), may hold values from -0.125 to 0.125
- w_down: bfloat16 [6144, 2048], P('col', 'row'), may hold values from -0.078125 to 0.078125
- cotangent: bfloat16 [8192, 2048], P('row', 'col'), may hold values from -6 to 6
Outputs:
- hidden_out: bfloat16 [8192, 2048], P('row', 'col')
- hidden_grad: float32 [8192, 2048], P('row', 'col')
- attn_norm_grad: float32 [2048], P('col')
- query_grad: float32 [2048, 2048], P('row', 'col')
- key_grad: float32 [2048, 1024], P('row', 'col')
- value_grad: float32 [2048, 1024], P('row', 'col')
- query_norm_grad: float32 [128], replicated
- key_norm_grad: float32 [128], replicated
- output_grad: float32 [2048, 2048], P('col', 'row')
- ffwd_norm_grad: float32 [2048], P('col')
- gate_grad: float32 [2048, 6144], P('row', 'col')
- up_grad: float32 [2048, 6144], P('row', 'col')
- down_grad: float32 [6144, 2048], P('col', 'row')
The draws below stay inside these ranges and needn't reach their ends.
Inputs may be any that keep to these rules, and one draw needn't show every extreme that they name: `seq_lengths`: each row sums to 1024 and has exactly one sequence of 512 tokens.
All inputs are finite; a program needn't handle non-finite values.
Results may differ from the reference program's by a relative error of at most 0.02.
Values may be sent and summed in bfloat16 or wider, within the bound.
No kernel may reach another device: no remote copies, remote signals or barrier semaphores. Data moves between devices by JAX's collectives and lax.ppermute only.
A program may use at most 256 MiB of HBM per device.

```python
import math
import jax
import jax.numpy as jnp
import numpy as np
from jax import lax

MODEL_WIDTH = 2048
QUERY_HEADS = 16
KEY_VALUE_HEADS = 8
HEAD_WIDTH = 128
FF = 6144
TOK_DEV = 1024
SEQ_DEV = 4
MOST = 512
TOKENS = 8192
N_ROW = 8


def draw_hidden_in(key, part):
    key = jax.random.fold_in(key, 11)
    col_key, row_key, base_key = jax.random.split(key, 3)
    col_rand = jax.random.uniform(col_key, (MODEL_WIDTH,), jnp.float32)
    ramp_up = jnp.arange(MODEL_WIDTH, dtype=jnp.float32) / MODEL_WIDTH
    col_scale = 2.0 ** (1.2 * ramp_up - 0.6 + 0.8 * (col_rand - 0.5))
    row_rand = jax.random.uniform(row_key, (TOKENS, 1), jnp.float32)
    mixed_rows = jnp.clip(jax.random.normal(base_key, (TOKENS, MODEL_WIDTH), jnp.float32), -5.0, 5.0)
    row_scale = 10.0 ** (row_rand - 0.5)
    return (mixed_rows * col_scale * row_scale).astype(jnp.bfloat16)


def levels(own_key, extent, cuts, least, high):
    def one(dim, parts):
        draws = jax.random.uniform(jax.random.fold_in(jax.random.fold_in(own_key, 6), dim), (parts,), jnp.float32, least / len(cuts), high / len(cuts))
        return jnp.repeat(jnp.exp(draws), extent[dim] // parts).reshape((-1,) + (1,) * (len(extent) - dim - 1))

    gain = one(*cuts[0])
    for cut in cuts[1:]:
        gain = gain * one(*cut)
    return gain


def profile(count, total, most, lean):
    portions = [(1 << 20) // math.isqrt(grade ** lean) + 1 for grade in range(2, count + 1)]
    spare, given = total - most - (count - 1), [1] * (count - 1)
    while spare > 0:
        free = [i for i in range(count - 1) if given[i] < most]
        pool, left = sum([portions[i] for i in free]), spare
        for i in free:
            addition = min(most - given[i], max(1, left * portions[i] // pool), spare)
            given[i] = given[i] + addition
            spare = spare - addition
    return np.array([most] + given)


def ragged(stream_key, count, total, limit, lean):
    if count == 2:
        one = jax.random.randint(stream_key, (), max(1, total - limit), min(limit, total - 1) + 1)
        return jnp.stack([one, total - one])
    sizes = jnp.asarray(profile(count, total, limit, lean), jnp.int32)
    pairs = (count - 1) // 2
    giver, receiver = sizes[1:1 + 2 * pairs:2], sizes[2:2 + 2 * pairs:2]
    slack = jnp.minimum(giver - 1, limit - receiver)
    passed = jax.random.randint(jax.random.fold_in(stream_key, 1), (pairs,), 0, 1 << 20) % (slack + 1)
    sizes = sizes.at[1:1 + 2 * pairs:2].set(giver - passed).at[2:2 + 2 * pairs:2].set(receiver + passed)
    return sizes[jax.random.permutation(jax.random.fold_in(stream_key, 2), count)]


def gaussian(stream_key, extent, deviation, most, cuts=(), kind=jnp.bfloat16):
    entries = jax.random.normal(stream_key, extent, jnp.float32) * deviation
    if len(cuts) > 0:
        entries = levels(stream_key, extent, cuts, -0.22, 0.18) * entries
    return jnp.clip(entries, min=-most, max=most).astype(kind)


def setup_inputs(seed: int = 0) -> dict:
    keys = jax.random.split(jax.random.key(seed), 15)
    hidden_in = draw_hidden_in(jax.random.fold_in(keys[14], 71), 0)
    seq_lengths = jax.vmap(lambda own: ragged(own, SEQ_DEV, TOK_DEV, MOST, 2))(jax.random.split(keys[1], N_ROW)).reshape((N_ROW, SEQ_DEV)).astype(jnp.int32)
    attn_norm = jnp.clip(1.0 + 0.1 * jax.random.normal(keys[2], (MODEL_WIDTH,), jnp.float32), 0.5, 1.5)
    w_query = gaussian(keys[3], (MODEL_WIDTH, QUERY_HEADS * HEAD_WIDTH), MODEL_WIDTH ** -0.5, 0.125, ((0, 8), (1, 4)))
    key_weight = gaussian(keys[4], (MODEL_WIDTH, KEY_VALUE_HEADS * HEAD_WIDTH), MODEL_WIDTH ** -0.5, 0.125, ((0, 8), (1, 4)))
    value_weight = gaussian(keys[5], (MODEL_WIDTH, KEY_VALUE_HEADS * HEAD_WIDTH), MODEL_WIDTH ** -0.5, 0.125, ((0, 8), (1, 4)))
    query_norm = jnp.clip(jnp.exp(jax.random.uniform(keys[6], (HEAD_WIDTH,), jnp.float32, math.log(0.8), math.log(2.0))), 0.8, 2.0)
    key_norm = jnp.clip(jnp.exp(jax.random.uniform(keys[7], (HEAD_WIDTH,), jnp.float32, math.log(0.8), math.log(2.0))), 0.8, 2.0)
    w_output = gaussian(keys[8], (QUERY_HEADS * HEAD_WIDTH, MODEL_WIDTH), (QUERY_HEADS * HEAD_WIDTH // 16) ** -0.5, 0.5, ((0, 4), (1, 8)))
    ffwd_norm = jnp.clip(1.0 + 0.1 * jax.random.normal(keys[9], (MODEL_WIDTH,), jnp.float32), 0.5, 1.5)
    w_gate = gaussian(keys[10], (MODEL_WIDTH, FF), MODEL_WIDTH ** -0.5, 0.125, ((0, 8), (1, 4)))
    w_up = gaussian(keys[11], (MODEL_WIDTH, FF), MODEL_WIDTH ** -0.5, 0.125, ((0, 8), (1, 4)))
    w_down = gaussian(keys[12], (FF, MODEL_WIDTH), FF ** -0.5, 0.078125, ((0, 4), (1, 8)))
    cotangent = gaussian(keys[13], (TOKENS, MODEL_WIDTH), 1.0, 6.0, ((0, 8), (1, 4)))
    return dict(hidden_in=hidden_in, seq_lengths=seq_lengths, attn_norm=attn_norm, w_query=w_query, key_weight=key_weight, value_weight=value_weight, query_norm=query_norm, key_norm=key_norm, w_output=w_output, ffwd_norm=ffwd_norm, w_gate=w_gate, w_up=w_up, w_down=w_down, cotangent=cotangent)


EPS = 1e-06
THETA = 1000000.0
NEGATIVE = -1e+30

@jax.custom_vjp
def lowered_forward(v):
    return lax.optimization_barrier(v.astype(jnp.bfloat16)).astype(jnp.float32)

@jax.custom_vjp
def lowered_backward(v):
    return v

def low_keep(v):
    return (lowered_forward(v), None)

def low_pass(kept, grad):
    return (grad,)

def back_keep(v):
    return (v, None)

def back_low(kept, grad):
    return (lowered_forward(grad),)
lowered_forward.defvjp(low_keep, low_pass)
lowered_backward.defvjp(back_keep, back_low)

def matrix_multiply(left_side, right_side):
    return jnp.dot(left_side, right_side, precision=lax.Precision.HIGHEST)

def rms_scale(values, gain_vec):
    return values * lax.rsqrt(lax.optimization_barrier(jnp.mean(values * values, -1, keepdims=True)) + EPS) * gain_vec

def tables(lengths_row, row_number_total):
    steps_idx = jnp.arange(row_number_total, dtype=jnp.int32)
    seq_ends = jnp.cumsum(lengths_row).astype(jnp.int32)
    seq_starts = (seq_ends - lengths_row).astype(jnp.int32)
    segment = lax.optimization_barrier(jnp.sum((steps_idx[:, None] >= seq_ends[None, :]).astype(jnp.int32), 1)).astype(jnp.int32)
    member = segment[:, None] == jnp.arange(lengths_row.shape[0], dtype=jnp.int32)[None, :]
    position = (steps_idx - lax.optimization_barrier(jnp.sum(jnp.where(member, seq_starts[None, :], 0), 1))).astype(jnp.int32)
    return (segment, position)

def rotary(position, head_size):
    half_size = head_size // 2
    frequency = THETA ** (-(jnp.arange(half_size, dtype=jnp.float32) * 2.0 / head_size))
    angles = position.astype(jnp.float32)[:, None] * frequency[None, :]
    return (jnp.cos(angles), jnp.sin(angles))

def rotate(values, cos_table, sin_table):
    half_size = values.shape[-1] // 2
    first_half = values[..., :half_size]
    second_half = values[..., half_size:]
    cos_wide = cos_table[:, None, :]
    sin_wide = sin_table[:, None, :]
    return jnp.concatenate([first_half * cos_wide - second_half * sin_wide, second_half * cos_wide + first_half * sin_wide], -1)

def layer_group(params, row_values, lengths_row):
    attn_norm, w_query, key_weight, value_weight, query_norm, key_norm, w_output, ffwd_norm, w_gate, w_up, w_down = params
    row_number_total = row_values.shape[0]
    heads_per_group = QUERY_HEADS // KEY_VALUE_HEADS
    score_factor = 1.0 / math.sqrt(HEAD_WIDTH)
    segment, position = tables(lengths_row, row_number_total)
    cos_table, sin_table = rotary(position, HEAD_WIDTH)
    steps_idx = jnp.arange(row_number_total, dtype=jnp.int32)
    input_normalized = lowered_forward(rms_scale(row_values, attn_norm))
    queries = lowered_backward(matrix_multiply(input_normalized, w_query)).reshape(row_number_total, QUERY_HEADS, HEAD_WIDTH)
    key_row_block = lowered_backward(matrix_multiply(input_normalized, key_weight)).reshape(row_number_total, KEY_VALUE_HEADS, HEAD_WIDTH)
    value_row_block = lowered_forward(lowered_backward(matrix_multiply(input_normalized, value_weight))).reshape(row_number_total, KEY_VALUE_HEADS, HEAD_WIDTH)
    query_rotated = lowered_forward(rotate(rms_scale(queries, query_norm), cos_table, sin_table))
    query_rotated = query_rotated.reshape(row_number_total, KEY_VALUE_HEADS, heads_per_group, HEAD_WIDTH)
    key_turned = lowered_forward(rotate(rms_scale(key_row_block, key_norm), cos_table, sin_table))
    allowed = (segment[:, None] == segment[None, :]) & (steps_idx[:, None] >= steps_idx[None, :])
    scores = lowered_backward(jnp.einsum('tgrd,ugd->grtu', query_rotated, key_turned, precision=lax.Precision.HIGHEST) * score_factor)
    scores = jnp.where(allowed[None, None], scores, NEGATIVE)
    row_peak = lax.optimization_barrier(jnp.max(scores, -1, keepdims=True))
    exp_scores = jnp.exp(scores - row_peak)
    prob_rows = lowered_forward(exp_scores / lax.optimization_barrier(jnp.sum(exp_scores, -1, keepdims=True)))
    mixed_out = jnp.einsum('grtu,ugd->tgrd', prob_rows, value_row_block, precision=lax.Precision.HIGHEST).reshape(row_number_total, QUERY_HEADS * HEAD_WIDTH)
    mixed_out = lowered_forward(lowered_backward(mixed_out))
    attn_out = lowered_backward(matrix_multiply(mixed_out, w_output))
    middle = row_values + attn_out
    normed_two = lowered_forward(rms_scale(middle, ffwd_norm))
    gate_pre = lowered_backward(matrix_multiply(normed_two, w_gate))
    up_pre = lowered_backward(matrix_multiply(normed_two, w_up))
    hidden = lowered_forward(jax.nn.silu(gate_pre) * up_pre)
    return middle + lowered_backward(matrix_multiply(hidden, w_down))

def reference(hidden_in, seq_lengths, attn_norm, w_query, key_weight, value_weight, query_norm, key_norm, w_output, ffwd_norm, w_gate, w_up, w_down, cotangent):
    params = tuple((weight.astype(jnp.float32) for weight in (attn_norm, w_query, key_weight, value_weight, query_norm, key_norm, w_output, ffwd_norm, w_gate, w_up, w_down)))
    rows_all = hidden_in.astype(jnp.float32)

    def forward(params_in, rows_in):
        groups = rows_in.reshape(N_ROW, TOK_DEV, MODEL_WIDTH)

        def per_group(packed):
            return layer_group(params_in, packed[0], packed[1])
        outputs = lax.map(jax.checkpoint(per_group), (groups, seq_lengths))
        return outputs.reshape(N_ROW * TOK_DEV, MODEL_WIDTH)
    out_rows, pull_back = jax.vjp(forward, params, rows_all)
    grad_params, grad_rows = pull_back(cotangent.astype(jnp.float32))
    return (out_rows.astype(jnp.bfloat16), grad_rows, grad_params[0], grad_params[1], grad_params[2], grad_params[3], grad_params[4], grad_params[5], grad_params[6], grad_params[7], grad_params[8], grad_params[9], grad_params[10])
```

```python
import math

import jax
import jax.numpy as jnp
from jax import lax
from jax.sharding import PartitionSpec as P

EPS = 1e-06
THETA = 1000000.0
NEGATIVE = -1e30


def matrix_multiply(left_side, right_side):
    return jnp.dot(left_side, right_side, preferred_element_type=jnp.float32)


def times_transposed(left_side, right_side):
    return lax.dot_general(
        left_side, right_side, (((1,), (1,)), ((), ())), preferred_element_type=jnp.float32
    )


def transposed_times(left_side, right_side):
    return lax.dot_general(
        left_side, right_side, (((0,), (0,)), ((), ())), preferred_element_type=jnp.float32
    )


def tables(lengths_row, row_number_total):
    steps_idx = jnp.arange(row_number_total, dtype=jnp.int32)
    seq_ends = jnp.cumsum(lengths_row)
    seq_starts = seq_ends - lengths_row
    segment = jnp.sum((steps_idx[:, None] >= seq_ends[None, :]).astype(jnp.int32), 1)
    member = segment[:, None] == jnp.arange(lengths_row.shape[0], dtype=jnp.int32)[None, :]
    position = steps_idx - jnp.sum(jnp.where(member, seq_starts[None, :], 0), 1)
    return (segment, position)


def rotary(position, head_size):
    half_size = head_size // 2
    frequency = THETA ** (-(jnp.arange(half_size, dtype=jnp.float32) * 2.0 / head_size))
    angles = position.astype(jnp.float32)[:, None] * frequency[None, :]
    return (jnp.cos(angles), jnp.sin(angles))


def rotate(values, cos_table, sin_table):
    half_size = values.shape[-1] // 2
    first_half = values[..., :half_size]
    second_half = values[..., half_size:]
    cos_wide = cos_table[:, None, :]
    sin_wide = sin_table[:, None, :]
    return jnp.concatenate(
        [
            first_half * cos_wide - second_half * sin_wide,
            second_half * cos_wide + first_half * sin_wide,
        ],
        -1,
    )


def head_turn(raw_rows, gain_vec, cos_table, sin_table, head_count):
    shaped = raw_rows.reshape(raw_rows.shape[0], head_count, -1)
    normed = shaped * lax.rsqrt(jnp.mean(shaped * shaped, -1, keepdims=True) + EPS) * gain_vec
    return rotate(normed, cos_table, sin_table)


def swish_product(gate_values, up_values):
    return jax.nn.silu(gate_values) * up_values


def ring_order(count):
    return list(range(0, count, 2)) + list(range(count - 1, 0, -2))


class Ring:
    def __init__(self, count):
        self.count = count
        self.half = count // 2
        order = ring_order(count)
        self.onward = [(order[i], order[(i + 1) % count]) for i in range(count)]
        self.backward = [(b, a) for a, b in self.onward]
        place_of = [order.index(r) for r in range(count)]
        behind = [[order[(place_of[r] - j) % count] for j in range(count)] for r in range(count)]
        distance = [[(place_of[r] - place_of[b]) % count for b in range(count)] for r in range(count)]
        me = lax.axis_index("row")
        self.behind = jnp.array(behind, jnp.int32)[me]
        self.distance = jnp.array(distance, jnp.int32)[me]

    def send_on(self, value):
        return lax.ppermute(value, "row", self.onward)

    def send_back(self, value):
        return lax.ppermute(value, "row", self.backward)


def after(value, *earlier):
    return lax.optimization_barrier((value,) + earlier)[0]


class Gather:
    def __init__(self, ring, block):
        self.ring, self.block = ring, block
        self.from_behind, self.from_ahead = [], []
        self.last = (block, block)

    def step(self, number, *earlier):
        ring = self.ring
        on, back = self.last
        if number == ring.half - 1:
            cut = self.block.shape[0] // 2
            on, back = on[:cut], back[cut:]
        if earlier:
            on, back = after(on, *earlier), after(back, *earlier)
        on, back = ring.send_on(on), ring.send_back(back)
        self.last = (on, back)
        if number == ring.half - 1:
            self.far = jnp.concatenate([on, back], 0)
        else:
            self.from_behind.append(on)
            self.from_ahead.append(back)

    def blocks(self):
        return [self.block] + self.from_behind + [self.far] + self.from_ahead[::-1]


class Scatter:
    def __init__(self, ring, part):
        self.ring, self.part = ring, part
        self.on = self.back = None

    def step(self, number, *earlier):
        ring = self.ring
        low = jnp.bfloat16
        if number == 0:
            whole = self.part(ring.half)
            cut = whole.shape[0] // 2
            on, back = whole[:cut].astype(low), whole[cut:].astype(low)
        else:
            on = self.part(ring.half + number)
            back = self.part(ring.half - number)
            if number == 1:
                cut = on.shape[0] // 2
                on = jnp.concatenate([on[:cut] + self.on, on[cut:]], 0)
                back = jnp.concatenate([back[:cut], back[cut:] + self.back], 0)
            else:
                on, back = on + self.on, back + self.back
            on, back = on.astype(low), back.astype(low)
        if earlier:
            on, back = after(on, *earlier), after(back, *earlier)
        self.on, self.back = ring.send_on(on), ring.send_back(back)
        self.last = (self.on, self.back)

    def total(self):
        return self.part(0) + self.on + self.back


def col_swap(value, bit):
    count = lax.axis_size("col")
    return lax.ppermute(value, "col", [(i, i ^ bit) for i in range(count)])


def spread(values):
    far = col_swap(values, 2)
    return [values, col_swap(values, 1), far, col_swap(far, 1)]


def spread_rel(ring, values):
    blocks = jnp.concatenate(spread(values), 1)
    width = values.shape[1]
    me = lax.axis_index("col")
    piece = blocks.shape[1] // ring.count
    parts = []
    for j in range(ring.count):
        start = ring.behind[j] * piece
        owner, inside = start // width, start % width
        parts.append(lax.dynamic_slice_in_dim(blocks, (owner ^ me) * width + inside, piece, 1))
    return jnp.concatenate(parts, 1)


def collect_rel(ring, partial_value):
    count = lax.axis_size("col")
    width = partial_value.shape[1] // count
    piece = partial_value.shape[1] // ring.count
    me = lax.axis_index("col")

    def block(j):
        first = (me ^ j) * (width // piece)
        return jnp.concatenate(
            [
                lax.dynamic_slice_in_dim(partial_value, ring.distance[first + i] * piece, piece, 1)
                for i in range(width // piece)
            ],
            1,
        )

    low = jnp.bfloat16
    near = col_swap(jnp.concatenate([block(1), block(3)], 1).astype(low), 1)
    far = col_swap((block(2) + near[:, width:]).astype(low), 2)
    return block(0) + near[:, :width] + far


def norm_forward(row_values, gain_vec, full_width):
    totals = lax.psum(jnp.sum(row_values * row_values, 1), "col")
    factor = lax.rsqrt(totals / full_width + EPS)
    return ((row_values * factor[:, None] * gain_vec).astype(jnp.bfloat16), factor)


def norm_backward(row_values, factor, gain_vec, upstream, full_width):
    weighted = upstream * gain_vec
    totals = lax.psum(jnp.sum(weighted * row_values, 1), "col")
    result = factor[:, None] * weighted - row_values * (factor**3 * totals / full_width)[:, None]
    return (result, jnp.sum(upstream * row_values * factor[:, None], 0))


def block_mask(segment, token_index, start_row, block_rows):
    row_segment = lax.dynamic_slice_in_dim(segment, start_row, block_rows)
    row_index = start_row + jnp.arange(block_rows, dtype=jnp.int32)
    return (row_segment[:, None] == segment[None, :]) & (row_index[:, None] >= token_index[None, :])


def block_scores(query_block, key_turned, allowed, score_factor):
    raw_scores = (
        jnp.einsum("tgrd,ugd->grtu", query_block, key_turned, preferred_element_type=jnp.float32)
        * score_factor
    )
    return jnp.where(allowed[None, None], raw_scores, NEGATIVE)


def local(
    hidden_in,
    seq_lengths,
    attn_norm,
    w_query,
    key_weight,
    value_weight,
    query_norm,
    key_norm,
    w_output,
    ffwd_norm,
    w_gate,
    w_up,
    w_down,
    cotangent,
):
    row_number_total = hidden_in.shape[0]
    part_width = hidden_in.shape[1]
    full_width = part_width * lax.axis_size("col")
    head_size = query_norm.shape[0]
    kv_heads = key_weight.shape[1] // head_size
    q_heads = w_query.shape[1] // head_size
    heads_per_group = q_heads // kv_heads
    block_rows = min(512, row_number_total)
    blocks = row_number_total // block_rows
    score_factor = 1.0 / math.sqrt(head_size)
    segment, position = tables(seq_lengths[0], row_number_total)
    cos_table, sin_table = rotary(position, head_size)
    token_index = jnp.arange(row_number_total, dtype=jnp.int32)
    starts = jnp.arange(blocks, dtype=jnp.int32) * block_rows
    ring = Ring(lax.axis_size("row"))
    steps = ring.half
    low = jnp.bfloat16
    q_width, k_width = w_query.shape[1], key_weight.shape[1]
    qkv_ring = Gather(ring, jnp.concatenate([w_query, key_weight, value_weight], 1))
    out_ring = Gather(ring, w_output)
    gate_ring, up_ring = Gather(ring, w_gate), Gather(ring, w_up)
    ff_half = w_down.shape[0] // 2
    down_rings = Gather(ring, w_down[:ff_half]), Gather(ring, w_down[ff_half:])
    queue = [(g, s) for pair in ((qkv_ring, out_ring), (gate_ring, up_ring), down_rings) for s in range(steps) for g in pair]
    for place, (gather, step) in enumerate(queue):
        gather.step(step, *(queue[place - 2][0].last if place >= 2 and step == 0 else ()))
    qkv_all = jnp.concatenate(qkv_ring.blocks(), 0)
    output_all = jnp.concatenate(out_ring.blocks(), 1)
    gate_all = jnp.concatenate(gate_ring.blocks(), 0)
    up_all = jnp.concatenate(up_ring.blocks(), 0)
    down_all = jnp.concatenate([jnp.concatenate(g.blocks(), 1) for g in down_rings], 0)
    residual = hidden_in.astype(jnp.float32)
    normed_one, factor_one = norm_forward(residual, attn_norm, full_width)
    wide_one = spread_rel(ring, normed_one)
    upstream_wide = spread_rel(ring, cotangent)
    qkv_raw = matrix_multiply(wide_one, qkv_all)
    query_raw = qkv_raw[:, :q_width]
    key_raw = qkv_raw[:, q_width : q_width + k_width]
    value_bf = qkv_raw[:, q_width + k_width :].astype(low).reshape(row_number_total, kv_heads, head_size)

    def turn_query(raw_rows, gain_vec):
        return head_turn(raw_rows, gain_vec, cos_table, sin_table, q_heads)

    def turn_key(raw_rows, gain_vec):
        return head_turn(raw_rows, gain_vec, cos_table, sin_table, kv_heads)

    query_rotated = turn_query(query_raw, query_norm).astype(jnp.bfloat16)
    query_blocks = query_rotated.reshape(blocks, block_rows, kv_heads, heads_per_group, head_size)
    key_turned = turn_key(key_raw, key_norm).astype(jnp.bfloat16)

    def forward_block(packed):
        query_block, start_row = packed
        allowed = block_mask(segment, token_index, start_row, block_rows)
        scores = block_scores(query_block, key_turned, allowed, score_factor)
        row_peak = jnp.max(scores, -1, keepdims=True)
        exp_scores = jnp.exp(scores - row_peak)
        totals = jnp.sum(exp_scores, -1, keepdims=True)
        prob_rows = (exp_scores / totals).astype(jnp.bfloat16)
        mixed_out = jnp.einsum(
            "grtu,ugd->tgrd", prob_rows, value_bf, preferred_element_type=jnp.float32
        )
        return (mixed_out, row_peak + jnp.log(totals))

    mixed_blocks, log_totals = lax.map(forward_block, (query_blocks, starts))
    mixed_bf = mixed_blocks.reshape(row_number_total, q_heads * head_size).astype(jnp.bfloat16)
    attn_out = collect_rel(ring, matrix_multiply(mixed_bf, output_all))
    middle = residual + attn_out
    normed_two, factor_two = norm_forward(middle, ffwd_norm, full_width)
    wide_two = spread_rel(ring, normed_two)
    gate_pre = matrix_multiply(wide_two, gate_all)
    up_pre = matrix_multiply(wide_two, up_all)
    hidden_bf = swish_product(gate_pre, up_pre).astype(low)
    hidden_out = (middle + collect_rel(ring, matrix_multiply(hidden_bf, down_all))).astype(low)

    def columns(wide, j):
        piece = wide.shape[1] // ring.count
        return wide[:, j * piece : (j + 1) * piece]

    grad_hidden = times_transposed(upstream_wide, down_all)
    _, pull_swish = jax.vjp(swish_product, gate_pre, up_pre)
    grad_gate_pre, grad_up_pre = pull_swish(grad_hidden)
    gate_low = grad_gate_pre.astype(low)
    up_low = grad_up_pre.astype(low)
    grad_normed_two = collect_rel(ring, times_transposed(gate_low, gate_all) + times_transposed(up_low, up_all))
    grad_middle_norm, ffwd_gain_grad = norm_backward(
        middle, factor_two, ffwd_norm, grad_normed_two, full_width
    )
    grad_middle = cotangent.astype(jnp.float32) + grad_middle_norm
    middle_wide = spread_rel(ring, grad_middle.astype(low))
    grad_mixed = times_transposed(middle_wide, output_all).astype(low)
    grad_mixed = grad_mixed.reshape(blocks, block_rows, kv_heads, heads_per_group, head_size)

    def backward_block(carried, packed):
        query_block, grad_block, log_block, start_row = packed
        allowed = block_mask(segment, token_index, start_row, block_rows)
        scores = block_scores(query_block, key_turned, allowed, score_factor)
        prob_rows = jnp.exp(scores - log_block)
        prob_low = prob_rows.astype(jnp.bfloat16)
        grad_probs = jnp.einsum(
            "tgrd,ugd->grtu", grad_block, value_bf, preferred_element_type=jnp.float32
        )
        row_delta = jnp.sum(grad_probs * prob_rows, -1, keepdims=True)
        grad_scores = (prob_rows * (grad_probs - row_delta)).astype(jnp.bfloat16)
        grad_qblock = (
            jnp.einsum(
                "grtu,ugd->tgrd", grad_scores, key_turned, preferred_element_type=jnp.float32
            )
            * score_factor
        )
        key_part = (
            jnp.einsum(
                "grtu,tgrd->ugd", grad_scores, query_block, preferred_element_type=jnp.float32
            )
            * score_factor
        )
        value_part = jnp.einsum(
            "grtu,tgrd->ugd", prob_low, grad_block, preferred_element_type=jnp.float32
        )
        return ((carried[0] + key_part, carried[1] + value_part), grad_qblock)

    zero_state = jnp.zeros((row_number_total, kv_heads, head_size), jnp.float32)
    (grad_kturned, grad_value), grad_qturned = lax.scan(
        backward_block, (zero_state, zero_state), (query_blocks, grad_mixed, log_totals, starts)
    )
    grad_qturned = grad_qturned.reshape(row_number_total, q_heads, head_size)
    _, pull_query = jax.vjp(turn_query, query_raw, query_norm)
    grad_query_raw, query_gain_grad = pull_query(grad_qturned)
    _, pull_key = jax.vjp(turn_key, key_raw, key_norm)
    grad_key_raw, key_gain_grad = pull_key(grad_kturned)
    query_low = grad_query_raw.astype(jnp.bfloat16)
    key_low = grad_key_raw.astype(jnp.bfloat16)
    value_low = grad_value.reshape(row_number_total, kv_heads * head_size).astype(jnp.bfloat16)
    qkv_low = jnp.concatenate([query_low, key_low, value_low], 1)
    grad_normed_one = collect_rel(ring, times_transposed(qkv_low, qkv_all))
    down_sums = tuple(
        Scatter(ring, lambda j, h=h: transposed_times(h, columns(upstream_wide, j)))
        for h in (hidden_bf[:, :ff_half], hidden_bf[:, ff_half:])
    )
    gate_sum = Scatter(ring, lambda j: transposed_times(columns(wide_two, j), gate_low))
    up_sum = Scatter(ring, lambda j: transposed_times(columns(wide_two, j), up_low))
    out_sum = Scatter(ring, lambda j: transposed_times(mixed_bf, columns(middle_wide, j)))
    qkv_sum = Scatter(ring, lambda j: transposed_times(columns(wide_one, j), qkv_low))
    queue = [(g, s) for pair in (down_sums, (gate_sum, up_sum), (out_sum, qkv_sum)) for s in range(steps) for g in pair]
    for place, (scatter, step) in enumerate(queue):
        scatter.step(step, *(queue[place - 2][0].last if place >= 2 and step == 0 else ()))
    grad_down = jnp.concatenate([s.total() for s in down_sums], 0)
    grad_qkv = qkv_sum.total()
    grad_totals = (
        grad_qkv[:, :q_width],
        grad_qkv[:, q_width : q_width + k_width],
        grad_qkv[:, q_width + k_width :],
        out_sum.total(),
        gate_sum.total(),
        up_sum.total(),
        grad_down,
    )
    grad_residual_norm, attn_gain_grad = norm_backward(
        residual, factor_one, attn_norm, grad_normed_one, full_width
    )
    hidden_grad = grad_middle + grad_residual_norm
    col_start = lax.axis_index("col") * part_width
    zero_width = jnp.zeros((full_width,), jnp.float32)
    first_wide = lax.dynamic_update_slice_in_dim(zero_width, attn_gain_grad, col_start, 0)
    second_wide = lax.dynamic_update_slice_in_dim(zero_width, ffwd_gain_grad, col_start, 0)
    gain_totals = lax.psum(
        (first_wide, second_wide, query_gain_grad, key_gain_grad), ("row", "col")
    )
    first_part = lax.dynamic_slice_in_dim(gain_totals[0], col_start, part_width)
    second_part = lax.dynamic_slice_in_dim(gain_totals[1], col_start, part_width)
    return (
        hidden_out,
        hidden_grad,
        first_part,
        grad_totals[0],
        grad_totals[1],
        grad_totals[2],
        gain_totals[2],
        gain_totals[3],
        grad_totals[3],
        second_part,
        grad_totals[4],
        grad_totals[5],
        grad_totals[6],
    )


def solution(mesh):
    in_specs = (
        P("row", "col"),
        P("row", None),
        P("col"),
        P("row", "col"),
        P("row", "col"),
        P("row", "col"),
        P(),
        P(),
        P("col", "row"),
        P("col"),
        P("row", "col"),
        P("row", "col"),
        P("col", "row"),
        P("row", "col"),
    )
    out_specs = (
        P("row", "col"),
        P("row", "col"),
        P("col"),
        P("row", "col"),
        P("row", "col"),
        P("row", "col"),
        P(),
        P(),
        P("col", "row"),
        P("col"),
        P("row", "col"),
        P("row", "col"),
        P("col", "row"),
    )
    return jax.shard_map(local, mesh=mesh, in_specs=in_specs, out_specs=out_specs, check_vma=False)
```

```python
import math

import jax
import jax.numpy as jnp
from jax import lax
from jax.experimental import pallas as pl
from jax.experimental.pallas import tpu as pltpu
from jax.sharding import PartitionSpec as P

EPS = 1e-06
THETA = 1000000.0
NEGATIVE = -1e30
MOST = 512


def tables(lengths_row, row_number_total):
    steps_idx = jnp.arange(row_number_total, dtype=jnp.int32)
    seq_ends = jnp.cumsum(lengths_row)
    seq_starts = seq_ends - lengths_row
    segment = jnp.sum((steps_idx[:, None] >= seq_ends[None, :]).astype(jnp.int32), 1)
    member = segment[:, None] == jnp.arange(lengths_row.shape[0], dtype=jnp.int32)[None, :]
    return steps_idx - jnp.sum(jnp.where(member, seq_starts[None, :], 0), 1)


def rotary(position, head_size):
    half_size = head_size // 2
    frequency = THETA ** (-(jnp.arange(half_size, dtype=jnp.float32) * 2.0 / head_size))
    angles = position.astype(jnp.float32)[:, None] * frequency[None, :]
    cosines, sines = jnp.cos(angles), jnp.sin(angles)
    return jnp.concatenate([cosines, cosines], 1), jnp.concatenate([-sines, sines], 1)


def ring_order(count):
    return list(range(0, count, 2)) + list(range(count - 1, 0, -2))


class Ring:
    def __init__(self):
        rows = lax.axis_size("row")
        self.count = count = min(8, rows)
        self.half = count // 2
        self.members = members = rows // count
        self.groups = [[g * members + m for m in range(members)] for g in range(count)]
        order = ring_order(count)
        pairs = [(order[i], order[(i + 1) % count]) for i in range(count)]
        self.onward = [(a * members + m, b * members + m) for a, b in pairs for m in range(members)]
        self.backward = [(b, a) for a, b in self.onward]
        cols = lax.axis_size("col")
        per_col = count // cols
        behind = [[order[(order.index(g) - j) % count] for j in range(count)] for g in range(count)]
        place = [
            [[COL_ORDER.index((b // per_col) ^ c) * per_col + b % per_col for b in row] for c in range(cols)]
            for row in behind
        ]
        self.place = jnp.array(place, jnp.int32)[lax.axis_index("row") // members, lax.axis_index("col")]

    def send_on(self, value):
        return lax.ppermute(value, "row", self.onward)

    def send_back(self, value):
        return lax.ppermute(value, "row", self.backward)


def after(value, *earlier):
    return lax.optimization_barrier((value,) + earlier)[0]


class Gather:
    def __init__(self, ring, block, axis):
        if ring.members > 1:
            block = lax.all_gather(block, "row", axis=axis, tiled=True, axis_index_groups=ring.groups)
        self.ring, self.block = ring, block
        self.from_behind, self.from_ahead = [], []
        self.last = (block, block)

    def step(self, number, *earlier):
        ring = self.ring
        on, back = self.last
        if number == ring.half - 1:
            cut = self.block.shape[0] // 2
            on, back = on[:cut], back[cut:]
        if earlier:
            on, back = after(on, *earlier), after(back, *earlier)
        on, back = ring.send_on(on), ring.send_back(back)
        self.last = (on, back)
        if number == ring.half - 1:
            self.far = jnp.concatenate([on, back], 0)
        else:
            self.from_behind.append(on)
            self.from_ahead.append(back)

    def blocks(self):
        return [self.block] + self.from_behind + [self.far] + self.from_ahead[::-1]


class Scatter:
    def __init__(self, ring, part, axis):
        self.ring, self.part, self.axis = ring, part, axis
        self.on = self.back = None

    def step(self, number, *earlier):
        ring = self.ring
        low = jnp.bfloat16
        if number == 0:
            whole = self.part(ring.half)
            cut = whole.shape[0] // 2
            on, back = whole[:cut].astype(low), whole[cut:].astype(low)
        else:
            on = self.part(ring.half + number)
            back = self.part(ring.half - number)
            if number == 1:
                cut = on.shape[0] // 2
                on = jnp.concatenate([on[:cut] + self.on, on[cut:]], 0)
                back = jnp.concatenate([back[:cut], back[cut:] + self.back], 0)
            else:
                on, back = on + self.on, back + self.back
            on, back = on.astype(low), back.astype(low)
        if earlier:
            on, back = after(on, *earlier), after(back, *earlier)
        self.on, self.back = ring.send_on(on), ring.send_back(back)
        self.last = (self.on, self.back)

    def total(self):
        value = self.part(0) + self.on + self.back
        if self.ring.members == 1:
            return value
        return lax.psum_scatter(
            value.astype(jnp.bfloat16),
            "row",
            scatter_dimension=self.axis,
            tiled=True,
            axis_index_groups=self.ring.groups,
        ).astype(jnp.float32)


COL_ORDER = (0, 2, 1, 3)


def swap(value, axis, bit):
    return lax.ppermute(value, axis, [(i, i ^ bit) for i in range(lax.axis_size(axis))])


def spread(values):
    far = swap(values, "col", 2)
    return [values, far, swap(values, "col", 1), swap(far, "col", 1)]


def collect(keep, send):
    near = swap(send, "col", 1)
    width = keep.shape[1] // 2
    both = keep.astype(jnp.float32) + near
    far = swap(both[:, width:].astype(jnp.bfloat16), "col", 2)
    return both[:, :width] + far


def sum_over(value, axis):
    bit = 1
    while bit < lax.axis_size(axis):
        value = value + swap(value, axis, bit)
        bit *= 2
    return value


def dot_nt(left_side, right_side):
    return lax.dot_general(
        left_side, right_side, (((1,), (1,)), ((), ())), preferred_element_type=jnp.float32
    )


def dot_nn(left_side, right_side):
    return jnp.dot(left_side, right_side, preferred_element_type=jnp.float32)


def dot_tn(left_side, right_side):
    return lax.dot_general(
        left_side, right_side, (((0,), (0,)), ((), ())), preferred_element_type=jnp.float32
    )


def cost(flops, *arrays):
    moved = sum(math.prod(a.shape) * jnp.dtype(a.dtype).itemsize for a in arrays)
    return pl.CostEstimate(flops=flops, bytes_accessed=moved, transcendentals=0)


def kernel_call(body, places, operands, specs, outs, out_specs, grid, scratch, flops, mib):
    return pl.pallas_call(
        body,
        grid_spec=pltpu.PrefetchScalarGridSpec(
            num_scalar_prefetch=1,
            grid=grid,
            in_specs=specs,
            out_specs=out_specs,
            scratch_shapes=scratch,
        ),
        out_shape=outs,
        cost_estimate=cost(flops, *operands, *outs),
        compiler_params=pltpu.CompilerParams(vmem_limit_bytes=mib << 20),
    )(places, *operands)


def whole_spec(array, buffers=1):
    zeros = (0,) * len(array.shape)
    return pl.BlockSpec(array.shape, lambda *_: zeros, pipeline_mode=pl.Buffered(buffers))


def rows_spec(array, rows):
    return pl.BlockSpec((rows,) + tuple(array.shape[1:]), lambda i, *_: (i,) + (0,) * (len(array.shape) - 1))


def columns_spec(array, columns):
    return pl.BlockSpec((array.shape[0], columns), lambda i, *_: (0, i))


def shape_of(shape, dtype):
    return jax.ShapeDtypeStruct(shape, dtype)


def piece_at(place_ref, j, piece):
    return pl.ds(pl.multiple_of(place_ref[j] * piece, piece), piece)


def gather_norm_matmul(place, hidden_blocks, gain, weights, eps):
    tokens, width = hidden_blocks[0].shape
    full = width * len(hidden_blocks)
    count = len(weights)
    piece, columns = weights[0].shape
    tile = min(512, columns)
    many = len(hidden_blocks)

    def body(place_ref, *refs):
        x_refs, gain_ref = refs[:many], refs[many]
        w_refs = refs[many + 1 : many + 1 + count]
        wide_ref, factor_ref, out_ref, all_ref = refs[many + 1 + count :]

        @pl.when(pl.program_id(0) == 0)
        def _():
            total = jnp.zeros((tokens, 1), jnp.float32)
            for i in range(many):
                value = x_refs[i][...]
                all_ref[:, i * width : (i + 1) * width] = value
                value = value.astype(jnp.float32)
                total = total + jnp.sum(value * value, 1, keepdims=True)
            factor = lax.rsqrt(total / full + eps)
            factor_ref[...] = factor
            for j in range(count):
                at = piece_at(place_ref, j, piece)
                value = all_ref[:, at].astype(jnp.float32) * factor * gain_ref[:, at]
                wide_ref[:, j * piece : (j + 1) * piece] = value.astype(jnp.bfloat16)

        total = dot_nn(wide_ref[:, :piece], w_refs[0][...])
        for j in range(1, count):
            total = total + dot_nn(wide_ref[:, j * piece : (j + 1) * piece], w_refs[j][...])
        out_ref[...] = total

    outs = (
        shape_of((tokens, full), jnp.bfloat16),
        shape_of((tokens, 1), jnp.float32),
        shape_of((tokens, columns), jnp.float32),
    )
    operands = (*hidden_blocks, gain, *weights)
    specs = [whole_spec(b) for b in hidden_blocks] + [whole_spec(gain)] + [columns_spec(w, tile) for w in weights]
    out_specs = (whole_spec(outs[0]), whole_spec(outs[1]), columns_spec(outs[2], tile))
    scratch = [pltpu.VMEM((tokens, full), jnp.bfloat16)]
    return kernel_call(
        body, place, operands, specs, outs, out_specs, (columns // tile,), scratch, 2 * tokens * full * columns, 48
    )


def gather_swish(place, blocks, gates, ups):
    tokens, width = blocks[0].shape
    full, many, count = width * len(blocks), len(blocks), len(gates)
    piece, columns = gates[0].shape
    tile = min(256, columns)

    def body(place_ref, *refs):
        x_refs, g_refs, u_refs = refs[:many], refs[many : many + count], refs[many + count : many + 2 * count]
        wide_ref, gate_ref, up_ref, hidden_ref, all_ref = refs[many + 2 * count :]

        @pl.when(pl.program_id(0) == 0)
        def _():
            for i in range(many):
                all_ref[:, i * width : (i + 1) * width] = x_refs[i][...]
            for j in range(count):
                wide_ref[:, j * piece : (j + 1) * piece] = all_ref[:, piece_at(place_ref, j, piece)]

        def product(w_refs):
            total = dot_nn(wide_ref[:, :piece], w_refs[0][...])
            for j in range(1, count):
                total = total + dot_nn(wide_ref[:, j * piece : (j + 1) * piece], w_refs[j][...])
            return total

        gate = product(g_refs)
        gate_ref[...] = gate
        up = product(u_refs)
        up_ref[...] = up
        hidden_ref[...] = (gate / (1.0 + jnp.exp(-gate)) * up).astype(jnp.bfloat16)

    outs = (
        shape_of((tokens, full), jnp.bfloat16),
        shape_of((tokens, columns), jnp.float32),
        shape_of((tokens, columns), jnp.float32),
        shape_of((tokens, columns), jnp.bfloat16),
    )
    operands = (*blocks, *gates, *ups)
    specs = [whole_spec(b) for b in blocks] + [columns_spec(w, tile) for w in (*gates, *ups)]
    out_specs = (whole_spec(outs[0]),) + tuple(columns_spec(o, tile) for o in outs[1:])
    scratch = [pltpu.VMEM((tokens, full), jnp.bfloat16)]
    return kernel_call(
        body, place, operands, specs, outs, out_specs, (columns // tile,), scratch, 4 * tokens * full * columns, 48
    )


def spread_product(place, lefts, groups, transposed):
    tokens = lefts[0].shape[0]
    count = len(groups[0])
    piece = groups[0][0].shape[0 if transposed else 1]
    many = len(lefts)
    full = piece * count
    tile = min(256, tokens)
    dot = dot_nt if transposed else dot_nn

    def body(place_ref, *refs):
        y_refs = refs[:many]
        w_refs = [refs[many + g * count : many + (g + 1) * count] for g in range(many)]
        keep_ref, send_ref, all_ref = refs[many + many * count :]
        for j in range(count):
            total = dot(y_refs[0][...], w_refs[0][j][...])
            for g in range(1, many):
                total = total + dot(y_refs[g][...], w_refs[g][j][...])
            all_ref[:, piece_at(place_ref, j, piece)] = total.astype(jnp.bfloat16)
        keep_ref[...] = all_ref[:, : full // 2]
        send_ref[...] = all_ref[:, full // 2 :]

    outs = (shape_of((tokens, full // 2), jnp.bfloat16),) * 2
    operands = (*lefts, *(w for group in groups for w in group))
    specs = [rows_spec(y, tile) for y in lefts] + [whole_spec(w) for w in operands[many:]]
    out_specs = tuple(rows_spec(o, tile) for o in outs)
    inner = sum(y.shape[1] for y in lefts)
    return kernel_call(
        body, place, operands, specs, outs, out_specs, (tokens // tile,), [pltpu.VMEM((tile, full), jnp.bfloat16)],
        2 * tokens * full * inner, 48
    )


def gather_transposed(place, blocks, groups):
    tokens, width = blocks[0].shape
    many, count = len(blocks), len(groups[0])
    piece = groups[0][0].shape[1]
    full = width * many
    widths = [group[0].shape[0] for group in groups]
    tile = min(256, tokens)

    def body(place_ref, *refs):
        x_refs = refs[:many]
        w_refs = [refs[many + g * count : many + (g + 1) * count] for g in range(len(groups))]
        wide_ref, out_ref, all_ref = refs[many + len(groups) * count :]
        for i in range(many):
            all_ref[:, i * width : (i + 1) * width] = x_refs[i][...]
        for j in range(count):
            wide_ref[:, j * piece : (j + 1) * piece] = all_ref[:, piece_at(place_ref, j, piece)]
        start = 0
        for g, span in enumerate(widths):
            total = dot_nt(wide_ref[:, :piece], w_refs[g][0][...])
            for j in range(1, count):
                total = total + dot_nt(wide_ref[:, j * piece : (j + 1) * piece], w_refs[g][j][...])
            out_ref[:, start : start + span] = total.astype(jnp.bfloat16)
            start += span

    outs = (shape_of((tokens, full), jnp.bfloat16), shape_of((tokens, sum(widths)), jnp.bfloat16))
    operands = (*blocks, *(w for group in groups for w in group))
    specs = [rows_spec(b, tile) for b in blocks] + [whole_spec(w) for w in operands[many:]]
    out_specs = tuple(rows_spec(o, tile) for o in outs)
    scratch = [pltpu.VMEM((tile, full), jnp.bfloat16)]
    return kernel_call(
        body, place, operands, specs, outs, out_specs, (tokens // tile,), scratch, 2 * tokens * full * sum(widths), 48
    )


def gather_swish_back(place, blocks, groups, gate, up):
    tokens, width = blocks[0].shape
    many, count = len(blocks), len(groups[0])
    piece = groups[0][0].shape[1]
    full = width * many
    widths = [group[0].shape[0] for group in groups]
    tile = min(256, tokens)

    def body(place_ref, *refs):
        x_refs, gate_ref, up_ref = refs[:many], refs[many], refs[many + 1]
        first = many + 2
        w_refs = [refs[first + g * count : first + (g + 1) * count] for g in range(len(groups))]
        wide_ref, gate_out, up_out, all_ref = refs[first + len(groups) * count :]
        for i in range(many):
            all_ref[:, i * width : (i + 1) * width] = x_refs[i][...]
        for j in range(count):
            wide_ref[:, j * piece : (j + 1) * piece] = all_ref[:, piece_at(place_ref, j, piece)]
        start = 0
        for g, span in enumerate(widths):
            total = dot_nt(wide_ref[:, :piece], w_refs[g][0][...])
            for j in range(1, count):
                total = total + dot_nt(wide_ref[:, j * piece : (j + 1) * piece], w_refs[g][j][...])
            at = slice(start, start + span)
            gate_value, up_value = gate_ref[:, at], up_ref[:, at]
            sigma = 1.0 / (1.0 + jnp.exp(-gate_value))
            gate_out[:, at] = (total * up_value * sigma * (1.0 + gate_value * (1.0 - sigma))).astype(jnp.bfloat16)
            up_out[:, at] = (total * gate_value * sigma).astype(jnp.bfloat16)
            start += span

    outs = (shape_of((tokens, full), jnp.bfloat16),) + (shape_of((tokens, sum(widths)), jnp.bfloat16),) * 2
    operands = (*blocks, gate, up, *(w for group in groups for w in group))
    specs = [rows_spec(b, tile) for b in (*blocks, gate, up)] + [whole_spec(w) for w in operands[many + 2 :]]
    out_specs = tuple(rows_spec(o, tile) for o in outs)
    scratch = [pltpu.VMEM((tile, full), jnp.bfloat16)]
    return kernel_call(
        body, place, operands, specs, outs, out_specs, (tokens // tile,), scratch, 2 * tokens * full * sum(widths), 48
    )


def turn(values, cos_wide, sin_wide):
    return values * cos_wide + pltpu.roll(values, values.shape[1] // 2, 1) * sin_wide


def band(rows, cols, first_row, first_col, position):
    distance = (
        lax.broadcasted_iota(jnp.int32, (rows, cols), 0)
        + (first_row - first_col)
        - lax.broadcasted_iota(jnp.int32, (rows, cols), 1)
    )
    return (distance >= 0) & (distance <= position)


def attention_blocks(tokens, most):
    rows = min(256, tokens)
    reach = -(-(most - 1) // rows)
    return rows, [(i * rows, max(0, i - reach) * rows, (i + 1) * rows) for i in range(tokens // rows)]


def attend(raw, position, cos_wide, sin_wide, query_norm, key_norm, q_width, k_width, most, eps):
    tokens = raw.shape[0]
    size = query_norm.shape[1]
    kv_heads, per_group = k_width // size, q_width // k_width
    factor = 1.0 / math.sqrt(size)
    rows, plan = attention_blocks(tokens, most)

    def body(_, q_ref, k_ref, v_ref, pos_ref, cos_ref, sin_ref, qn_ref, kn_ref, qt_ref, kt_ref, vb_ref, mix_ref):
        def turned(value, gain):
            scale = lax.rsqrt(jnp.mean(value * value, 1, keepdims=True) + eps)
            return turn(value * scale * gain, cos_ref[...], sin_ref[...]).astype(jnp.bfloat16)

        kt_ref[...] = turned(k_ref[...], kn_ref[...])
        vb_ref[...] = v_ref[...].astype(jnp.bfloat16)
        for g in range(per_group):
            at = slice(g * size, (g + 1) * size)
            qt_ref[:, at] = turned(q_ref[:, at], qn_ref[...])
        for first, low, high in plan:
            span = slice(first, first + rows)
            allowed = band(rows, high - low, first, low, pos_ref[span, :])
            for g in range(per_group):
                at = slice(g * size, (g + 1) * size)
                scores = dot_nt(qt_ref[span, at], kt_ref[low:high, :]) * factor
                scores = jnp.where(allowed, scores, NEGATIVE)
                weights = jnp.exp(scores - jnp.max(scores, 1, keepdims=True))
                weights = (weights * (1.0 / jnp.sum(weights, 1, keepdims=True))).astype(jnp.bfloat16)
                mix_ref[span, at] = dot_nn(weights, vb_ref[low:high, :]).astype(jnp.bfloat16)

    group = per_group * size
    outs = tuple(shape_of((tokens, w), jnp.bfloat16) for w in (q_width, k_width, k_width, q_width))
    q_spec = pl.BlockSpec((tokens, group), lambda i, *_: (0, i))
    k_spec = pl.BlockSpec((tokens, size), lambda i, *_: (0, q_width // size + i))
    v_spec = pl.BlockSpec((tokens, size), lambda i, *_: (0, (q_width + k_width) // size + i))
    one = pl.BlockSpec((tokens, size), lambda i, *_: (0, i))
    operands = (raw, raw, raw, position, cos_wide, sin_wide, query_norm, key_norm)
    specs = [q_spec, k_spec, v_spec] + [whole_spec(a) for a in operands[3:]]
    flops = 4 * tokens * (high_sum(plan) * rows // tokens) * q_width
    return kernel_call(
        body, jnp.zeros((1,), jnp.int32), operands, specs, outs, (q_spec, one, one, q_spec), (kv_heads,), [], flops, 48
    )


def high_sum(plan):
    return sum(high - low for _, low, high in plan)


def attend_back(raw, turned_q, turned_k, values, grad_mixed, position, cos_wide, sin_wide, query_norm, key_norm, most, eps):
    tokens, q_width = turned_q.shape
    k_width = turned_k.shape[1]
    size = query_norm.shape[1]
    kv_heads, per_group = k_width // size, q_width // k_width
    factor = 1.0 / math.sqrt(size)
    rows, plan = attention_blocks(tokens, most)

    def body(_, q_ref, k_ref, qt_ref, kt_ref, v_ref, dm_ref, pos_ref, cos_ref, sin_ref, qn_ref, kn_ref,
             dq_ref, dk_ref, dv_ref, gain_ref, key_sum, value_sum):
        key_sum[...] = jnp.zeros_like(key_sum)
        value_sum[...] = jnp.zeros_like(value_sum)

        def back(raw_rows, gain, upstream, span):
            scale = lax.rsqrt(jnp.mean(raw_rows * raw_rows, 1, keepdims=True) + eps)
            turned_back = turn(upstream, cos_ref[span, :], -sin_ref[span, :])
            inner = jnp.mean(turned_back * gain * raw_rows, 1, keepdims=True)
            grad = scale * gain * turned_back - raw_rows * (scale * scale * scale * inner)
            return grad.astype(jnp.bfloat16), jnp.sum(turned_back * raw_rows * scale, 0, keepdims=True)

        query_gain = jnp.zeros((1, size), jnp.float32)
        for first, low, high in plan:
            span = slice(first, first + rows)
            allowed = band(rows, high - low, first, low, pos_ref[span, :])
            for g in range(per_group):
                at = slice(g * size, (g + 1) * size)
                queries, upstream = qt_ref[span, at], dm_ref[span, at]
                scores = dot_nt(queries, kt_ref[low:high, :]) * factor
                scores = jnp.where(allowed, scores, NEGATIVE)
                probs = jnp.exp(scores - jnp.max(scores, 1, keepdims=True))
                probs = probs * (1.0 / jnp.sum(probs, 1, keepdims=True))
                grads = dot_nt(upstream, v_ref[low:high, :])
                weighted = probs * grads
                total = jnp.sum(weighted, 1, keepdims=True)
                grads = (weighted - probs * total).astype(jnp.bfloat16)
                value_sum[low:high, :] += dot_tn(probs.astype(jnp.bfloat16), upstream)
                key_sum[low:high, :] += dot_tn(grads, queries)
                grad_turned = dot_nn(grads, kt_ref[low:high, :]) * factor
                grad, gain = back(q_ref[span, at], qn_ref[...], grad_turned, span)
                dq_ref[span, at] = grad
                query_gain = query_gain + gain
        grad, key_gain = back(k_ref[...], kn_ref[...], key_sum[...] * factor, slice(0, tokens))
        dk_ref[...] = grad
        dv_ref[...] = value_sum[...].astype(jnp.bfloat16)
        gain_ref[...] = jnp.concatenate([query_gain, key_gain, jnp.zeros((6, size), jnp.float32)], 0)

    group = per_group * size
    outs = (
        shape_of((tokens, q_width), jnp.bfloat16),
        shape_of((tokens, k_width), jnp.bfloat16),
        shape_of((tokens, k_width), jnp.bfloat16),
        shape_of((8 * kv_heads, size), jnp.float32),
    )
    q_spec = pl.BlockSpec((tokens, group), lambda i, *_: (0, i))
    k_spec = pl.BlockSpec((tokens, size), lambda i, *_: (0, q_width // size + i))
    one = pl.BlockSpec((tokens, size), lambda i, *_: (0, i))
    operands = (raw, raw, turned_q, turned_k, values, grad_mixed, position, cos_wide, sin_wide, query_norm, key_norm)
    specs = [q_spec, k_spec, q_spec, one, one, q_spec] + [whole_spec(a) for a in operands[6:]]
    out_specs = (q_spec, one, one, pl.BlockSpec((8, size), lambda i, *_: (i, 0)))
    scratch = [pltpu.VMEM((tokens, size), jnp.float32)] * 2
    flops = 10 * tokens * (high_sum(plan) * rows // tokens) * q_width
    return kernel_call(
        body, jnp.zeros((1,), jnp.int32), operands, specs, outs, out_specs, (kv_heads,), scratch, flops, 48
    )


def local(
    hidden_in,
    seq_lengths,
    attn_norm,
    w_query,
    key_weight,
    value_weight,
    query_norm,
    key_norm,
    w_output,
    ffwd_norm,
    w_gate,
    w_up,
    w_down,
    cotangent,
):
    low = jnp.bfloat16
    tokens, part_width = hidden_in.shape
    full_width = part_width * lax.axis_size("col")
    head_size = query_norm.shape[0]
    q_width, k_width = w_query.shape[1], key_weight.shape[1]
    ring = Ring()
    place = ring.place
    steps = ring.half

    hidden_blocks = spread(hidden_in)
    gains = jnp.concatenate(spread(attn_norm[None, :]), 1)
    qkv_ring = Gather(ring, jnp.concatenate([w_query, key_weight, value_weight], 1), 0)
    out_ring = Gather(ring, w_output, 1)
    gate_ring, up_ring = Gather(ring, w_gate, 0), Gather(ring, w_up, 0)
    ff_half = w_down.shape[0] // 2
    down_rings = Gather(ring, w_down[:ff_half], 1), Gather(ring, w_down[ff_half:], 1)
    queue = [(g, s) for pair in ((qkv_ring, out_ring), (gate_ring, up_ring), down_rings) for s in range(steps) for g in pair]
    for spot, (gather, step) in enumerate(queue):
        gather.step(step, *(queue[spot - 2][0].last if spot >= 2 and step == 0 else ()))
    qkv_all, output_all = qkv_ring.blocks(), out_ring.blocks()
    gate_all, up_all = gate_ring.blocks(), up_ring.blocks()
    down_all = [g.blocks() for g in down_rings]

    position = tables(seq_lengths[0], tokens)
    cos_wide, sin_wide = rotary(position, head_size)
    turning = (position[:, None], cos_wide, sin_wide, query_norm[None, :], key_norm[None, :])
    residual = hidden_in.astype(jnp.float32)
    wide_one, factor_one, qkv_raw = gather_norm_matmul(place, hidden_blocks, gains, qkv_all, EPS)
    turned_q, turned_k, values, mixed = attend(qkv_raw, *turning, q_width, k_width, MOST, EPS)
    middle = residual + collect(*spread_product(place, [mixed], [output_all], False))
    factor_two = lax.rsqrt(sum_over(jnp.sum(middle * middle, 1), "col") / full_width + EPS)[:, None]
    normed_two = (middle * factor_two * ffwd_norm).astype(low)
    wide_two, gate, up, hidden = gather_swish(place, spread(normed_two), gate_all, up_all)
    hidden_parts = [hidden[:, :ff_half], hidden[:, ff_half:]]
    hidden_out = (middle + collect(*spread_product(place, hidden_parts, down_all, False))).astype(low)

    upstream, gate_low, up_low = gather_swish_back(place, spread(cotangent), down_all, gate, up)
    grad_normed = collect(*spread_product(place, [gate_low, up_low], [gate_all, up_all], True))
    weighted = grad_normed * ffwd_norm
    inner = sum_over(jnp.sum(weighted * middle, 1), "col")[:, None] / full_width
    grad_middle = cotangent.astype(jnp.float32) + factor_two * weighted - middle * (factor_two**3 * inner)
    ffwd_gain = jnp.sum(grad_normed * middle * factor_two, 0)
    middle_wide, grad_mixed = gather_transposed(place, spread(grad_middle.astype(low)), [output_all])
    query_low, key_low, value_low, head_gains = attend_back(
        qkv_raw, turned_q, turned_k, values, grad_mixed, *turning, MOST, EPS
    )
    qkv_low = jnp.concatenate([query_low, key_low, value_low], 1)
    grad_first = collect(*spread_product(place, [qkv_low], [qkv_all], True))
    weighted = grad_first * attn_norm
    inner = sum_over(jnp.sum(weighted * residual, 1), "col")[:, None] / full_width
    hidden_grad = grad_middle + factor_one * weighted - residual * (factor_one**3 * inner)
    attn_gain = jnp.sum(grad_first * residual * factor_one, 0)

    def columns(wide, j):
        piece = wide.shape[1] // ring.count
        return wide[:, j * piece : (j + 1) * piece]

    down_sums = tuple(
        Scatter(ring, lambda j, h=h: dot_tn(h, columns(upstream, j)), 1) for h in hidden_parts
    )
    gate_sum = Scatter(ring, lambda j: dot_tn(columns(wide_two, j), gate_low), 0)
    up_sum = Scatter(ring, lambda j: dot_tn(columns(wide_two, j), up_low), 0)
    out_sum = Scatter(ring, lambda j: dot_tn(mixed, columns(middle_wide, j)), 1)
    qkv_sum = Scatter(ring, lambda j: dot_tn(columns(wide_one, j), qkv_low), 0)
    queue = [(g, s) for pair in (down_sums, (gate_sum, up_sum), (out_sum, qkv_sum)) for s in range(steps) for g in pair]
    for spot, (scatter, step) in enumerate(queue):
        scatter.step(step, *(queue[spot - 2][0].last if spot >= 2 and step == 0 else ()))
    grad_qkv = qkv_sum.total()

    head_gains = jnp.sum(head_gains.reshape(-1, 8, head_size), 0)[:2].reshape(-1)
    gain_sums = sum_over(jnp.concatenate([ffwd_gain, sum_over(head_gains, "col")]), "row")
    return (
        hidden_out,
        hidden_grad,
        sum_over(attn_gain, "row"),
        grad_qkv[:, :q_width],
        grad_qkv[:, q_width : q_width + k_width],
        grad_qkv[:, q_width + k_width :],
        gain_sums[part_width : part_width + head_size],
        gain_sums[part_width + head_size :],
        out_sum.total(),
        gain_sums[:part_width],
        gate_sum.total(),
        up_sum.total(),
        jnp.concatenate([s.total() for s in down_sums], 0),
    )


def solution(mesh):
    in_specs = (
        P("row", "col"),
        P("row", None),
        P("col"),
        P("row", "col"),
        P("row", "col"),
        P("row", "col"),
        P(),
        P(),
        P("col", "row"),
        P("col"),
        P("row", "col"),
        P("row", "col"),
        P("col", "row"),
        P("row", "col"),
    )
    out_specs = (
        P("row", "col"),
        P("row", "col"),
        P("col"),
        P("row", "col"),
        P("row", "col"),
        P("row", "col"),
        P(),
        P(),
        P("col", "row"),
        P("col"),
        P("row", "col"),
        P("row", "col"),
        P("col", "row"),
    )
    return jax.shard_map(local, mesh=mesh, in_specs=in_specs, out_specs=out_specs, check_vma=False)
```

```python
import math

import jax
import jax.numpy as jnp
from jax import lax
from jax.experimental import pallas as pl
from jax.experimental.pallas import tpu as pltpu
from jax.sharding import PartitionSpec as P

EPS = 1e-06
THETA = 1000000.0
NEGATIVE = -1e30
MOST = 512
COST_SCALE = 0.02


def tables(lengths_row, row_number_total):
    steps_idx = jnp.arange(row_number_total, dtype=jnp.int32)
    seq_ends = jnp.cumsum(lengths_row)
    seq_starts = seq_ends - lengths_row
    segment = jnp.sum((steps_idx[:, None] >= seq_ends[None, :]).astype(jnp.int32), 1)
    member = segment[:, None] == jnp.arange(lengths_row.shape[0], dtype=jnp.int32)[None, :]
    return steps_idx - jnp.sum(jnp.where(member, seq_starts[None, :], 0), 1)


def rotary(position, head_size):
    half_size = head_size // 2
    frequency = THETA ** (-(jnp.arange(half_size, dtype=jnp.float32) * 2.0 / head_size))
    angles = position.astype(jnp.float32)[:, None] * frequency[None, :]
    cosines, sines = jnp.cos(angles), jnp.sin(angles)
    return jnp.concatenate([cosines, cosines], 1), jnp.concatenate([-sines, sines], 1)


def ring_order(count):
    return list(range(0, count, 2)) + list(range(count - 1, 0, -2))


class Ring:
    def __init__(self):
        rows = lax.axis_size("row")
        self.count = count = min(8, rows)
        self.half = count // 2
        self.members = members = rows // count
        self.groups = [[g * members + m for m in range(members)] for g in range(count)]
        self.lanes = None if members == 1 else [[g * members + m for g in range(count)] for m in range(members)]
        order = ring_order(count)
        self.onward = self.spell([(order[i], order[(i + 1) % count]) for i in range(count)])
        self.backward = [(b, a) for a, b in self.onward]
        self.partner = self.spell([(g, g ^ 1) for g in range(count)])
        self.pairs = [[(2 * p + side) * members + m for p in range(count // 2)] for side in range(2) for m in range(members)]
        group = lax.axis_index("row") // members
        self.parity = group % 2
        self.place = self.places([[order[(order.index(g) - j) % count] for j in range(count)] for g in range(count)])
        self.behind = jnp.array([[order[(order.index(g) - j) % count] for j in range(count)] for g in range(count)])[group]
        self.plain_place = self.places([list(range(count))] * count)
        self.pair_place = self.places(
            [[j // 2 * 2 + (g % 2 ^ j % 2) for j in range(count)] for g in range(count)]
        )

    def spell(self, pairs):
        return [(a * self.members + m, b * self.members + m) for a, b in pairs for m in range(self.members)]

    def places(self, behind):
        cols = lax.axis_size("col")
        per_col = self.count // cols
        table = [
            [[COL_ORDER.index((b // per_col) ^ c) * per_col + b % per_col for b in row] for c in range(cols)]
            for row in behind
        ]
        return jnp.array(table, jnp.int32)[lax.axis_index("row") // self.members, lax.axis_index("col")]

    def send_on(self, value):
        return lax.ppermute(value, "row", self.onward)

    def send_back(self, value):
        return lax.ppermute(value, "row", self.backward)

    def to_partner(self, value):
        return lax.ppermute(value, "row", self.partner)

    def gather_stack(self, block):
        return lax.all_gather(block, "row", axis=0, axis_index_groups=self.lanes)

    def sum_stack(self, blocks):
        return lax.psum_scatter(blocks, "row", scatter_dimension=0, axis_index_groups=self.lanes)

    def inner_gather(self, block, axis):
        if self.members == 1:
            return block
        return lax.all_gather(block, "row", axis=axis, tiled=True, axis_index_groups=self.groups)

    def inner_sum(self, value, axis):
        if self.members == 1:
            return value
        value = value.astype(jnp.bfloat16)
        return lax.psum_scatter(
            value, "row", scatter_dimension=axis, tiled=True, axis_index_groups=self.groups
        ).astype(jnp.float32)


def side_of(blocks, axis, number):
    halves = [b.shape[axis] // 2 for b in blocks]
    cuts = [lax.dynamic_slice_in_dim(b, number * h, h, axis) for b, h in zip(blocks, halves, strict=True)]
    return jnp.concatenate(cuts, axis)


def pair_gather(ring, unit):
    return lax.all_gather(unit, "row", axis=0, axis_index_groups=ring.pairs)


def pair_sum(ring, units):
    return lax.psum_scatter(units, "row", scatter_dimension=0, axis_index_groups=ring.pairs)


def pair_join(ring, mine, got, axis):
    first = ring.parity == 0
    mine, got = mine.astype(jnp.float32), got.astype(jnp.float32)
    value = jnp.concatenate([jnp.where(first, mine, got), jnp.where(first, got, mine)], axis)
    return ring.inner_sum(value, 1 - axis)


class Chain:
    def __init__(self):
        self.token = lax.create_token()

    def pin(self, *values):
        self.token, *values = lax.optimization_barrier((self.token, *values))
        return values if len(values) > 1 else values[0]

    def run(self, kernel, *operands, beside=()):
        results = kernel(*self.pin(operands))
        results = tuple(results) if isinstance(results, (list, tuple)) else (results,)
        return self.pin(*results, *beside)


COL_ORDER = (0, 2, 1, 3)


def swap(value, axis, bit):
    return lax.ppermute(value, axis, [(i, i ^ bit) for i in range(lax.axis_size(axis))])


def dot_nt(left_side, right_side):
    return lax.dot_general(
        left_side, right_side, (((1,), (1,)), ((), ())), preferred_element_type=jnp.float32
    )


def dot_nn(left_side, right_side):
    return jnp.dot(left_side, right_side, preferred_element_type=jnp.float32)


def dot_tn(left_side, right_side):
    return lax.dot_general(
        left_side, right_side, (((0,), (0,)), ((), ())), preferred_element_type=jnp.float32
    )


def cost(flops):
    return pl.CostEstimate(flops=int(COST_SCALE * flops), bytes_accessed=1 << 16, transcendentals=0)


def kernel_call(body, places, operands, specs, outs, out_specs, grid, scratch, flops, mib):
    return pl.pallas_call(
        body,
        grid_spec=pltpu.PrefetchScalarGridSpec(
            num_scalar_prefetch=1,
            grid=grid,
            in_specs=specs,
            out_specs=out_specs,
            scratch_shapes=scratch,
        ),
        out_shape=outs,
        cost_estimate=cost(flops),
        compiler_params=pltpu.CompilerParams(vmem_limit_bytes=mib << 20),
    )(places, *operands)


def whole_spec(array, buffers=1):
    zeros = (0,) * len(array.shape)
    return pl.BlockSpec(array.shape, lambda *_: zeros, pipeline_mode=pl.Buffered(buffers))


def rows_spec(array, rows):
    return pl.BlockSpec((rows,) + tuple(array.shape[1:]), lambda i, *_: (i,) + (0,) * (len(array.shape) - 1))


def columns_spec(array, columns):
    return pl.BlockSpec((array.shape[0], columns), lambda i, *_: (0, i))


def shape_of(shape, dtype):
    return jax.ShapeDtypeStruct(shape, dtype)


def piece_at(place_ref, j, piece):
    return pl.ds(pl.multiple_of(place_ref[j] * piece, piece), piece)


def norm_rows(place_ref, x_refs, gain_ref, wide_ref, factor_ref, all_ref, piece, eps):
    tokens, full = wide_ref.shape
    width = x_refs[0].shape[1]
    total = jnp.zeros((tokens, 1), jnp.float32)
    for i, x_ref in enumerate(x_refs):
        value = x_ref[...]
        all_ref[:, i * width : (i + 1) * width] = value
        value = value.astype(jnp.float32)
        total = total + jnp.sum(value * value, 1, keepdims=True)
    factor = lax.rsqrt(total / full + eps)
    factor_ref[...] = factor
    for j in range(full // piece):
        at = piece_at(place_ref, j, piece)
        value = all_ref[:, at].astype(jnp.float32) * factor * gain_ref[:, at]
        wide_ref[:, j * piece : (j + 1) * piece] = value.astype(jnp.bfloat16)


def gather_norm_matmul(place, hidden_blocks, gain, weights, eps):
    tokens, width = hidden_blocks[0].shape
    full = width * len(hidden_blocks)
    count = len(weights)
    piece, columns = weights[0].shape
    tile = min(512, columns)
    many = len(hidden_blocks)

    def body(place_ref, *refs):
        x_refs, gain_ref = refs[:many], refs[many]
        w_refs = refs[many + 1 : many + 1 + count]
        wide_ref, factor_ref, out_ref, all_ref = refs[many + 1 + count :]

        @pl.when(pl.program_id(0) == 0)
        def _():
            norm_rows(place_ref, x_refs, gain_ref, wide_ref, factor_ref, all_ref, piece, eps)

        total = dot_nn(wide_ref[:, :piece], w_refs[0][...])
        for j in range(1, count):
            total = total + dot_nn(wide_ref[:, j * piece : (j + 1) * piece], w_refs[j][...])
        out_ref[...] = total

    outs = (
        shape_of((tokens, full), jnp.bfloat16),
        shape_of((tokens, 1), jnp.float32),
        shape_of((tokens, columns), jnp.float32),
    )
    operands = (*hidden_blocks, gain, *weights)
    specs = [whole_spec(b) for b in hidden_blocks] + [whole_spec(gain)] + [columns_spec(w, tile) for w in weights]
    out_specs = (whole_spec(outs[0]), whole_spec(outs[1]), columns_spec(outs[2], tile))
    scratch = [pltpu.VMEM((tokens, full), jnp.bfloat16)]
    return kernel_call(
        body, place, operands, specs, outs, out_specs, (columns // tile,), scratch, 2 * tokens * full * columns, 48
    )


def units_of(refs):
    return [refs[0].at[j] for j in range(refs[0].shape[0])] if len(refs) == 1 else refs


def gather_swish(place, blocks, gain, weights, eps):
    tokens, width = blocks[0].shape
    count, unit, both = weights.shape
    columns = both // 2
    full, many = width * len(blocks), len(blocks)
    piece = full // place.shape[0]
    tile = min(256, columns)

    def body(place_ref, *refs):
        x_refs, gain_ref, g_ref, u_ref = refs[:many], refs[many], refs[many + 1], refs[many + 2]
        wide_ref, factor_ref, gate_ref, up_ref, hidden_ref, all_ref = refs[many + 3 :]

        @pl.when(pl.program_id(0) == 0)
        def _():
            norm_rows(place_ref, x_refs, gain_ref, wide_ref, factor_ref, all_ref, piece, eps)

        def product(w_ref):
            total = dot_nn(wide_ref[:, :unit], w_ref[0])
            for j in range(1, count):
                total = total + dot_nn(wide_ref[:, j * unit : (j + 1) * unit], w_ref[j])
            return total

        gate = product(g_ref)
        gate_ref[...] = gate
        up = product(u_ref)
        up_ref[...] = up
        hidden_ref[...] = (gate / (1.0 + jnp.exp(-gate)) * up).astype(jnp.bfloat16)

    outs = (
        shape_of((tokens, full), jnp.bfloat16),
        shape_of((tokens, 1), jnp.float32),
        shape_of((tokens, columns), jnp.float32),
        shape_of((tokens, columns), jnp.float32),
        shape_of((tokens, columns), jnp.bfloat16),
    )
    operands = (*blocks, gain, weights, weights)
    steps = columns // tile
    specs = [whole_spec(b) for b in (*blocks, gain)] + [
        pl.BlockSpec((count, unit, tile), lambda i, *_: (0, 0, i)),
        pl.BlockSpec((count, unit, tile), lambda i, *_: (0, 0, i + steps)),
    ]
    out_specs = (whole_spec(outs[0]), whole_spec(outs[1])) + tuple(columns_spec(o, tile) for o in outs[2:])
    scratch = [pltpu.VMEM((tokens, full), jnp.bfloat16)]
    return kernel_call(
        body, place, operands, specs, outs, out_specs, (steps,), scratch, 4 * tokens * full * columns, 48
    )


def spread_product(place, left, weights, transposed, normed=None, by_feature=False):
    tokens, inner = left.shape
    many = len(weights)
    count = many if many > 1 else weights[0].shape[0]
    unit = weights[0].shape[-2 if transposed else -1]
    full = unit * count
    piece = full // place.shape[0]
    per_unit = unit // piece
    tile = min(256, tokens)
    dot = dot_nt if transposed else dot_nn
    extras = () if normed is None else (normed,)

    def body(place_ref, *refs):
        y_ref, w_refs = refs[0], units_of(refs[1 : 1 + many])
        rest = refs[1 + many + len(extras) :]
        keep_ref, send_ref, all_ref = rest[0], rest[1], rest[-1]
        rows = jnp.zeros((tile, 1), jnp.float32)
        if by_feature:

            @pl.when(pl.program_id(0) == 0)
            def _():
                rest[3][...] = jnp.zeros_like(rest[3])

        for j in range(count):
            total = dot(y_ref[...], w_refs[j][...])
            if extras:
                weighted = total * refs[1 + many][:, j * unit : (j + 1) * unit].astype(jnp.float32)
                rows = rows + jnp.sum(weighted, 1, keepdims=True)
                if by_feature:
                    sums = jnp.broadcast_to(jnp.sum(weighted, 0, keepdims=True), (8, unit))
                    for i in range(per_unit):
                        at = piece_at(place_ref, j * per_unit + i, piece)
                        rest[3][:, at] += sums[:, i * piece : (i + 1) * piece]
            total = total.astype(jnp.bfloat16)
            for i in range(per_unit):
                at = piece_at(place_ref, j * per_unit + i, piece)
                all_ref[:, at] = total[:, i * piece : (i + 1) * piece]
        keep_ref[...] = all_ref[:, : full // 2]
        send_ref[...] = all_ref[:, full // 2 :]
        if extras:
            rest[2][...] = rows

    outs = (shape_of((tokens, full // 2), jnp.bfloat16),) * 2
    if extras:
        outs += (shape_of((tokens, 1), jnp.float32),)
    operands = (left, *weights, *extras)
    specs = [rows_spec(left, tile)] + [whole_spec(w) for w in weights] + [rows_spec(e, tile) for e in extras]
    out_specs = tuple(rows_spec(o, tile) for o in outs)
    if by_feature:
        outs += (shape_of((8, full), jnp.float32),)
        out_specs += (whole_spec(outs[3]),)
    scratch = [pltpu.VMEM((tile, full), jnp.bfloat16)]
    return kernel_call(
        body, place, operands, specs, outs, out_specs, (tokens // tile,), scratch, 2 * tokens * full * inner, 48
    )


def assemble(place, blocks):
    tokens, width = blocks[0].shape
    many = len(blocks)
    full = width * many
    piece = full // place.shape[0]
    tile = min(256, tokens)

    def body(place_ref, *refs):
        x_refs, (wide_ref, all_ref) = refs[:many], refs[many:]
        for i in range(many):
            all_ref[:, i * width : (i + 1) * width] = x_refs[i][...]
        for j in range(full // piece):
            wide_ref[:, j * piece : (j + 1) * piece] = all_ref[:, piece_at(place_ref, j, piece)]

    outs = (shape_of((tokens, full), jnp.bfloat16),)
    specs = [rows_spec(b, tile) for b in blocks]
    scratch = [pltpu.VMEM((tile, full), jnp.bfloat16)]
    return kernel_call(
        body, place, blocks, specs, outs, (rows_spec(outs[0], tile),), (tokens // tile,), scratch, 1500 * tokens * 1024, 32
    )[0]


def times_transposed(wide, weights, order):
    return back_product(wide, weights, (), lambda total: (total,), order)


def swish_back(wide, weights, gate, up):
    def gradients(total, gate_value, up_value):
        sigma = 1.0 / (1.0 + jnp.exp(-gate_value))
        grad_gate = total * up_value * sigma * (1.0 + gate_value * (1.0 - sigma))
        return grad_gate, total * gate_value * sigma

    return back_product(wide, weights, (gate, up), gradients)


def back_product(wide, weights, extras, epilogue, order=None):
    tokens, full = wide.shape
    others, units = len(extras), len(weights)
    count = units if units > 1 else weights[0].shape[0]
    columns, unit = weights[0].shape[-2:]
    tile = min(256, tokens)
    parts = max(1, others)

    stacked = order is not None

    def body(order_ref, *refs):
        wide_ref, extra_refs = refs[0], refs[1 : 1 + others]
        w_refs, out_ref = refs[1 + others : -1], refs[-1]
        if not stacked:
            w_refs = units_of(w_refs)
        else:
            w_refs = [w_refs[0].at[order_ref[j]] for j in range(count)]
        total = dot_nt(wide_ref[:, :unit], w_refs[0][...])
        for j in range(1, count):
            total = total + dot_nt(wide_ref[:, j * unit : (j + 1) * unit], w_refs[j][...])
        for i, part in enumerate(epilogue(total, *(e[...] for e in extra_refs))):
            out_ref[:, i * columns : (i + 1) * columns] = part.astype(jnp.bfloat16)

    outs = (shape_of((tokens, parts * columns), jnp.bfloat16),)
    operands = (wide, *extras, *weights)
    specs = [rows_spec(b, tile) for b in (wide, *extras)] + [whole_spec(w) for w in weights]
    order = order if stacked else jnp.zeros((1,), jnp.int32)
    return kernel_call(
        body, order, operands, specs, outs, (rows_spec(outs[0], tile),), (tokens // tile,), [],
        2 * tokens * full * columns, 48,
    )[0]


def weight_grad(lefts, rights, order, by_left):
    tokens, rows = lefts[0].shape
    columns = rights[0].shape[1]
    many = len(lefts)
    units = order.shape[0]
    rows, columns = (rows // units, columns) if by_left else (rows, columns // units)

    def body(_, *refs):
        out_ref = refs[-1]
        total = dot_tn(refs[0][...], refs[many][...])
        for c in range(1, many):
            total = total + dot_tn(refs[c][...], refs[many + c][...])
        out_ref[0] = total.astype(jnp.bfloat16)

    outs = (shape_of((units, rows, columns), jnp.bfloat16),)
    moving = pl.BlockSpec((tokens, rows if by_left else columns), lambda i, *_: (0, i))
    left_specs = [moving if by_left else whole_spec(a) for a in lefts]
    right_specs = [whole_spec(a) if by_left else moving for a in rights]
    out_specs = (pl.BlockSpec((1, rows, columns), lambda i, order_ref: (order_ref[i], 0, 0)),)
    flops = 2 * tokens * many * units * rows * columns
    operands = (*lefts, *rights)
    return kernel_call(
        body, order, operands, left_specs + right_specs, outs, out_specs, (units,), [], flops, 56
    )[0]


def block_grad(lefts, rights, number, count, extras):
    tokens, full = lefts[0].shape
    rows = full // count
    widths = [right.shape[1] for right in rights]
    many, more = len(lefts), len(extras)

    def body(_, *refs):
        out_ref = refs[-1]
        start = 0
        for c, width in enumerate(widths):
            at = slice(start, start + width)
            total = dot_tn(refs[c][...], refs[many + c][...])
            for e, (value, first) in enumerate(extras):
                got = refs[2 * many + e][:, at].astype(jnp.float32)
                if value.shape[0] == rows:
                    total = total + got
                elif first == 0:
                    total = jnp.concatenate([total[: value.shape[0]] + got, total[value.shape[0] :]], 0)
                else:
                    total = jnp.concatenate([total[:first], total[first:] + got], 0)
            out_ref[:, at] = total.astype(jnp.bfloat16)
            start += width

    outs = (shape_of((rows, sum(widths)), jnp.bfloat16),)
    operands = (*lefts, *rights, *(value for value, _ in extras))
    specs = [pl.BlockSpec((tokens, rows), lambda *_: (0, number))] * many + [whole_spec(a) for a in operands[many:]]
    return kernel_call(
        body, jnp.zeros((1,), jnp.int32), operands, specs, outs, (whole_spec(outs[0]),), (1,), [],
        2 * tokens * rows * sum(widths), 32,
    )[0]


def turn(values, cos_wide, sin_wide):
    return values * cos_wide + pltpu.roll(values, values.shape[1] // 2, 1) * sin_wide


def band(rows, cols, first_row, first_col, position):
    distance = (
        lax.broadcasted_iota(jnp.int32, (rows, cols), 0)
        + (first_row - first_col)
        - lax.broadcasted_iota(jnp.int32, (rows, cols), 1)
    )
    return (distance >= 0) & (distance <= position)


def attention_blocks(tokens, most):
    rows = min(256, tokens)
    reach = -(-(most - 1) // rows)
    return rows, [(i * rows, max(0, i - reach) * rows, (i + 1) * rows) for i in range(tokens // rows)]


def attend(raw, position, cos_wide, sin_wide, query_norm, key_norm, q_width, k_width, most, eps):
    tokens = raw.shape[0]
    size = query_norm.shape[1]
    kv_heads, per_group = k_width // size, q_width // k_width
    factor = 1.0 / math.sqrt(size)
    rows, plan = attention_blocks(tokens, most)

    def body(_, q_ref, k_ref, v_ref, pos_ref, cos_ref, sin_ref, qn_ref, kn_ref, qt_ref, kt_ref, vb_ref, mix_ref):
        def turned(value, gain):
            scale = lax.rsqrt(jnp.mean(value * value, 1, keepdims=True) + eps)
            return turn(value * scale * gain, cos_ref[...], sin_ref[...]).astype(jnp.bfloat16)

        kt_ref[...] = turned(k_ref[...], kn_ref[...])
        vb_ref[...] = v_ref[...].astype(jnp.bfloat16)
        for g in range(per_group):
            at = slice(g * size, (g + 1) * size)
            qt_ref[:, at] = turned(q_ref[:, at], qn_ref[...])
        for first, low, high in plan:
            span = slice(first, first + rows)
            allowed = band(rows, high - low, first, low, pos_ref[span, :])
            for g in range(per_group):
                at = slice(g * size, (g + 1) * size)
                scores = dot_nt(qt_ref[span, at], kt_ref[low:high, :]) * factor
                scores = jnp.where(allowed, scores, NEGATIVE)
                weights = jnp.exp(scores - jnp.max(scores, 1, keepdims=True))
                weights = (weights * (1.0 / jnp.sum(weights, 1, keepdims=True))).astype(jnp.bfloat16)
                mix_ref[span, at] = dot_nn(weights, vb_ref[low:high, :]).astype(jnp.bfloat16)

    group = per_group * size
    outs = tuple(shape_of((tokens, w), jnp.bfloat16) for w in (q_width, k_width, k_width, q_width))
    q_spec = pl.BlockSpec((tokens, group), lambda i, *_: (0, i))
    k_spec = pl.BlockSpec((tokens, size), lambda i, *_: (0, q_width // size + i))
    v_spec = pl.BlockSpec((tokens, size), lambda i, *_: (0, (q_width + k_width) // size + i))
    one = pl.BlockSpec((tokens, size), lambda i, *_: (0, i))
    operands = (raw, raw, raw, position, cos_wide, sin_wide, query_norm, key_norm)
    specs = [q_spec, k_spec, v_spec] + [whole_spec(a) for a in operands[3:]]
    flops = 20 * tokens * (high_sum(plan) * rows // tokens) * q_width
    return kernel_call(
        body, jnp.zeros((1,), jnp.int32), operands, specs, outs, (q_spec, one, one, q_spec), (kv_heads,), [], flops, 48
    )


def high_sum(plan):
    return sum(high - low for _, low, high in plan)


def attend_back(raw, turned_q, turned_k, values, grad_mixed, position, cos_wide, sin_wide, query_norm, key_norm, most, eps):
    tokens, q_width = turned_q.shape
    k_width = turned_k.shape[1]
    size = query_norm.shape[1]
    kv_heads, per_group = k_width // size, q_width // k_width
    factor = 1.0 / math.sqrt(size)
    rows, plan = attention_blocks(tokens, most)

    def body(_, q_ref, k_ref, qt_ref, kt_ref, v_ref, dm_ref, pos_ref, cos_ref, sin_ref, qn_ref, kn_ref,
             dq_ref, dk_ref, dv_ref, gain_ref, key_sum, value_sum):
        key_sum[...] = jnp.zeros_like(key_sum)
        value_sum[...] = jnp.zeros_like(value_sum)

        def back(raw_rows, gain, upstream, span):
            scale = lax.rsqrt(jnp.mean(raw_rows * raw_rows, 1, keepdims=True) + eps)
            turned_back = turn(upstream, cos_ref[span, :], -sin_ref[span, :])
            inner = jnp.mean(turned_back * gain * raw_rows, 1, keepdims=True)
            grad = scale * gain * turned_back - raw_rows * (scale * scale * scale * inner)
            return grad.astype(jnp.bfloat16), jnp.sum(turned_back * raw_rows * scale, 0, keepdims=True)

        query_gain = jnp.zeros((1, size), jnp.float32)
        for first, low, high in plan:
            span = slice(first, first + rows)
            allowed = band(rows, high - low, first, low, pos_ref[span, :])
            for g in range(per_group):
                at = slice(g * size, (g + 1) * size)
                queries, upstream = qt_ref[span, at], dm_ref[span, at]
                scores = dot_nt(queries, kt_ref[low:high, :]) * factor
                scores = jnp.where(allowed, scores, NEGATIVE)
                probs = jnp.exp(scores - jnp.max(scores, 1, keepdims=True))
                probs = probs * (1.0 / jnp.sum(probs, 1, keepdims=True))
                grads = dot_nt(upstream, v_ref[low:high, :])
                weighted = probs * grads
                total = jnp.sum(weighted, 1, keepdims=True)
                grads = (weighted - probs * total).astype(jnp.bfloat16)
                value_sum[low:high, :] += dot_tn(probs.astype(jnp.bfloat16), upstream)
                key_sum[low:high, :] += dot_tn(grads, queries)
                grad_turned = dot_nn(grads, kt_ref[low:high, :]) * factor
                grad, gain = back(q_ref[span, at], qn_ref[...], grad_turned, span)
                dq_ref[span, at] = grad
                query_gain = query_gain + gain
        grad, key_gain = back(k_ref[...], kn_ref[...], key_sum[...] * factor, slice(0, tokens))
        dk_ref[...] = grad
        dv_ref[...] = value_sum[...].astype(jnp.bfloat16)
        gain_ref[...] = jnp.concatenate([query_gain, key_gain, jnp.zeros((6, size), jnp.float32)], 0)

    group = per_group * size
    outs = (
        shape_of((tokens, q_width), jnp.bfloat16),
        shape_of((tokens, k_width), jnp.bfloat16),
        shape_of((tokens, k_width), jnp.bfloat16),
        shape_of((8 * kv_heads, size), jnp.float32),
    )
    q_spec = pl.BlockSpec((tokens, group), lambda i, *_: (0, i))
    k_spec = pl.BlockSpec((tokens, size), lambda i, *_: (0, q_width // size + i))
    one = pl.BlockSpec((tokens, size), lambda i, *_: (0, i))
    operands = (raw, raw, turned_q, turned_k, values, grad_mixed, position, cos_wide, sin_wide, query_norm, key_norm)
    specs = [q_spec, k_spec, q_spec, one, one, q_spec] + [whole_spec(a) for a in operands[6:]]
    out_specs = (q_spec, one, one, pl.BlockSpec((8, size), lambda i, *_: (i, 0)))
    scratch = [pltpu.VMEM((tokens, size), jnp.float32)] * 2
    flops = 28 * tokens * (high_sum(plan) * rows // tokens) * q_width
    return kernel_call(
        body, jnp.zeros((1,), jnp.int32), operands, specs, outs, out_specs, (kv_heads,), scratch, flops, 48
    )


def local(
    hidden_in,
    seq_lengths,
    attn_norm,
    w_query,
    key_weight,
    value_weight,
    query_norm,
    key_norm,
    w_output,
    ffwd_norm,
    w_gate,
    w_up,
    w_down,
    cotangent,
):
    low, f32 = jnp.bfloat16, jnp.float32
    tokens, part_width = hidden_in.shape
    full_width = part_width * lax.axis_size("col")
    head_size = query_norm.shape[0]
    q_width, k_width = w_query.shape[1], key_weight.shape[1]
    ring = Ring()
    place, plain_place, pair_place = ring.place, ring.plain_place, ring.pair_place
    steps, pairs, half = ring.half, ring.half, tokens // 2
    pair_order = jnp.arange(pairs, dtype=jnp.int32)
    chain = Chain()
    pin, run = chain.pin, chain.run

    def near(value):
        return swap(value, "col", 1)

    def far(value):
        return swap(value, "col", 2)

    qkv = pin(jnp.concatenate([w_query, key_weight, value_weight], 1))
    qkv = ring.inner_gather(qkv, 0)
    on, back = ring.send_on(qkv), ring.send_back(qkv)
    output_all = ring.gather_stack(ring.inner_gather(w_output, 1))
    hidden_far = far(hidden_in)
    gains = jnp.stack([attn_norm, ffwd_norm])
    gains_far = far(gains)
    behind, ahead = [], []
    on, back = pin(on, back)
    behind.append(on)
    ahead.append(back)
    on, back = ring.send_on(on), ring.send_back(back)
    hidden_far, gains_far = pin(hidden_far, gains_far)
    hidden_blocks = [hidden_in, hidden_far, near(hidden_in), near(hidden_far)]
    gains_near = near(gains)
    on, back, gains_near, gate, up = pin(on, back, gains_near, w_gate, w_up)
    behind.append(on)
    ahead.append(back)
    on, back = ring.send_on(on), ring.send_back(back)
    gate_up = [ring.inner_gather(w, 0) for w in (gate, up)]
    gate_up_mine = side_of(gate_up, 1, ring.parity)
    gate_up_got = ring.to_partner(side_of(gate_up, 1, 1 - ring.parity))
    gains_diagonal, gate_up_mine, *hidden_blocks = pin(near(gains_far), gate_up_mine, *hidden_blocks)
    on, back = pin(on, back)
    behind.append(on)
    ahead.append(back)
    cut = on.shape[0] // 2
    on, back = ring.send_on(on[:cut]), ring.send_back(back[cut:])
    on, back, gate_up_got = pin(on, back, gate_up_got)
    qkv_all = [qkv, *behind, jnp.concatenate([on, back], 0), *ahead[::-1]]
    gate_up, output_all = pin(jnp.concatenate([gate_up_mine, gate_up_got], 0), output_all)
    gate_up_all = pair_gather(ring, gate_up)
    gains = jnp.stack([gains, gains_far, gains_near, gains_diagonal], 1).reshape(2, 1, full_width)

    down, upstream = pin(w_down, cotangent)
    down = [ring.inner_gather(down, 1)]
    down_mine = side_of(down, 0, ring.parity)
    down_got = ring.to_partner(side_of(down, 0, 1 - ring.parity))
    up_far, up_partner = far(upstream), ring.to_partner(upstream)
    position = tables(seq_lengths[0], tokens)
    cos_wide, sin_wide = rotary(position, head_size)
    turning = (position[:, None], cos_wide, sin_wide, query_norm[None, :], key_norm[None, :])
    residual = hidden_in.astype(f32)
    wide_one, factor_one, qkv_raw = run(
        lambda blocks, gain, weights: gather_norm_matmul(place, blocks, gain, weights, EPS), hidden_blocks, gains[0], qkv_all
    )
    turned_q, turned_k, values, mixed = run(
        lambda raw: attend(raw, *turning, q_width, k_width, MOST, EPS), qkv_raw
    )
    up_far, up_partner, down_got, down_mine = pin(up_far, up_partner, down_got, down_mine)
    keep, send = run(lambda left, weights: spread_product(plain_place, left, [weights], False), mixed, output_all)
    got = near(send)
    up_near, up_diagonal = near(upstream), near(up_far)
    keep, got = pin(keep, got)
    both = keep.astype(f32) + got
    attended = far(pin(both[:, part_width:].astype(low)))
    corner = far(pin(up_partner[:half])), ring.to_partner(up_far[half:])
    up_near, up_diagonal = pin(up_near, up_diagonal)
    upstream_wide = run(lambda *blocks: assemble(pair_place, blocks), upstream, up_far, up_near, up_diagonal)
    attended, both = pin(attended, both)

    middle = residual + both[:, :part_width] + attended
    middle, middle_low = pin(middle, middle.astype(low))
    mid_far, mid_partner = far(middle_low), ring.to_partner(middle_low)
    mid_near = near(middle_low)
    up_corner = pin(jnp.concatenate(pin(*corner), 0))
    up_partner_near, up_corner_near = near(up_partner), near(up_corner)
    down_unit = pin(jnp.concatenate([down_mine, down_got], 1))
    mid_near, up_partner_near, up_corner_near = pin(mid_near, up_partner_near, up_corner_near)
    upstream_other = run(lambda *blocks: assemble(pair_place, blocks), up_partner, up_corner, up_partner_near, up_corner_near)
    mid_far = pin(mid_far)
    mid_diagonal = near(mid_far)
    mid_partner = pin(mid_partner)
    corner = far(mid_partner[:half]), ring.to_partner(mid_far[half:])
    mid_partner_near = near(mid_partner)
    gate_up_all = pin(gate_up_all)
    down_all = pair_gather(ring, pin(down_unit))
    mid_diagonal = pin(mid_diagonal)

    def swish(blocks, gain, weights):
        return gather_swish(pair_place, blocks, gain, weights, EPS)

    normed, factor_two, gate, up, hidden = run(
        swish, [middle_low, mid_far, mid_near, mid_diagonal], gains[1], gate_up_all
    )
    mid_partner_near, *corner = pin(mid_partner_near, *corner)
    mid_corner = pin(jnp.concatenate(corner, 0))
    mid_corner_near = pin(near(mid_corner))
    normed_other, _, gate_other, up_other, hidden_other = run(
        swish, [mid_partner, mid_corner, mid_partner_near, mid_corner_near], gains[1], gate_up_all
    )
    down_grad = run(
        lambda *ops: weight_grad(ops[:2], ops[2:], pair_order, False), hidden, hidden_other, upstream_wide, upstream_other
    )
    down_grad = pair_sum(ring, down_grad)

    down_all = pin(down_all)

    def back_swish(wide, weights, gate_value, up_value):
        return swish_back(wide, [weights], gate_value, up_value)

    def spread_back(left, weights, normed_rows):
        return spread_product(pair_place, left, [weights], True, normed_rows)

    low_other = run(back_swish, upstream_other, down_all, gate_other, up_other)
    keep_other, send_other, inner_other = run(spread_back, low_other, gate_up_all, normed_other)
    got_other, inner_other = near(send_other), ring.to_partner(pin(inner_other[:, 0]))
    low_mine, got_other, inner_other = run(
        back_swish, upstream_wide, down_all, gate, up, beside=(got_other, inner_other)
    )
    both_other = pin(keep_other).astype(f32) + got_other
    both_other, corner = pin(both_other, both_other[:, part_width:].astype(low))
    from_far, from_partner = far(corner[:half]), ring.to_partner(corner[half:])
    gate_up_grad, from_far, from_partner = run(
        lambda *ops: weight_grad(ops[:2], ops[2:], pair_order, True),
        normed,
        normed_other,
        low_mine,
        low_other,
        beside=(from_far, from_partner),
    )
    to_partner = jnp.concatenate([both_other[:half, :part_width] + from_far, both_other[half:, :part_width]], 0)
    to_partner, down_grad = pin(to_partner.astype(low), down_grad)
    gate_up_grad = pair_sum(ring, gate_up_grad)
    to_partner = ring.to_partner(to_partner)
    keep, send, inner = run(spread_back, low_mine, gate_up_all, normed)
    got = near(send)
    inner = pin(inner[:, 0] + inner_other)
    inner_near = near(inner)
    keep, got, inner_near = pin(keep, got, inner_near)
    both = keep.astype(f32) + got
    to_far = jnp.concatenate([both[:half, part_width:], both[half:, part_width:] + from_partner], 0)
    own, to_far, inner = pin(both[:, :part_width], to_far.astype(low), inner + inner_near)
    inner_far = far(inner)
    from_far = far(to_far)
    cut = down_grad.shape[1] // 2
    down_got = ring.to_partner(pin(down_grad[:, cut:]))

    def spread_down(left, weights):
        return spread_product(pair_place, left, [weights], False)

    out_keep_other, out_send_other = run(spread_down, hidden_other, down_all)
    out_keep, out_send, inner_far = run(spread_down, hidden, down_all, beside=(inner_far,))
    own, from_partner, from_far = pin(own, to_partner, from_far)
    grad_normed = own + from_partner + from_far
    inner = (inner + inner_far)[:, None] / full_width
    grad_middle = (
        cotangent.astype(f32)
        + factor_two * ffwd_norm * grad_normed
        - middle * (factor_two * factor_two * inner)
    )
    grad_middle, grad_low = pin(grad_middle, grad_middle.astype(low))
    grad_far, grad_near = far(grad_low), near(grad_low)
    out_got_other, out_got = near(out_send_other), near(out_send)
    out_got_other, out_got, out_keep_other = pin(out_got_other, out_got, out_keep_other)
    both_other = out_keep_other.astype(f32) + out_got_other
    both_other, corner = pin(both_other, both_other[:, part_width:].astype(low))
    grad_far, grad_near, down_got = pin(grad_far, grad_near, down_got)
    grad_diagonal = pin(near(grad_far))

    middle_wide = run(lambda *blocks: assemble(place, blocks), grad_low, grad_far, grad_near, grad_diagonal)
    grad_mixed = run(lambda wide, weights: times_transposed(wide, [weights], ring.behind), middle_wide, output_all)
    gate_up_grad = pin(gate_up_grad)
    columns_here = gate_up_grad.shape[0] // 2
    gate_up_got = ring.to_partner(pin(gate_up_grad[columns_here:]))
    out_far, out_partner = far(corner[:half]), ring.to_partner(corner[half:])
    query_low, key_low, value_low, head_gains, gate_up_got, out_far, out_partner = run(
        lambda *ops: attend_back(*ops, *turning, MOST, EPS),
        qkv_raw,
        turned_q,
        turned_k,
        values,
        grad_mixed,
        beside=(gate_up_got, out_far, out_partner),
    )
    qkv_low = pin(jnp.concatenate([query_low, key_low, value_low], 1))

    def part(j, extras):
        ops = (wide_one, middle_wide, qkv_low, mixed, *(value for value, _ in extras))
        return run(
            lambda *ops: block_grad(ops[:2], ops[2:4], j, ring.count, list(zip(ops[4:], (r for _, r in extras), strict=True))), *ops
        )

    first = part(ring.half, [])
    cut = first.shape[0] // 2
    on, back = ring.send_on(first[:cut]), ring.send_back(first[cut:])
    keep, send, inner, attn_gain, on, back = run(
        lambda left, weights, wide: spread_product(place, left, weights, True, wide, True),
        qkv_low,
        qkv_all,
        wide_one,
        beside=(on, back),
    )
    got = near(send)
    gain_keep, gain_send = attn_gain[:1, : full_width // 2], attn_gain[:1, full_width // 2 :]
    head_gains = jnp.sum(head_gains.reshape(-1, 8, head_size), 0)[:2].reshape(-1)
    sums = pin(jnp.concatenate([gain_send[0], head_gains, inner[:, 0]]))
    sums_got = near(sums)
    on = part(ring.half + 1, [(on, 0)])
    back, got, sums_got = run(
        lambda *ops: block_grad(ops[:2], ops[2:4], ring.half - 1, ring.count, [(ops[4], cut)]),
        wide_one,
        middle_wide,
        qkv_low,
        mixed,
        back,
        beside=(got, sums_got),
    )
    on, back = ring.send_on(on), ring.send_back(back)
    both_gain = gain_keep[0] + sums_got[: full_width // 2]
    sums = jnp.concatenate([both_gain[part_width:], (sums + sums_got)[full_width // 2 :]])
    sums = pin(sums)
    sums_got = far(sums)
    both = keep.astype(f32) + got
    both, to_far, sums_got = pin(both, both[:, part_width:].astype(low), sums_got)
    grad_far = far(to_far)
    to_partner = jnp.concatenate([both_other[:half, :part_width] + out_far, both_other[half:, :part_width]], 0)
    out_both = out_keep.astype(f32) + out_got
    to_far = jnp.concatenate([out_both[:half, part_width:], out_both[half:, part_width:] + out_partner], 0)
    attn_gain = (both_gain[:part_width] + sums_got[:part_width]) / attn_norm
    rest = (sums + sums_got)[part_width:]
    inner = rest[2 * head_size :][:, None] / full_width
    ffwd_gain = jnp.sum(grad_normed * middle * factor_two, 0)
    sums = jnp.concatenate([attn_gain, ffwd_gain, rest[: 2 * head_size]])
    out_own, to_partner, to_far, sums, on, back = pin(
        out_both[:, :part_width], to_partner.astype(low), to_far.astype(low), sums, on, back
    )
    on, back = part(ring.half + 2, [(on, 0)]), part(ring.half - 2, [(back, 0)])
    on, back = ring.send_on(on), ring.send_back(back)
    bit, rows = 1, lax.axis_size("row")
    sums_got = swap(sums, "row", bit)
    grad_far, sums_got = pin(grad_far, sums_got)
    out_partner, out_far = ring.to_partner(to_partner), far(to_far)
    hidden_grad = (
        grad_middle
        + factor_one * attn_norm * (both[:, :part_width] + grad_far)
        - residual * (factor_one * factor_one * inner)
    )
    sums, hidden_grad = pin(sums + sums_got, hidden_grad)
    gate_grad, up_grad = (
        pair_join(ring, gate_up_grad[:columns_here, at], gate_up_got[:, at], 1)
        for at in (slice(0, gate_up_grad.shape[1] // 2), slice(gate_up_grad.shape[1] // 2, None))
    )
    gate_grad, up_grad = pin(gate_grad, up_grad)
    bit *= 2
    sums_got = swap(sums, "row", bit)
    on, back, sums_got = pin(on, back, sums_got)
    on, back = part(ring.half + 3, [(on, 0)]), part(ring.half - 3, [(back, 0)])
    on, back = ring.send_on(on), ring.send_back(back)
    sums = pin(sums + sums_got)
    bit *= 2
    while bit < rows:
        sums = pin(sums + swap(sums, "row", bit))
        bit *= 2
    out_partner, out_far = pin(out_partner, out_far)
    hidden_out = pin((middle + out_own + out_partner + out_far).astype(low))
    down_cut = down_grad.shape[1] // 2
    down_out = pin(pair_join(ring, down_grad[:, :down_cut], down_got, 0))
    on, back = pin(on, back)
    total = ring.inner_sum(part(0, [(on, 0), (back, 0)]).astype(f32), 0)
    attn_gain, ffwd_gain, query_gain, key_gain = jnp.split(
        sums, [part_width, 2 * part_width, 2 * part_width + head_size]
    )
    return (
        hidden_out,
        hidden_grad,
        attn_gain,
        total[:, :q_width],
        total[:, q_width : q_width + k_width],
        total[:, q_width + k_width : q_width + 2 * k_width],
        query_gain,
        key_gain,
        total[:, q_width + 2 * k_width :].T,
        ffwd_gain,
        gate_grad,
        up_grad,
        down_out,
    )


def solution(mesh):
    in_specs = (
        P("row", "col"),
        P("row", None),
        P("col"),
        P("row", "col"),
        P("row", "col"),
        P("row", "col"),
        P(),
        P(),
        P("col", "row"),
        P("col"),
        P("row", "col"),
        P("row", "col"),
        P("col", "row"),
        P("row", "col"),
    )
    out_specs = (
        P("row", "col"),
        P("row", "col"),
        P("col"),
        P("row", "col"),
        P("row", "col"),
        P("row", "col"),
        P(),
        P(),
        P("col", "row"),
        P("col"),
        P("row", "col"),
        P("row", "col"),
        P("col", "row"),
    )
    return jax.shard_map(local, mesh=mesh, in_specs=in_specs, out_specs=out_specs, check_vma=False)
```

```python
import math

import jax
import jax.numpy as jnp
from jax import lax
from jax.experimental import pallas as pl
from jax.experimental.pallas import tpu as pltpu
from jax.sharding import PartitionSpec as P

EPS = 1e-06
THETA = 1000000.0
NEGATIVE = -1e30
MOST = 512
COST_SCALE = 0.02


def tables(lengths_row, row_number_total):
    steps_idx = jnp.arange(row_number_total, dtype=jnp.int32)
    seq_ends = jnp.cumsum(lengths_row)
    seq_starts = seq_ends - lengths_row
    segment = jnp.sum((steps_idx[:, None] >= seq_ends[None, :]).astype(jnp.int32), 1)
    member = segment[:, None] == jnp.arange(lengths_row.shape[0], dtype=jnp.int32)[None, :]
    return steps_idx - jnp.sum(jnp.where(member, seq_starts[None, :], 0), 1)


def rotary(position, head_size):
    half_size = head_size // 2
    frequency = THETA ** (-(jnp.arange(half_size, dtype=jnp.float32) * 2.0 / head_size))
    angles = position.astype(jnp.float32)[:, None] * frequency[None, :]
    cosines, sines = jnp.cos(angles), jnp.sin(angles)
    return jnp.concatenate([cosines, cosines], 1), jnp.concatenate([-sines, sines], 1)


def ring_order(count):
    return list(range(0, count, 2)) + list(range(count - 1, 0, -2))


class Ring:
    def __init__(self):
        rows = lax.axis_size("row")
        self.count = count = min(8, rows)
        self.half = count // 2
        self.members = members = rows // count
        self.groups = [[g * members + m for m in range(members)] for g in range(count)]
        self.lanes = None if members == 1 else [[g * members + m for g in range(count)] for m in range(members)]
        order = ring_order(count)
        self.onward = self.spell([(order[i], order[(i + 1) % count]) for i in range(count)])
        self.backward = [(b, a) for a, b in self.onward]
        self.partner = self.spell([(g, g ^ 1) for g in range(count)])
        self.pairs = [[(2 * p + side) * members + m for p in range(count // 2)] for side in range(2) for m in range(members)]
        group = lax.axis_index("row") // members
        self.parity = group % 2
        self.place = self.places([[order[(order.index(g) - j) % count] for j in range(count)] for g in range(count)])
        self.behind = jnp.array([[order[(order.index(g) - j) % count] for j in range(count)] for g in range(count)])[group]
        self.plain_place = self.places([list(range(count))] * count)
        self.pair_place = self.places(
            [[j // 2 * 2 + (g % 2 ^ j % 2) for j in range(count)] for g in range(count)]
        )

    def spell(self, pairs):
        return [(a * self.members + m, b * self.members + m) for a, b in pairs for m in range(self.members)]

    def places(self, behind):
        cols = lax.axis_size("col")
        per_col = self.count // cols
        table = [
            [[COL_ORDER.index((b // per_col) ^ c) * per_col + b % per_col for b in row] for c in range(cols)]
            for row in behind
        ]
        return jnp.array(table, jnp.int32)[lax.axis_index("row") // self.members, lax.axis_index("col")]

    def send_on(self, value):
        return lax.ppermute(value, "row", self.onward)

    def send_back(self, value):
        return lax.ppermute(value, "row", self.backward)

    def to_partner(self, value):
        return lax.ppermute(value, "row", self.partner)

    def gather_stack(self, block):
        return lax.all_gather(block, "row", axis=0, axis_index_groups=self.lanes)

    def sum_stack(self, blocks):
        return lax.psum_scatter(blocks, "row", scatter_dimension=0, axis_index_groups=self.lanes)

    def inner_gather(self, block, axis):
        if self.members == 1:
            return block
        return lax.all_gather(block, "row", axis=axis, tiled=True, axis_index_groups=self.groups)

    def inner_sum(self, value, axis):
        if self.members == 1:
            return value
        value = value.astype(jnp.bfloat16)
        return lax.psum_scatter(
            value, "row", scatter_dimension=axis, tiled=True, axis_index_groups=self.groups
        ).astype(jnp.float32)


def side_of(blocks, axis, number):
    halves = [b.shape[axis] // 2 for b in blocks]
    cuts = [lax.dynamic_slice_in_dim(b, number * h, h, axis) for b, h in zip(blocks, halves, strict=True)]
    return jnp.concatenate(cuts, axis)


def pair_gather(ring, unit):
    return lax.all_gather(unit, "row", axis=0, axis_index_groups=ring.pairs)


def pair_sum(ring, units):
    return lax.psum_scatter(units, "row", scatter_dimension=0, axis_index_groups=ring.pairs)


def pair_join(ring, mine, got, axis):
    first = ring.parity == 0
    mine, got = mine.astype(jnp.float32), got.astype(jnp.float32)
    value = jnp.concatenate([jnp.where(first, mine, got), jnp.where(first, got, mine)], axis)
    return ring.inner_sum(value, 1 - axis)


class Chain:
    def __init__(self):
        self.token = lax.create_token()

    def pin(self, *values):
        self.token, *values = lax.optimization_barrier((self.token, *values))
        return values if len(values) > 1 else values[0]

    def run(self, kernel, *operands, beside=()):
        results = kernel(*self.pin(operands))
        results = tuple(results) if isinstance(results, (list, tuple)) else (results,)
        return self.pin(*results, *beside)


COL_ORDER = (0, 2, 1, 3)


def swap(value, axis, bit):
    return lax.ppermute(value, axis, [(i, i ^ bit) for i in range(lax.axis_size(axis))])


def dot_nt(left_side, right_side):
    return lax.dot_general(
        left_side, right_side, (((1,), (1,)), ((), ())), preferred_element_type=jnp.float32
    )


def dot_nn(left_side, right_side):
    return jnp.dot(left_side, right_side, preferred_element_type=jnp.float32)


def dot_tn(left_side, right_side):
    return lax.dot_general(
        left_side, right_side, (((0,), (0,)), ((), ())), preferred_element_type=jnp.float32
    )


def cost(flops):
    return pl.CostEstimate(flops=int(COST_SCALE * flops), bytes_accessed=1 << 16, transcendentals=0)


def kernel_call(body, places, operands, specs, outs, out_specs, grid, scratch, flops, mib):
    return pl.pallas_call(
        body,
        grid_spec=pltpu.PrefetchScalarGridSpec(
            num_scalar_prefetch=1,
            grid=grid,
            in_specs=specs,
            out_specs=out_specs,
            scratch_shapes=scratch,
        ),
        out_shape=outs,
        cost_estimate=cost(flops),
        compiler_params=pltpu.CompilerParams(vmem_limit_bytes=mib << 20),
    )(places, *operands)


def whole_spec(array, buffers=1):
    zeros = (0,) * len(array.shape)
    return pl.BlockSpec(array.shape, lambda *_: zeros, pipeline_mode=pl.Buffered(buffers))


def rows_spec(array, rows):
    return pl.BlockSpec((rows,) + tuple(array.shape[1:]), lambda i, *_: (i,) + (0,) * (len(array.shape) - 1))


def columns_spec(array, columns):
    return pl.BlockSpec((array.shape[0], columns), lambda i, *_: (0, i))


def shape_of(shape, dtype):
    return jax.ShapeDtypeStruct(shape, dtype)


def piece_at(place_ref, j, piece):
    return pl.ds(pl.multiple_of(place_ref[j] * piece, piece), piece)


def norm_rows(place_ref, x_refs, gain_ref, wide_ref, factor_ref, all_ref, piece, eps):
    tokens, full = wide_ref.shape
    width = x_refs[0].shape[1]
    total = jnp.zeros((tokens, 1), jnp.float32)
    for i, x_ref in enumerate(x_refs):
        value = x_ref[...]
        all_ref[:, i * width : (i + 1) * width] = value
        value = value.astype(jnp.float32)
        total = total + jnp.sum(value * value, 1, keepdims=True)
    factor = lax.rsqrt(total / full + eps)
    factor_ref[...] = factor
    for j in range(full // piece):
        at = piece_at(place_ref, j, piece)
        value = all_ref[:, at].astype(jnp.float32) * factor * gain_ref[:, at]
        wide_ref[:, j * piece : (j + 1) * piece] = value.astype(jnp.bfloat16)


def gather_norm_matmul(place, hidden_blocks, gain, weights, eps):
    tokens, width = hidden_blocks[0].shape
    full = width * len(hidden_blocks)
    count = len(weights)
    piece, columns = weights[0].shape
    tile = min(512, columns)
    many = len(hidden_blocks)

    def body(place_ref, *refs):
        x_refs, gain_ref = refs[:many], refs[many]
        w_refs = refs[many + 1 : many + 1 + count]
        wide_ref, factor_ref, out_ref, all_ref = refs[many + 1 + count :]

        @pl.when(pl.program_id(0) == 0)
        def _():
            norm_rows(place_ref, x_refs, gain_ref, wide_ref, factor_ref, all_ref, piece, eps)

        total = dot_nn(wide_ref[:, :piece], w_refs[0][...])
        for j in range(1, count):
            total = total + dot_nn(wide_ref[:, j * piece : (j + 1) * piece], w_refs[j][...])
        out_ref[...] = total

    outs = (
        shape_of((tokens, full), jnp.bfloat16),
        shape_of((tokens, 1), jnp.float32),
        shape_of((tokens, columns), jnp.float32),
    )
    operands = (*hidden_blocks, gain, *weights)
    specs = [whole_spec(b) for b in hidden_blocks] + [whole_spec(gain)] + [columns_spec(w, tile) for w in weights]
    out_specs = (whole_spec(outs[0]), whole_spec(outs[1]), columns_spec(outs[2], tile))
    scratch = [pltpu.VMEM((tokens, full), jnp.bfloat16)]
    return kernel_call(
        body, place, operands, specs, outs, out_specs, (columns // tile,), scratch, 2 * tokens * full * columns, 48
    )


def units_of(refs):
    return [refs[0].at[j] for j in range(refs[0].shape[0])] if len(refs) == 1 else refs


def gather_swish(place, blocks, gain, weights, eps):
    tokens, width = blocks[0].shape
    count, unit, both = weights.shape
    columns = both // 2
    full, many = width * len(blocks), len(blocks)
    piece = full // place.shape[0]
    tile = min(256, columns)

    def body(place_ref, *refs):
        x_refs, gain_ref, g_ref, u_ref = refs[:many], refs[many], refs[many + 1], refs[many + 2]
        wide_ref, factor_ref, gate_ref, up_ref, hidden_ref, all_ref = refs[many + 3 :]

        @pl.when(pl.program_id(0) == 0)
        def _():
            norm_rows(place_ref, x_refs, gain_ref, wide_ref, factor_ref, all_ref, piece, eps)

        def product(w_ref):
            total = dot_nn(wide_ref[:, :unit], w_ref[0])
            for j in range(1, count):
                total = total + dot_nn(wide_ref[:, j * unit : (j + 1) * unit], w_ref[j])
            return total

        gate = product(g_ref)
        gate_ref[...] = gate
        up = product(u_ref)
        up_ref[...] = up
        hidden_ref[...] = (gate / (1.0 + jnp.exp(-gate)) * up).astype(jnp.bfloat16)

    outs = (
        shape_of((tokens, full), jnp.bfloat16),
        shape_of((tokens, 1), jnp.float32),
        shape_of((tokens, columns), jnp.float32),
        shape_of((tokens, columns), jnp.float32),
        shape_of((tokens, columns), jnp.bfloat16),
    )
    operands = (*blocks, gain, weights, weights)
    steps = columns // tile
    specs = [whole_spec(b) for b in (*blocks, gain)] + [
        pl.BlockSpec((count, unit, tile), lambda i, *_: (0, 0, i)),
        pl.BlockSpec((count, unit, tile), lambda i, *_: (0, 0, i + steps)),
    ]
    out_specs = (whole_spec(outs[0]), whole_spec(outs[1])) + tuple(columns_spec(o, tile) for o in outs[2:])
    scratch = [pltpu.VMEM((tokens, full), jnp.bfloat16)]
    return kernel_call(
        body, place, operands, specs, outs, out_specs, (steps,), scratch, 4 * tokens * full * columns, 48
    )


def spread_product(place, left, weights, transposed, normed=None, by_feature=False):
    tokens, inner = left.shape
    many = len(weights)
    count = many if many > 1 else weights[0].shape[0]
    unit = weights[0].shape[-2 if transposed else -1]
    full = unit * count
    piece = full // place.shape[0]
    per_unit = unit // piece
    tile = min(256, tokens)
    dot = dot_nt if transposed else dot_nn
    extras = () if normed is None else (normed,)

    def body(place_ref, *refs):
        y_ref, w_refs = refs[0], units_of(refs[1 : 1 + many])
        rest = refs[1 + many + len(extras) :]
        keep_ref, send_ref, all_ref = rest[0], rest[1], rest[-1]
        rows = jnp.zeros((tile, 1), jnp.float32)
        if by_feature:

            @pl.when(pl.program_id(0) == 0)
            def _():
                rest[3][...] = jnp.zeros_like(rest[3])

        for j in range(count):
            total = dot(y_ref[...], w_refs[j][...])
            if extras:
                weighted = total * refs[1 + many][:, j * unit : (j + 1) * unit].astype(jnp.float32)
                rows = rows + jnp.sum(weighted, 1, keepdims=True)
                if by_feature:
                    sums = jnp.broadcast_to(jnp.sum(weighted, 0, keepdims=True), (8, unit))
                    for i in range(per_unit):
                        at = piece_at(place_ref, j * per_unit + i, piece)
                        rest[3][:, at] += sums[:, i * piece : (i + 1) * piece]
            total = total.astype(jnp.bfloat16)
            for i in range(per_unit):
                at = piece_at(place_ref, j * per_unit + i, piece)
                all_ref[:, at] = total[:, i * piece : (i + 1) * piece]
        keep_ref[...] = all_ref[:, : full // 2]
        send_ref[...] = all_ref[:, full // 2 :]
        if extras:
            rest[2][...] = rows

    outs = (shape_of((tokens, full // 2), jnp.bfloat16),) * 2
    if extras:
        outs += (shape_of((tokens, 1), jnp.float32),)
    operands = (left, *weights, *extras)
    specs = [rows_spec(left, tile)] + [whole_spec(w) for w in weights] + [rows_spec(e, tile) for e in extras]
    out_specs = tuple(rows_spec(o, tile) for o in outs)
    if by_feature:
        outs += (shape_of((8, full), jnp.float32),)
        out_specs += (whole_spec(outs[3]),)
    scratch = [pltpu.VMEM((tile, full), jnp.bfloat16)]
    return kernel_call(
        body, place, operands, specs, outs, out_specs, (tokens // tile,), scratch, 2 * tokens * full * inner, 48
    )


def assemble(place, blocks):
    tokens, width = blocks[0].shape
    many = len(blocks)
    full = width * many
    piece = full // place.shape[0]
    tile = min(256, tokens)

    def body(place_ref, *refs):
        x_refs, (wide_ref, all_ref) = refs[:many], refs[many:]
        for i in range(many):
            all_ref[:, i * width : (i + 1) * width] = x_refs[i][...]
        for j in range(full // piece):
            wide_ref[:, j * piece : (j + 1) * piece] = all_ref[:, piece_at(place_ref, j, piece)]

    outs = (shape_of((tokens, full), jnp.bfloat16),)
    specs = [rows_spec(b, tile) for b in blocks]
    scratch = [pltpu.VMEM((tile, full), jnp.bfloat16)]
    return kernel_call(
        body, place, blocks, specs, outs, (rows_spec(outs[0], tile),), (tokens // tile,), scratch, 1500 * tokens * 1024, 32
    )[0]


def times_transposed(wide, weights, order):
    return back_product(wide, weights, (), lambda total: (total,), order)


def swish_back(wide, weights, gate, up):
    def gradients(total, gate_value, up_value):
        sigma = 1.0 / (1.0 + jnp.exp(-gate_value))
        grad_gate = total * up_value * sigma * (1.0 + gate_value * (1.0 - sigma))
        return grad_gate, total * gate_value * sigma

    return back_product(wide, weights, (gate, up), gradients)


def back_product(wide, weights, extras, epilogue, order=None):
    tokens, full = wide.shape
    others, units = len(extras), len(weights)
    count = units if units > 1 else weights[0].shape[0]
    columns, unit = weights[0].shape[-2:]
    tile = min(256, tokens)
    parts = max(1, others)

    stacked = order is not None

    def body(order_ref, *refs):
        wide_ref, extra_refs = refs[0], refs[1 : 1 + others]
        w_refs, out_ref = refs[1 + others : -1], refs[-1]
        if not stacked:
            w_refs = units_of(w_refs)
        else:
            w_refs = [w_refs[0].at[order_ref[j]] for j in range(count)]
        total = dot_nt(wide_ref[:, :unit], w_refs[0][...])
        for j in range(1, count):
            total = total + dot_nt(wide_ref[:, j * unit : (j + 1) * unit], w_refs[j][...])
        for i, part in enumerate(epilogue(total, *(e[...] for e in extra_refs))):
            out_ref[:, i * columns : (i + 1) * columns] = part.astype(jnp.bfloat16)

    outs = (shape_of((tokens, parts * columns), jnp.bfloat16),)
    operands = (wide, *extras, *weights)
    specs = [rows_spec(b, tile) for b in (wide, *extras)] + [whole_spec(w) for w in weights]
    order = order if stacked else jnp.zeros((1,), jnp.int32)
    return kernel_call(
        body, order, operands, specs, outs, (rows_spec(outs[0], tile),), (tokens // tile,), [],
        2 * tokens * full * columns, 48,
    )[0]


def weight_grad(lefts, rights, order, by_left):
    tokens, rows = lefts[0].shape
    columns = rights[0].shape[1]
    many = len(lefts)
    units = order.shape[0]
    rows, columns = (rows // units, columns) if by_left else (rows, columns // units)

    def body(_, *refs):
        out_ref = refs[-1]
        total = dot_tn(refs[0][...], refs[many][...])
        for c in range(1, many):
            total = total + dot_tn(refs[c][...], refs[many + c][...])
        out_ref[0] = total.astype(jnp.bfloat16)

    outs = (shape_of((units, rows, columns), jnp.bfloat16),)
    moving = pl.BlockSpec((tokens, rows if by_left else columns), lambda i, *_: (0, i))
    left_specs = [moving if by_left else whole_spec(a) for a in lefts]
    right_specs = [whole_spec(a) if by_left else moving for a in rights]
    out_specs = (pl.BlockSpec((1, rows, columns), lambda i, order_ref: (order_ref[i], 0, 0)),)
    flops = 2 * tokens * many * units * rows * columns
    operands = (*lefts, *rights)
    return kernel_call(
        body, order, operands, left_specs + right_specs, outs, out_specs, (units,), [], flops, 56
    )[0]


def block_grads(lefts, rights, order, count):
    tokens, full = lefts[0].shape
    rows = full // count
    widths = [right.shape[1] for right in rights]
    many, steps = len(lefts), order.shape[0]

    def body(_, *refs):
        start = 0
        for c, width in enumerate(widths):
            refs[-1][0, :, start : start + width] = dot_tn(refs[c][...], refs[many + c][...]).astype(jnp.bfloat16)
            start += width

    outs = (shape_of((steps, rows, sum(widths)), jnp.bfloat16),)
    operands = (*lefts, *rights)
    specs = [pl.BlockSpec((tokens, rows), lambda i, order_ref: (0, order_ref[i]))] * many
    specs += [whole_spec(a) for a in operands[many:]]
    return kernel_call(
        body, order, operands, specs, outs, (pl.BlockSpec((1, rows, sum(widths)), lambda i, *_: (i, 0, 0)),), (steps,), [],
        2 * tokens * steps * rows * sum(widths), 60,
    )[0]


def turn(values, cos_wide, sin_wide):
    return values * cos_wide + pltpu.roll(values, values.shape[1] // 2, 1) * sin_wide


def band(rows, cols, first_row, first_col, position):
    distance = (
        lax.broadcasted_iota(jnp.int32, (rows, cols), 0)
        + (first_row - first_col)
        - lax.broadcasted_iota(jnp.int32, (rows, cols), 1)
    )
    return (distance >= 0) & (distance <= position)


def attention_blocks(tokens, most):
    rows = min(256, tokens)
    reach = -(-(most - 1) // rows)
    return rows, [(i * rows, max(0, i - reach) * rows, (i + 1) * rows) for i in range(tokens // rows)]


def attend(raw, position, cos_wide, sin_wide, query_norm, key_norm, q_width, k_width, most, eps):
    tokens = raw.shape[0]
    size = query_norm.shape[1]
    kv_heads, per_group = k_width // size, q_width // k_width
    factor = 1.0 / math.sqrt(size)
    rows, plan = attention_blocks(tokens, most)

    def body(_, q_ref, k_ref, v_ref, pos_ref, cos_ref, sin_ref, qn_ref, kn_ref, qt_ref, kt_ref, vb_ref, mix_ref):
        def turned(value, gain):
            scale = lax.rsqrt(jnp.mean(value * value, 1, keepdims=True) + eps)
            return turn(value * scale * gain, cos_ref[...], sin_ref[...]).astype(jnp.bfloat16)

        kt_ref[...] = turned(k_ref[...], kn_ref[...])
        vb_ref[...] = v_ref[...].astype(jnp.bfloat16)
        for g in range(per_group):
            at = slice(g * size, (g + 1) * size)
            qt_ref[:, at] = turned(q_ref[:, at], qn_ref[...])
        for first, low, high in plan:
            span = slice(first, first + rows)
            allowed = band(rows, high - low, first, low, pos_ref[span, :])
            for g in range(per_group):
                at = slice(g * size, (g + 1) * size)
                scores = dot_nt(qt_ref[span, at], kt_ref[low:high, :]) * factor
                scores = jnp.where(allowed, scores, NEGATIVE)
                weights = jnp.exp(scores - jnp.max(scores, 1, keepdims=True))
                weights = (weights * (1.0 / jnp.sum(weights, 1, keepdims=True))).astype(jnp.bfloat16)
                mix_ref[span, at] = dot_nn(weights, vb_ref[low:high, :]).astype(jnp.bfloat16)

    group = per_group * size
    outs = tuple(shape_of((tokens, w), jnp.bfloat16) for w in (q_width, k_width, k_width, q_width))
    q_spec = pl.BlockSpec((tokens, group), lambda i, *_: (0, i))
    k_spec = pl.BlockSpec((tokens, size), lambda i, *_: (0, q_width // size + i))
    v_spec = pl.BlockSpec((tokens, size), lambda i, *_: (0, (q_width + k_width) // size + i))
    one = pl.BlockSpec((tokens, size), lambda i, *_: (0, i))
    operands = (raw, raw, raw, position, cos_wide, sin_wide, query_norm, key_norm)
    specs = [q_spec, k_spec, v_spec] + [whole_spec(a) for a in operands[3:]]
    flops = 20 * tokens * (high_sum(plan) * rows // tokens) * q_width
    return kernel_call(
        body, jnp.zeros((1,), jnp.int32), operands, specs, outs, (q_spec, one, one, q_spec), (kv_heads,), [], flops, 48
    )


def high_sum(plan):
    return sum(high - low for _, low, high in plan)


def attend_back(raw, turned_q, turned_k, values, grad_mixed, position, cos_wide, sin_wide, query_norm, key_norm, most, eps):
    tokens, q_width = turned_q.shape
    k_width = turned_k.shape[1]
    size = query_norm.shape[1]
    kv_heads, per_group = k_width // size, q_width // k_width
    factor = 1.0 / math.sqrt(size)
    rows, plan = attention_blocks(tokens, most)

    def body(_, q_ref, k_ref, qt_ref, kt_ref, v_ref, dm_ref, pos_ref, cos_ref, sin_ref, qn_ref, kn_ref,
             dq_ref, dk_ref, dv_ref, gain_ref, key_sum, value_sum):
        key_sum[...] = jnp.zeros_like(key_sum)
        value_sum[...] = jnp.zeros_like(value_sum)

        def back(raw_rows, gain, upstream, span):
            scale = lax.rsqrt(jnp.mean(raw_rows * raw_rows, 1, keepdims=True) + eps)
            turned_back = turn(upstream, cos_ref[span, :], -sin_ref[span, :])
            inner = jnp.mean(turned_back * gain * raw_rows, 1, keepdims=True)
            grad = scale * gain * turned_back - raw_rows * (scale * scale * scale * inner)
            return grad.astype(jnp.bfloat16), jnp.sum(turned_back * raw_rows * scale, 0, keepdims=True)

        query_gain = jnp.zeros((1, size), jnp.float32)
        for first, low, high in plan:
            span = slice(first, first + rows)
            allowed = band(rows, high - low, first, low, pos_ref[span, :])
            for g in range(per_group):
                at = slice(g * size, (g + 1) * size)
                queries, upstream = qt_ref[span, at], dm_ref[span, at]
                scores = dot_nt(queries, kt_ref[low:high, :]) * factor
                scores = jnp.where(allowed, scores, NEGATIVE)
                probs = jnp.exp(scores - jnp.max(scores, 1, keepdims=True))
                probs = probs * (1.0 / jnp.sum(probs, 1, keepdims=True))
                grads = dot_nt(upstream, v_ref[low:high, :])
                weighted = probs * grads
                total = jnp.sum(weighted, 1, keepdims=True)
                grads = (weighted - probs * total).astype(jnp.bfloat16)
                value_sum[low:high, :] += dot_tn(probs.astype(jnp.bfloat16), upstream)
                key_sum[low:high, :] += dot_tn(grads, queries)
                grad_turned = dot_nn(grads, kt_ref[low:high, :]) * factor
                grad, gain = back(q_ref[span, at], qn_ref[...], grad_turned, span)
                dq_ref[span, at] = grad
                query_gain = query_gain + gain
        grad, key_gain = back(k_ref[...], kn_ref[...], key_sum[...] * factor, slice(0, tokens))
        dk_ref[...] = grad
        dv_ref[...] = value_sum[...].astype(jnp.bfloat16)
        gain_ref[...] = jnp.concatenate([query_gain, key_gain, jnp.zeros((6, size), jnp.float32)], 0)

    group = per_group * size
    outs = (
        shape_of((tokens, q_width), jnp.bfloat16),
        shape_of((tokens, k_width), jnp.bfloat16),
        shape_of((tokens, k_width), jnp.bfloat16),
        shape_of((8 * kv_heads, size), jnp.float32),
    )
    q_spec = pl.BlockSpec((tokens, group), lambda i, *_: (0, i))
    k_spec = pl.BlockSpec((tokens, size), lambda i, *_: (0, q_width // size + i))
    one = pl.BlockSpec((tokens, size), lambda i, *_: (0, i))
    operands = (raw, raw, turned_q, turned_k, values, grad_mixed, position, cos_wide, sin_wide, query_norm, key_norm)
    specs = [q_spec, k_spec, q_spec, one, one, q_spec] + [whole_spec(a) for a in operands[6:]]
    out_specs = (q_spec, one, one, pl.BlockSpec((8, size), lambda i, *_: (i, 0)))
    scratch = [pltpu.VMEM((tokens, size), jnp.float32)] * 2
    flops = 28 * tokens * (high_sum(plan) * rows // tokens) * q_width
    return kernel_call(
        body, jnp.zeros((1,), jnp.int32), operands, specs, outs, out_specs, (kv_heads,), scratch, flops, 48
    )


def local(
    hidden_in,
    seq_lengths,
    attn_norm,
    w_query,
    key_weight,
    value_weight,
    query_norm,
    key_norm,
    w_output,
    ffwd_norm,
    w_gate,
    w_up,
    w_down,
    cotangent,
):
    low, f32 = jnp.bfloat16, jnp.float32
    tokens, part_width = hidden_in.shape
    full_width = part_width * lax.axis_size("col")
    head_size = query_norm.shape[0]
    q_width, k_width = w_query.shape[1], key_weight.shape[1]
    ring = Ring()
    place, plain_place, pair_place = ring.place, ring.plain_place, ring.pair_place
    steps, pairs, half = ring.half, ring.half, tokens // 2
    pair_order = jnp.arange(pairs, dtype=jnp.int32)
    chain = Chain()
    pin, run = chain.pin, chain.run

    def near(value):
        return swap(value, "col", 1)

    def far(value):
        return swap(value, "col", 2)

    qkv = pin(jnp.concatenate([w_query, key_weight, value_weight], 1))
    qkv = ring.inner_gather(qkv, 0)
    on, back = ring.send_on(qkv), ring.send_back(qkv)
    output_all = ring.gather_stack(ring.inner_gather(w_output, 1))
    hidden_far = far(hidden_in)
    gains = jnp.stack([attn_norm, ffwd_norm])
    gains_far = far(gains)
    behind, ahead = [], []
    on, back = pin(on, back)
    behind.append(on)
    ahead.append(back)
    on, back = ring.send_on(on), ring.send_back(back)
    hidden_far, gains_far = pin(hidden_far, gains_far)
    hidden_blocks = [hidden_in, hidden_far, near(hidden_in), near(hidden_far)]
    gains_near = near(gains)
    on, back, gains_near, gate, up = pin(on, back, gains_near, w_gate, w_up)
    behind.append(on)
    ahead.append(back)
    on, back = ring.send_on(on), ring.send_back(back)
    gate_up = [ring.inner_gather(w, 0) for w in (gate, up)]
    gate_up_mine = side_of(gate_up, 1, ring.parity)
    gate_up_got = ring.to_partner(side_of(gate_up, 1, 1 - ring.parity))
    gains_diagonal, gate_up_mine, *hidden_blocks = pin(near(gains_far), gate_up_mine, *hidden_blocks)
    on, back = pin(on, back)
    behind.append(on)
    ahead.append(back)
    cut = on.shape[0] // 2
    on, back = ring.send_on(on[:cut]), ring.send_back(back[cut:])
    on, back, gate_up_got = pin(on, back, gate_up_got)
    qkv_all = [qkv, *behind, jnp.concatenate([on, back], 0), *ahead[::-1]]
    gate_up, output_all = pin(jnp.concatenate([gate_up_mine, gate_up_got], 0), output_all)
    gate_up_all = pair_gather(ring, gate_up)
    gains = jnp.stack([gains, gains_far, gains_near, gains_diagonal], 1).reshape(2, 1, full_width)

    down, upstream = pin(w_down, cotangent)
    down = [ring.inner_gather(down, 1)]
    down_mine = side_of(down, 0, ring.parity)
    down_got = ring.to_partner(side_of(down, 0, 1 - ring.parity))
    up_far, up_partner = far(upstream), ring.to_partner(upstream)
    position = tables(seq_lengths[0], tokens)
    cos_wide, sin_wide = rotary(position, head_size)
    turning = (position[:, None], cos_wide, sin_wide, query_norm[None, :], key_norm[None, :])
    residual = hidden_in.astype(f32)
    wide_one, factor_one, qkv_raw = run(
        lambda blocks, gain, weights: gather_norm_matmul(place, blocks, gain, weights, EPS), hidden_blocks, gains[0], qkv_all
    )
    turned_q, turned_k, values, mixed = run(
        lambda raw: attend(raw, *turning, q_width, k_width, MOST, EPS), qkv_raw
    )
    up_far, up_partner, down_got, down_mine = pin(up_far, up_partner, down_got, down_mine)
    keep, send = run(lambda left, weights: spread_product(plain_place, left, [weights], False), mixed, output_all)
    got = near(send)
    up_near, up_diagonal = near(upstream), near(up_far)
    keep, got = pin(keep, got)
    both = keep.astype(f32) + got
    attended = far(pin(both[:, part_width:].astype(low)))
    corner = far(pin(up_partner[:half])), ring.to_partner(up_far[half:])
    up_near, up_diagonal = pin(up_near, up_diagonal)
    upstream_wide = run(lambda *blocks: assemble(pair_place, blocks), upstream, up_far, up_near, up_diagonal)
    attended, both = pin(attended, both)

    middle = residual + both[:, :part_width] + attended
    middle, middle_low = pin(middle, middle.astype(low))
    mid_far, mid_partner = far(middle_low), ring.to_partner(middle_low)
    mid_near = near(middle_low)
    up_corner = pin(jnp.concatenate(pin(*corner), 0))
    up_partner_near, up_corner_near = near(up_partner), near(up_corner)
    down_unit = pin(jnp.concatenate([down_mine, down_got], 1))
    mid_near, up_partner_near, up_corner_near = pin(mid_near, up_partner_near, up_corner_near)
    upstream_other = run(lambda *blocks: assemble(pair_place, blocks), up_partner, up_corner, up_partner_near, up_corner_near)
    mid_far = pin(mid_far)
    mid_diagonal = near(mid_far)
    mid_partner = pin(mid_partner)
    corner = far(mid_partner[:half]), ring.to_partner(mid_far[half:])
    mid_partner_near = near(mid_partner)
    gate_up_all = pin(gate_up_all)
    down_all = pair_gather(ring, pin(down_unit))
    mid_diagonal = pin(mid_diagonal)

    def swish(blocks, gain, weights):
        return gather_swish(pair_place, blocks, gain, weights, EPS)

    normed, factor_two, gate, up, hidden = run(
        swish, [middle_low, mid_far, mid_near, mid_diagonal], gains[1], gate_up_all
    )
    mid_partner_near, *corner = pin(mid_partner_near, *corner)
    mid_corner = pin(jnp.concatenate(corner, 0))
    mid_corner_near = pin(near(mid_corner))
    normed_other, _, gate_other, up_other, hidden_other = run(
        swish, [mid_partner, mid_corner, mid_partner_near, mid_corner_near], gains[1], gate_up_all
    )
    down_grad = run(
        lambda *ops: weight_grad(ops[:2], ops[2:], pair_order, False), hidden, hidden_other, upstream_wide, upstream_other
    )
    down_grad = pair_sum(ring, down_grad)

    down_all = pin(down_all)

    def back_swish(wide, weights, gate_value, up_value):
        return swish_back(wide, [weights], gate_value, up_value)

    def spread_back(left, weights, normed_rows):
        return spread_product(pair_place, left, [weights], True, normed_rows)

    low_other = run(back_swish, upstream_other, down_all, gate_other, up_other)
    keep_other, send_other, inner_other = run(spread_back, low_other, gate_up_all, normed_other)
    got_other, inner_other = near(send_other), ring.to_partner(pin(inner_other[:, 0]))
    low_mine, got_other, inner_other = run(
        back_swish, upstream_wide, down_all, gate, up, beside=(got_other, inner_other)
    )
    both_other = pin(keep_other).astype(f32) + got_other
    both_other, corner = pin(both_other, both_other[:, part_width:].astype(low))
    from_far, from_partner = far(corner[:half]), ring.to_partner(corner[half:])
    keep, send, inner, from_far, from_partner = run(
        spread_back, low_mine, gate_up_all, normed, beside=(from_far, from_partner)
    )
    got = near(send)
    inner = pin(inner[:, 0] + inner_other)
    inner_near = near(inner)
    to_partner = jnp.concatenate([both_other[:half, :part_width] + from_far, both_other[half:, :part_width]], 0)
    keep, got, inner_near, to_partner = pin(keep, got, inner_near, to_partner.astype(low))
    to_partner = ring.to_partner(to_partner)
    both = keep.astype(f32) + got
    to_far = jnp.concatenate([both[:half, part_width:], both[half:, part_width:] + from_partner], 0)
    own, to_far, inner = pin(both[:, :part_width], to_far.astype(low), inner + inner_near)
    inner_far = far(inner)
    from_far = far(to_far)
    gate_up_grad = run(
        lambda *ops: weight_grad(ops[:2], ops[2:], pair_order, True), normed, normed_other, low_mine, low_other
    )
    own, from_partner, from_far, inner_far, down_grad, gate_up_grad = pin(
        own, to_partner, from_far, inner_far, down_grad, gate_up_grad
    )
    gate_up_grad = pair_sum(ring, gate_up_grad)

    def spread_down(left, weights):
        return spread_product(pair_place, left, [weights], False)

    grad_normed = own + from_partner + from_far
    inner = (inner + inner_far)[:, None] / full_width
    grad_middle = (
        cotangent.astype(f32)
        + factor_two * ffwd_norm * grad_normed
        - middle * (factor_two * factor_two * inner)
    )
    grad_middle, grad_low = pin(grad_middle, grad_middle.astype(low))
    grad_far, grad_near = far(grad_low), near(grad_low)
    down_got = ring.to_partner(pin(down_grad[:, down_grad.shape[1] // 2 :]))
    out_keep_other, out_send_other = run(spread_down, hidden_other, down_all)
    out_keep, out_send, grad_near, down_got = run(spread_down, hidden, down_all, beside=(grad_near, down_got))
    grad_far = pin(grad_far)
    grad_diagonal = near(grad_far)
    out_got_other, out_got = near(out_send_other), near(out_send)
    out_got_other, out_got, out_keep_other, grad_diagonal = pin(out_got_other, out_got, out_keep_other, grad_diagonal)
    out_other = pin((out_keep_other.astype(f32) + out_got_other).astype(low))
    out_partner = ring.to_partner(out_other)
    ffwd_gain = pin(jnp.sum(grad_normed * middle * factor_two, 0))

    middle_wide = run(lambda *blocks: assemble(place, blocks), grad_low, grad_far, grad_near, grad_diagonal)
    grad_mixed = run(lambda wide, weights: times_transposed(wide, [weights], ring.behind), middle_wide, output_all)
    query_low, key_low, value_low, head_gains = run(
        lambda *ops: attend_back(*ops, *turning, MOST, EPS), qkv_raw, turned_q, turned_k, values, grad_mixed
    )
    qkv_low = pin(jnp.concatenate([query_low, key_low, value_low], 1))

    def parts(*numbers, beside=()):
        order = jnp.array(numbers, jnp.int32)
        return run(
            lambda *ops: block_grads(ops[:2], ops[2:], order, ring.count), wide_one, middle_wide, qkv_low, mixed, beside=beside
        )

    def go(on, back, *beside):
        on, back, *beside = pin(on.astype(low), back.astype(low), *beside)
        return ring.send_on(on), ring.send_back(back), *beside

    first = parts(steps)[0]
    cut = first.shape[0] // 2
    on, back = go(first[:cut], first[cut:])
    own, on, back = parts(steps + 1, steps - 1, beside=(on, back))
    on = jnp.concatenate([own[0, :cut] + on.astype(f32), own[0, cut:].astype(f32)], 0)
    back = jnp.concatenate([own[1, :cut].astype(f32), own[1, cut:] + back.astype(f32)], 0)
    on, back = go(on, back)
    keep, send, inner, attn_gain = run(
        lambda left, weights, wide: spread_product(place, left, weights, True, wide, True), qkv_low, qkv_all, wide_one
    )
    got = near(send)
    own, out_partner, got = parts(
        *(n for s in range(2, steps) for n in (steps + s, steps - s)), 0, beside=(out_partner, got)
    )
    gain_keep, gain_send = attn_gain[:1, : full_width // 2], attn_gain[:1, full_width // 2 :]
    head_gains = jnp.sum(head_gains.reshape(-1, 8, head_size), 0)[:2].reshape(-1)
    sums = pin(jnp.concatenate([gain_send[0], head_gains, inner[:, 0]]))
    sums_got, keep, gate_up_grad = pin(near(sums), keep, gate_up_grad)
    both = keep.astype(f32) + got
    both_gain = gain_keep[0] + sums_got[: full_width // 2]
    sums = jnp.concatenate([both_gain[part_width:], (sums + sums_got)[full_width // 2 :]])
    both, to_far, sums = pin(both, both[:, part_width:].astype(low), sums)
    sums_got = far(sums)
    grad_far = far(to_far)
    columns_here = gate_up_grad.shape[0] // 2
    gate_up_got = ring.to_partner(pin(gate_up_grad[columns_here:]))
    on, back = pin(on, back)
    on, back, sums_got = go(own[0] + on.astype(f32), own[1] + back.astype(f32), sums_got)
    attn_gain = (both_gain[:part_width] + sums_got[:part_width]) / attn_norm
    rest = (sums + sums_got)[part_width:]
    inner = rest[2 * head_size :][:, None] / full_width
    sums = jnp.concatenate([attn_gain, ffwd_gain, rest[: 2 * head_size]])
    sums, grad_far, out_keep, out_got = pin(sums, grad_far, out_keep, out_got)
    bit, rows = 1, lax.axis_size("row")
    sums_got = swap(sums, "row", bit)
    out_both = out_keep.astype(f32) + out_got + out_partner
    out_own, to_far = pin(out_both[:, :part_width], out_both[:, part_width:].astype(low))
    out_far = far(to_far)
    hidden_grad = (
        grad_middle
        + factor_one * attn_norm * (both[:, :part_width] + grad_far)
        - residual * (factor_one * factor_one * inner)
    )
    hidden_grad, on, back, sums_got = pin(hidden_grad, on, back, sums_got)
    on, back, gate_up_grad, gate_up_got, down_got = go(
        own[2] + on.astype(f32), own[3] + back.astype(f32), gate_up_grad, gate_up_got, down_got
    )
    sums = pin(sums + sums_got)
    bit *= 2
    sums_got = swap(sums, "row", bit)
    gate_grad, up_grad = (
        pair_join(ring, gate_up_grad[:columns_here, at], gate_up_got[:, at], 1)
        for at in (slice(0, gate_up_grad.shape[1] // 2), slice(gate_up_grad.shape[1] // 2, None))
    )
    down_out = pair_join(ring, down_grad[:, : down_grad.shape[1] // 2], down_got, 0)
    gate_grad, up_grad, down_out, sums_got = pin(gate_grad, up_grad, down_out, sums_got)
    sums = pin(sums + sums_got)
    bit *= 2
    while bit < rows:
        sums_got = swap(sums, "row", bit)
        bit *= 2
        if bit < rows:
            sums = pin(sums + sums_got)
    on, back, sums_got, out_far = pin(on, back, sums_got, out_far)
    sums = sums + sums_got
    total = ring.inner_sum(own[4].astype(f32) + on + back, 0)
    hidden_out = (middle + out_own + out_far).astype(low)
    attn_gain, ffwd_gain, query_gain, key_gain = jnp.split(
        sums, [part_width, 2 * part_width, 2 * part_width + head_size]
    )
    return (
        hidden_out,
        hidden_grad,
        attn_gain,
        total[:, :q_width],
        total[:, q_width : q_width + k_width],
        total[:, q_width + k_width : q_width + 2 * k_width],
        query_gain,
        key_gain,
        total[:, q_width + 2 * k_width :].T,
        ffwd_gain,
        gate_grad,
        up_grad,
        down_out,
    )


def solution(mesh):
    in_specs = (
        P("row", "col"),
        P("row", None),
        P("col"),
        P("row", "col"),
        P("row", "col"),
        P("row", "col"),
        P(),
        P(),
        P("col", "row"),
        P("col"),
        P("row", "col"),
        P("row", "col"),
        P("col", "row"),
        P("row", "col"),
    )
    out_specs = (
        P("row", "col"),
        P("row", "col"),
        P("col"),
        P("row", "col"),
        P("row", "col"),
        P("row", "col"),
        P(),
        P(),
        P("col", "row"),
        P("col"),
        P("row", "col"),
        P("row", "col"),
        P("col", "row"),
    )
    return jax.shard_map(local, mesh=mesh, in_specs=in_specs, out_specs=out_specs, check_vma=False)
```

```python
import math

import jax
import jax.numpy as jnp
from jax import lax
from jax.experimental import pallas as pl
from jax.experimental.pallas import tpu as pltpu
from jax.sharding import PartitionSpec as P

EPS = 1e-06
THETA = 1000000.0
NEGATIVE = -1e30
MOST = 512
COST_SCALE = 0.02


def tables(lengths_row, row_number_total):
    steps_idx = jnp.arange(row_number_total, dtype=jnp.int32)
    seq_ends = jnp.cumsum(lengths_row)
    seq_starts = seq_ends - lengths_row
    segment = jnp.sum((steps_idx[:, None] >= seq_ends[None, :]).astype(jnp.int32), 1)
    member = segment[:, None] == jnp.arange(lengths_row.shape[0], dtype=jnp.int32)[None, :]
    return steps_idx - jnp.sum(jnp.where(member, seq_starts[None, :], 0), 1)


def rotary(position, head_size):
    half_size = head_size // 2
    frequency = THETA ** (-(jnp.arange(half_size, dtype=jnp.float32) * 2.0 / head_size))
    angles = position.astype(jnp.float32)[:, None] * frequency[None, :]
    cosines, sines = jnp.cos(angles), jnp.sin(angles)
    return jnp.concatenate([cosines, cosines], 1), jnp.concatenate([-sines, sines], 1)


def ring_order(count):
    return list(range(0, count, 2)) + list(range(count - 1, 0, -2))


class Ring:
    def __init__(self):
        rows = lax.axis_size("row")
        self.count = count = min(8, rows)
        self.half = count // 2
        self.members = members = rows // count
        self.groups = [[g * members + m for m in range(members)] for g in range(count)]
        self.lanes = None if members == 1 else [[g * members + m for g in range(count)] for m in range(members)]
        order = ring_order(count)
        self.onward = self.spell([(order[i], order[(i + 1) % count]) for i in range(count)])
        self.backward = [(b, a) for a, b in self.onward]
        self.partner = self.spell([(g, g ^ 1) for g in range(count)])
        self.pairs = [[(2 * p + side) * members + m for p in range(count // 2)] for side in range(2) for m in range(members)]
        group = lax.axis_index("row") // members
        self.parity = group % 2
        self.place = self.places([[order[(order.index(g) - j) % count] for j in range(count)] for g in range(count)])
        self.behind = jnp.array([[order[(order.index(g) - j) % count] for j in range(count)] for g in range(count)])[group]
        self.plain_place = self.places([list(range(count))] * count)
        self.pair_place = self.places(
            [[j // 2 * 2 + (g % 2 ^ j % 2) for j in range(count)] for g in range(count)]
        )

    def spell(self, pairs):
        return [(a * self.members + m, b * self.members + m) for a, b in pairs for m in range(self.members)]

    def places(self, behind):
        cols = lax.axis_size("col")
        per_col = self.count // cols
        table = [
            [[COL_ORDER.index((b // per_col) ^ c) * per_col + b % per_col for b in row] for c in range(cols)]
            for row in behind
        ]
        return jnp.array(table, jnp.int32)[lax.axis_index("row") // self.members, lax.axis_index("col")]

    def send_on(self, value):
        return lax.ppermute(value, "row", self.onward)

    def send_back(self, value):
        return lax.ppermute(value, "row", self.backward)

    def to_partner(self, value):
        return lax.ppermute(value, "row", self.partner)

    def gather_stack(self, block):
        return lax.all_gather(block, "row", axis=0, axis_index_groups=self.lanes)

    def sum_stack(self, blocks):
        return lax.psum_scatter(blocks, "row", scatter_dimension=0, axis_index_groups=self.lanes)

    def inner_gather(self, block, axis):
        if self.members == 1:
            return block
        return lax.all_gather(block, "row", axis=axis, tiled=True, axis_index_groups=self.groups)

    def inner_sum(self, value, axis):
        if self.members == 1:
            return value
        value = value.astype(jnp.bfloat16)
        return lax.psum_scatter(
            value, "row", scatter_dimension=axis, tiled=True, axis_index_groups=self.groups
        ).astype(jnp.float32)


def side_of(blocks, axis, number):
    halves = [b.shape[axis] // 2 for b in blocks]
    cuts = [lax.dynamic_slice_in_dim(b, number * h, h, axis) for b, h in zip(blocks, halves, strict=True)]
    return jnp.concatenate(cuts, axis)


def pair_gather(ring, unit):
    return lax.all_gather(unit, "row", axis=0, axis_index_groups=ring.pairs)


def pair_sum(ring, units):
    return lax.psum_scatter(units, "row", scatter_dimension=0, axis_index_groups=ring.pairs)


def pair_join(ring, mine, got, axis):
    first = ring.parity == 0
    mine, got = mine.astype(jnp.float32), got.astype(jnp.float32)
    value = jnp.concatenate([jnp.where(first, mine, got), jnp.where(first, got, mine)], axis)
    return ring.inner_sum(value, 1 - axis)


class Chain:
    def __init__(self):
        self.token = lax.create_token()

    def pin(self, *values):
        self.token, *values = lax.optimization_barrier((self.token, *values))
        return values if len(values) > 1 else values[0]

    def run(self, kernel, *operands, beside=()):
        results = kernel(*self.pin(operands))
        results = tuple(results) if isinstance(results, (list, tuple)) else (results,)
        return self.pin(*results, *beside)


COL_ORDER = (0, 2, 1, 3)


def swap(value, axis, bit):
    return lax.ppermute(value, axis, [(i, i ^ bit) for i in range(lax.axis_size(axis))])


def dot_nt(left_side, right_side):
    return lax.dot_general(
        left_side, right_side, (((1,), (1,)), ((), ())), preferred_element_type=jnp.float32
    )


def dot_nn(left_side, right_side):
    return jnp.dot(left_side, right_side, preferred_element_type=jnp.float32)


def dot_tn(left_side, right_side):
    return lax.dot_general(
        left_side, right_side, (((0,), (0,)), ((), ())), preferred_element_type=jnp.float32
    )


def cost(flops):
    return pl.CostEstimate(flops=int(COST_SCALE * flops), bytes_accessed=1 << 16, transcendentals=0)


def kernel_call(body, places, operands, specs, outs, out_specs, grid, scratch, flops, mib):
    return pl.pallas_call(
        body,
        grid_spec=pltpu.PrefetchScalarGridSpec(
            num_scalar_prefetch=1,
            grid=grid,
            in_specs=specs,
            out_specs=out_specs,
            scratch_shapes=scratch,
        ),
        out_shape=outs,
        cost_estimate=cost(flops),
        compiler_params=pltpu.CompilerParams(vmem_limit_bytes=mib << 20),
    )(places, *operands)


def whole_spec(array, buffers=1):
    zeros = (0,) * len(array.shape)
    return pl.BlockSpec(array.shape, lambda *_: zeros, pipeline_mode=pl.Buffered(buffers))


def rows_spec(array, rows):
    return pl.BlockSpec((rows,) + tuple(array.shape[1:]), lambda i, *_: (i,) + (0,) * (len(array.shape) - 1))


def columns_spec(array, columns):
    return pl.BlockSpec((array.shape[0], columns), lambda i, *_: (0, i))


def shape_of(shape, dtype):
    return jax.ShapeDtypeStruct(shape, dtype)


def piece_at(place_ref, j, piece):
    return pl.ds(pl.multiple_of(place_ref[j] * piece, piece), piece)


def norm_rows(place_ref, x_refs, gain_ref, wide_ref, factor_ref, all_ref, piece, eps):
    tokens, full = wide_ref.shape
    width = x_refs[0].shape[1]
    total = jnp.zeros((tokens, 1), jnp.float32)
    for i, x_ref in enumerate(x_refs):
        value = x_ref[...]
        all_ref[:, i * width : (i + 1) * width] = value
        value = value.astype(jnp.float32)
        total = total + jnp.sum(value * value, 1, keepdims=True)
    factor = lax.rsqrt(total / full + eps)
    factor_ref[...] = factor
    for j in range(full // piece):
        at = piece_at(place_ref, j, piece)
        value = all_ref[:, at].astype(jnp.float32) * factor * gain_ref[:, at]
        wide_ref[:, j * piece : (j + 1) * piece] = value.astype(jnp.bfloat16)


def gather_norm_matmul(place, hidden_blocks, gain, weights, eps):
    tokens, width = hidden_blocks[0].shape
    full = width * len(hidden_blocks)
    count = len(weights)
    piece, columns = weights[0].shape
    tile = min(512, columns)
    many = len(hidden_blocks)

    def body(place_ref, *refs):
        x_refs, gain_ref = refs[:many], refs[many]
        w_refs = refs[many + 1 : many + 1 + count]
        wide_ref, factor_ref, out_ref, all_ref = refs[many + 1 + count :]

        @pl.when(pl.program_id(0) == 0)
        def _():
            norm_rows(place_ref, x_refs, gain_ref, wide_ref, factor_ref, all_ref, piece, eps)

        total = dot_nn(wide_ref[:, :piece], w_refs[0][...])
        for j in range(1, count):
            total = total + dot_nn(wide_ref[:, j * piece : (j + 1) * piece], w_refs[j][...])
        out_ref[...] = total

    outs = (
        shape_of((tokens, full), jnp.bfloat16),
        shape_of((tokens, 1), jnp.float32),
        shape_of((tokens, columns), jnp.float32),
    )
    operands = (*hidden_blocks, gain, *weights)
    specs = [whole_spec(b) for b in hidden_blocks] + [whole_spec(gain)] + [columns_spec(w, tile) for w in weights]
    out_specs = (whole_spec(outs[0]), whole_spec(outs[1]), columns_spec(outs[2], tile))
    scratch = [pltpu.VMEM((tokens, full), jnp.bfloat16)]
    return kernel_call(
        body, place, operands, specs, outs, out_specs, (columns // tile,), scratch, 2 * tokens * full * columns, 48
    )


def units_of(refs):
    return [refs[0].at[j] for j in range(refs[0].shape[0])] if len(refs) == 1 else refs


def gather_swish(place, blocks, gain, weights, eps):
    tokens, width = blocks[0].shape
    count, unit, both = weights.shape
    columns = both // 2
    full, many = width * len(blocks), len(blocks)
    piece = full // place.shape[0]
    tile = min(256, columns)

    def body(place_ref, *refs):
        x_refs, gain_ref, g_ref, u_ref = refs[:many], refs[many], refs[many + 1], refs[many + 2]
        wide_ref, factor_ref, gate_ref, up_ref, hidden_ref, all_ref = refs[many + 3 :]

        @pl.when(pl.program_id(0) == 0)
        def _():
            norm_rows(place_ref, x_refs, gain_ref, wide_ref, factor_ref, all_ref, piece, eps)

        def product(w_ref):
            total = dot_nn(wide_ref[:, :unit], w_ref[0])
            for j in range(1, count):
                total = total + dot_nn(wide_ref[:, j * unit : (j + 1) * unit], w_ref[j])
            return total

        gate = product(g_ref)
        gate_ref[...] = gate
        up = product(u_ref)
        up_ref[...] = up
        hidden_ref[...] = (gate / (1.0 + jnp.exp(-gate)) * up).astype(jnp.bfloat16)

    outs = (
        shape_of((tokens, full), jnp.bfloat16),
        shape_of((tokens, 1), jnp.float32),
        shape_of((tokens, columns), jnp.float32),
        shape_of((tokens, columns), jnp.float32),
        shape_of((tokens, columns), jnp.bfloat16),
    )
    operands = (*blocks, gain, weights, weights)
    steps = columns // tile
    specs = [whole_spec(b) for b in (*blocks, gain)] + [
        pl.BlockSpec((count, unit, tile), lambda i, *_: (0, 0, i)),
        pl.BlockSpec((count, unit, tile), lambda i, *_: (0, 0, i + steps)),
    ]
    out_specs = (whole_spec(outs[0]), whole_spec(outs[1])) + tuple(columns_spec(o, tile) for o in outs[2:])
    scratch = [pltpu.VMEM((tokens, full), jnp.bfloat16)]
    return kernel_call(
        body, place, operands, specs, outs, out_specs, (steps,), scratch, 4 * tokens * full * columns, 48
    )


def spread_product(place, left, weights, transposed, normed=None, by_feature=False):
    tokens, inner = left.shape
    many = len(weights)
    count = many if many > 1 else weights[0].shape[0]
    unit = weights[0].shape[-2 if transposed else -1]
    full = unit * count
    piece = full // place.shape[0]
    per_unit = unit // piece
    tile = min(256, tokens)
    dot = dot_nt if transposed else dot_nn
    extras = () if normed is None else (normed,)

    def body(place_ref, *refs):
        y_ref, w_refs = refs[0], units_of(refs[1 : 1 + many])
        rest = refs[1 + many + len(extras) :]
        part_refs, all_ref = rest[:cols], rest[-1]
        rows = jnp.zeros((tile, 1), jnp.float32)
        if by_feature:

            @pl.when(pl.program_id(0) == 0)
            def _():
                rest[cols + 1][...] = jnp.zeros_like(rest[cols + 1])

        for j in range(count):
            total = dot(y_ref[...], w_refs[j][...])
            if extras:
                weighted = total * refs[1 + many][:, j * unit : (j + 1) * unit].astype(jnp.float32)
                rows = rows + jnp.sum(weighted, 1, keepdims=True)
                if by_feature:
                    sums = jnp.broadcast_to(jnp.sum(weighted, 0, keepdims=True), (8, unit))
                    for i in range(per_unit):
                        at = piece_at(place_ref, j * per_unit + i, piece)
                        rest[cols + 1][:, at] += sums[:, i * piece : (i + 1) * piece]
            total = total.astype(jnp.bfloat16)
            for i in range(per_unit):
                at = piece_at(place_ref, j * per_unit + i, piece)
                all_ref[:, at] = total[:, i * piece : (i + 1) * piece]
        for c, ref in enumerate(part_refs):
            ref[...] = all_ref[:, c * (full // cols) : (c + 1) * (full // cols)]
        if extras:
            rest[cols][...] = rows

    cols = len(COL_ORDER)
    outs = (shape_of((tokens, full // cols), jnp.bfloat16),) * cols
    if extras:
        outs += (shape_of((tokens, 1), jnp.float32),)
    operands = (left, *weights, *extras)
    specs = [rows_spec(left, tile)] + [whole_spec(w) for w in weights] + [rows_spec(e, tile) for e in extras]
    out_specs = tuple(rows_spec(o, tile) for o in outs)
    if by_feature:
        outs += (shape_of((8, full), jnp.float32),)
        out_specs += (whole_spec(outs[cols + 1]),)
    scratch = [pltpu.VMEM((tile, full), jnp.bfloat16)]
    return kernel_call(
        body, place, operands, specs, outs, out_specs, (tokens // tile,), scratch, 2 * tokens * full * inner, 48
    )


def assemble(place, blocks):
    tokens, width = blocks[0].shape
    many = len(blocks)
    full = width * many
    piece = full // place.shape[0]
    tile = min(256, tokens)

    def body(place_ref, *refs):
        x_refs, (wide_ref, all_ref) = refs[:many], refs[many:]
        for i in range(many):
            all_ref[:, i * width : (i + 1) * width] = x_refs[i][...]
        for j in range(full // piece):
            wide_ref[:, j * piece : (j + 1) * piece] = all_ref[:, piece_at(place_ref, j, piece)]

    outs = (shape_of((tokens, full), jnp.bfloat16),)
    specs = [rows_spec(b, tile) for b in blocks]
    scratch = [pltpu.VMEM((tile, full), jnp.bfloat16)]
    return kernel_call(
        body, place, blocks, specs, outs, (rows_spec(outs[0], tile),), (tokens // tile,), scratch, 1500 * tokens * 1024, 32
    )[0]


def times_transposed(wide, weights, order):
    return back_product(wide, weights, (), lambda total: (total,), order)[0]


def swish_back(wide, weights, gate, up):
    def gradients(total, gate_value, up_value):
        sigma = 1.0 / (1.0 + jnp.exp(-gate_value))
        grad_gate = total * up_value * sigma * (1.0 + gate_value * (1.0 - sigma))
        grad_up = total * gate_value * sigma
        return grad_gate, grad_up, jnp.sum(grad_gate * gate_value + grad_up * up_value, 1, keepdims=True)

    return back_product(wide, weights, (gate, up), gradients)


def back_product(wide, weights, extras, epilogue, order=None):
    tokens, full = wide.shape
    others, units = len(extras), len(weights)
    count = units if units > 1 else weights[0].shape[0]
    columns, unit = weights[0].shape[-2:]
    tile = min(256, tokens)
    parts = max(1, others)

    stacked = order is not None

    def body(order_ref, *refs):
        wide_ref, extra_refs = refs[0], refs[1 : 1 + others]
        w_refs, out_ref = refs[1 + others : 1 + others + units], refs[1 + others + units]
        if not stacked:
            w_refs = units_of(w_refs)
        else:
            w_refs = [w_refs[0].at[order_ref[j]] for j in range(count)]
        total = dot_nt(wide_ref[:, :unit], w_refs[0][...])
        for j in range(1, count):
            total = total + dot_nt(wide_ref[:, j * unit : (j + 1) * unit], w_refs[j][...])
        results = epilogue(total, *(e[...] for e in extra_refs))
        for i, part in enumerate(results[:parts]):
            out_ref[:, i * columns : (i + 1) * columns] = part.astype(jnp.bfloat16)
        for ref, value in zip(refs[2 + others + units :], results[parts:], strict=True):
            ref[...] = value

    outs = (shape_of((tokens, parts * columns), jnp.bfloat16),)
    if extras:
        outs += (shape_of((tokens, 1), jnp.float32),)
    operands = (wide, *extras, *weights)
    specs = [rows_spec(b, tile) for b in (wide, *extras)] + [whole_spec(w) for w in weights]
    order = order if stacked else jnp.zeros((1,), jnp.int32)
    return kernel_call(
        body, order, operands, specs, outs, tuple(rows_spec(o, tile) for o in outs), (tokens // tile,), [],
        2 * tokens * full * columns, 48,
    )


def weight_grad(lefts, rights, order, by_left):
    tokens, rows = lefts[0].shape
    columns = rights[0].shape[1]
    many = len(lefts)
    units = order.shape[0]
    rows, columns = (rows // units, columns) if by_left else (rows, columns // units)

    def body(_, *refs):
        out_ref = refs[-1]
        total = dot_tn(refs[0][...], refs[many][...])
        for c in range(1, many):
            total = total + dot_tn(refs[c][...], refs[many + c][...])
        out_ref[0] = total.astype(jnp.bfloat16)

    outs = (shape_of((units, rows, columns), jnp.bfloat16),)
    moving = pl.BlockSpec((tokens, rows if by_left else columns), lambda i, *_: (0, i))
    left_specs = [moving if by_left else whole_spec(a) for a in lefts]
    right_specs = [whole_spec(a) if by_left else moving for a in rights]
    out_specs = (pl.BlockSpec((1, rows, columns), lambda i, order_ref: (order_ref[i], 0, 0)),)
    flops = 2 * tokens * many * units * rows * columns
    operands = (*lefts, *rights)
    return kernel_call(
        body, order, operands, left_specs + right_specs, outs, out_specs, (units,), [], flops, 56
    )[0]


def block_grads(lefts, rights, order, count):
    tokens, full = lefts[0].shape
    rows = full // count
    widths = [right.shape[1] for right in rights]
    many, steps = len(lefts), order.shape[0]

    def body(_, *refs):
        start = 0
        for c, width in enumerate(widths):
            refs[-1][0, :, start : start + width] = dot_tn(refs[c][...], refs[many + c][...]).astype(jnp.bfloat16)
            start += width

    outs = (shape_of((steps, rows, sum(widths)), jnp.bfloat16),)
    operands = (*lefts, *rights)
    specs = [pl.BlockSpec((tokens, rows), lambda i, order_ref: (0, order_ref[i]))] * many
    specs += [whole_spec(a) for a in operands[many:]]
    return kernel_call(
        body, order, operands, specs, outs, (pl.BlockSpec((1, rows, sum(widths)), lambda i, *_: (i, 0, 0)),), (steps,), [],
        2 * tokens * steps * rows * sum(widths), 60,
    )[0]


def turn(values, cos_wide, sin_wide):
    return values * cos_wide + pltpu.roll(values, values.shape[1] // 2, 1) * sin_wide


def band(rows, cols, first_row, first_col, position):
    distance = (
        lax.broadcasted_iota(jnp.int32, (rows, cols), 0)
        + (first_row - first_col)
        - lax.broadcasted_iota(jnp.int32, (rows, cols), 1)
    )
    return (distance >= 0) & (distance <= position)


def attention_blocks(tokens, most):
    rows = min(256, tokens)
    reach = -(-(most - 1) // rows)
    return rows, [(i * rows, max(0, i - reach) * rows, (i + 1) * rows) for i in range(tokens // rows)]


def attend(raw, position, cos_wide, sin_wide, query_norm, key_norm, q_width, k_width, most, eps):
    tokens = raw.shape[0]
    size = query_norm.shape[1]
    kv_heads, per_group = k_width // size, q_width // k_width
    factor = 1.0 / math.sqrt(size)
    rows, plan = attention_blocks(tokens, most)

    def body(_, q_ref, k_ref, v_ref, pos_ref, cos_ref, sin_ref, qn_ref, kn_ref, qt_ref, kt_ref, vb_ref, mix_ref):
        def turned(value, gain):
            scale = lax.rsqrt(jnp.mean(value * value, 1, keepdims=True) + eps)
            return turn(value * scale * gain, cos_ref[...], sin_ref[...]).astype(jnp.bfloat16)

        kt_ref[...] = turned(k_ref[...], kn_ref[...])
        vb_ref[...] = v_ref[...].astype(jnp.bfloat16)
        for g in range(per_group):
            at = slice(g * size, (g + 1) * size)
            qt_ref[:, at] = turned(q_ref[:, at], qn_ref[...])
        for first, low, high in plan:
            span = slice(first, first + rows)
            allowed = band(rows, high - low, first, low, pos_ref[span, :])
            for g in range(per_group):
                at = slice(g * size, (g + 1) * size)
                scores = dot_nt(qt_ref[span, at], kt_ref[low:high, :]) * factor
                scores = jnp.where(allowed, scores, NEGATIVE)
                weights = jnp.exp(scores - jnp.max(scores, 1, keepdims=True))
                weights = (weights * (1.0 / jnp.sum(weights, 1, keepdims=True))).astype(jnp.bfloat16)
                mix_ref[span, at] = dot_nn(weights, vb_ref[low:high, :]).astype(jnp.bfloat16)

    group = per_group * size
    outs = tuple(shape_of((tokens, w), jnp.bfloat16) for w in (q_width, k_width, k_width, q_width))
    q_spec = pl.BlockSpec((tokens, group), lambda i, *_: (0, i))
    k_spec = pl.BlockSpec((tokens, size), lambda i, *_: (0, q_width // size + i))
    v_spec = pl.BlockSpec((tokens, size), lambda i, *_: (0, (q_width + k_width) // size + i))
    one = pl.BlockSpec((tokens, size), lambda i, *_: (0, i))
    operands = (raw, raw, raw, position, cos_wide, sin_wide, query_norm, key_norm)
    specs = [q_spec, k_spec, v_spec] + [whole_spec(a) for a in operands[3:]]
    flops = 20 * tokens * (high_sum(plan) * rows // tokens) * q_width
    return kernel_call(
        body, jnp.zeros((1,), jnp.int32), operands, specs, outs, (q_spec, one, one, q_spec), (kv_heads,), [], flops, 48
    )


def high_sum(plan):
    return sum(high - low for _, low, high in plan)


def attend_back(raw, turned_q, turned_k, values, grad_mixed, position, cos_wide, sin_wide, query_norm, key_norm, most, eps):
    tokens, q_width = turned_q.shape
    k_width = turned_k.shape[1]
    size = query_norm.shape[1]
    kv_heads, per_group = k_width // size, q_width // k_width
    factor = 1.0 / math.sqrt(size)
    rows, plan = attention_blocks(tokens, most)

    def body(_, q_ref, k_ref, qt_ref, kt_ref, v_ref, dm_ref, pos_ref, cos_ref, sin_ref, qn_ref, kn_ref,
             dq_ref, dk_ref, dv_ref, gain_ref, key_sum, value_sum):
        key_sum[...] = jnp.zeros_like(key_sum)
        value_sum[...] = jnp.zeros_like(value_sum)

        def back(raw_rows, gain, upstream, span):
            scale = lax.rsqrt(jnp.mean(raw_rows * raw_rows, 1, keepdims=True) + eps)
            turned_back = turn(upstream, cos_ref[span, :], -sin_ref[span, :])
            inner = jnp.mean(turned_back * gain * raw_rows, 1, keepdims=True)
            grad = scale * gain * turned_back - raw_rows * (scale * scale * scale * inner)
            return grad.astype(jnp.bfloat16), jnp.sum(turned_back * raw_rows * scale, 0, keepdims=True)

        query_gain = jnp.zeros((1, size), jnp.float32)
        for first, low, high in plan:
            span = slice(first, first + rows)
            allowed = band(rows, high - low, first, low, pos_ref[span, :])
            for g in range(per_group):
                at = slice(g * size, (g + 1) * size)
                queries, upstream = qt_ref[span, at], dm_ref[span, at]
                scores = dot_nt(queries, kt_ref[low:high, :]) * factor
                scores = jnp.where(allowed, scores, NEGATIVE)
                probs = jnp.exp(scores - jnp.max(scores, 1, keepdims=True))
                probs = probs * (1.0 / jnp.sum(probs, 1, keepdims=True))
                grads = dot_nt(upstream, v_ref[low:high, :])
                weighted = probs * grads
                total = jnp.sum(weighted, 1, keepdims=True)
                grads = (weighted - probs * total).astype(jnp.bfloat16)
                value_sum[low:high, :] += dot_tn(probs.astype(jnp.bfloat16), upstream)
                key_sum[low:high, :] += dot_tn(grads, queries)
                grad_turned = dot_nn(grads, kt_ref[low:high, :]) * factor
                grad, gain = back(q_ref[span, at], qn_ref[...], grad_turned, span)
                dq_ref[span, at] = grad
                query_gain = query_gain + gain
        grad, key_gain = back(k_ref[...], kn_ref[...], key_sum[...] * factor, slice(0, tokens))
        dk_ref[...] = grad
        dv_ref[...] = value_sum[...].astype(jnp.bfloat16)
        gain_ref[...] = jnp.concatenate([query_gain, key_gain, jnp.zeros((6, size), jnp.float32)], 0)

    group = per_group * size
    outs = (
        shape_of((tokens, q_width), jnp.bfloat16),
        shape_of((tokens, k_width), jnp.bfloat16),
        shape_of((tokens, k_width), jnp.bfloat16),
        shape_of((8 * kv_heads, size), jnp.float32),
    )
    q_spec = pl.BlockSpec((tokens, group), lambda i, *_: (0, i))
    k_spec = pl.BlockSpec((tokens, size), lambda i, *_: (0, q_width // size + i))
    one = pl.BlockSpec((tokens, size), lambda i, *_: (0, i))
    operands = (raw, raw, turned_q, turned_k, values, grad_mixed, position, cos_wide, sin_wide, query_norm, key_norm)
    specs = [q_spec, k_spec, q_spec, one, one, q_spec] + [whole_spec(a) for a in operands[6:]]
    out_specs = (q_spec, one, one, pl.BlockSpec((8, size), lambda i, *_: (i, 0)))
    scratch = [pltpu.VMEM((tokens, size), jnp.float32)] * 2
    flops = 28 * tokens * (high_sum(plan) * rows // tokens) * q_width
    return kernel_call(
        body, jnp.zeros((1,), jnp.int32), operands, specs, outs, out_specs, (kv_heads,), scratch, flops, 48
    )


def local(
    hidden_in,
    seq_lengths,
    attn_norm,
    w_query,
    key_weight,
    value_weight,
    query_norm,
    key_norm,
    w_output,
    ffwd_norm,
    w_gate,
    w_up,
    w_down,
    cotangent,
):
    low, f32 = jnp.bfloat16, jnp.float32
    tokens, part_width = hidden_in.shape
    full_width = part_width * lax.axis_size("col")
    head_size = query_norm.shape[0]
    q_width, k_width = w_query.shape[1], key_weight.shape[1]
    ring = Ring()
    place, plain_place, pair_place = ring.place, ring.plain_place, ring.pair_place
    steps, pairs, half = ring.half, ring.half, tokens // 2
    pair_order = jnp.arange(pairs, dtype=jnp.int32)
    chain = Chain()
    pin, run = chain.pin, chain.run

    def near(value):
        return swap(value, "col", 1)

    def far(value):
        return swap(value, "col", 2)

    qkv, hidden_in = pin(jnp.concatenate([w_query, key_weight, value_weight], 1), hidden_in)
    qkv = ring.inner_gather(qkv, 0)
    on, back = ring.send_on(qkv), ring.send_back(qkv)
    output_all = ring.gather_stack(ring.inner_gather(w_output, 1))
    hidden_far = far(hidden_in)
    gains = jnp.stack([attn_norm, ffwd_norm])
    gains_far = far(gains)
    behind, ahead = [], []
    on, back = pin(on, back)
    behind.append(on)
    ahead.append(back)
    on, back = ring.send_on(on), ring.send_back(back)
    hidden_far, gains_far = pin(hidden_far, gains_far)
    hidden_blocks = [hidden_in, hidden_far, near(hidden_in), near(hidden_far)]
    gains_near = near(gains)
    on, back, gains_near, gate, up = pin(on, back, gains_near, w_gate, w_up)
    behind.append(on)
    ahead.append(back)
    on, back = ring.send_on(on), ring.send_back(back)
    gate_up = [ring.inner_gather(w, 0) for w in (gate, up)]
    gate_up_mine = side_of(gate_up, 1, ring.parity)
    gate_up_got = ring.to_partner(side_of(gate_up, 1, 1 - ring.parity))
    gains_diagonal, gate_up_mine, *hidden_blocks = pin(near(gains_far), gate_up_mine, *hidden_blocks)
    position = tables(seq_lengths[0], tokens)[:, None]
    position, cos_wide, sin_wide, behind_order = pin(position, *rotary(position[:, 0], head_size), ring.behind)
    on, back = pin(on, back)
    behind.append(on)
    ahead.append(back)
    cut = on.shape[0] // 2
    on, back = ring.send_on(on[:cut]), ring.send_back(back[cut:])
    on, back, gate_up_got = pin(on, back, gate_up_got)
    qkv_all = [qkv, *behind, jnp.concatenate([on, back], 0), *ahead[::-1]]
    gate_up, output_all = pin(jnp.concatenate([gate_up_mine, gate_up_got], 0), output_all)
    gate_up_all = pair_gather(ring, gate_up)
    gains = jnp.stack([gains, gains_far, gains_near, gains_diagonal], 1).reshape(2, 1, full_width)

    down, upstream = pin(w_down, cotangent)
    down = [ring.inner_gather(down, 1)]
    down_mine = side_of(down, 0, ring.parity)
    down_got = ring.to_partner(side_of(down, 0, 1 - ring.parity))
    up_far, up_partner = far(upstream), ring.to_partner(upstream)
    turning = (position, cos_wide, sin_wide, query_norm[None, :], key_norm[None, :])
    residual = hidden_in.astype(f32)
    wide_one, factor_one, qkv_raw = run(
        lambda blocks, gain, weights: gather_norm_matmul(place, blocks, gain, weights, EPS), hidden_blocks, gains[0], qkv_all
    )
    turned_q, turned_k, values, mixed = run(
        lambda raw: attend(raw, *turning, q_width, k_width, MOST, EPS), qkv_raw
    )
    up_far, up_partner, down_got, down_mine = pin(up_far, up_partner, down_got, down_mine)
    own, to_far, to_near, to_diagonal = run(
        lambda left, weights: spread_product(plain_place, left, [weights], False), mixed, output_all
    )
    got_far, got_own = near(to_diagonal), near(to_near)
    up_near, up_diagonal = near(upstream), near(up_far)
    to_far, got_far = pin(to_far, got_far)
    attended = far(pin((to_far.astype(f32) + got_far).astype(low)))
    corner = far(pin(up_partner[:half])), ring.to_partner(up_far[half:])
    up_near, up_diagonal = pin(up_near, up_diagonal)
    upstream_wide = run(lambda *blocks: assemble(pair_place, blocks), upstream, up_far, up_near, up_diagonal)
    attended, own, got_own = pin(attended, own, got_own)

    middle = residual + own + got_own + attended
    middle, middle_low = pin(middle, middle.astype(low))
    mid_far, mid_partner = far(middle_low), ring.to_partner(middle_low)
    mid_near = near(middle_low)
    up_corner = pin(jnp.concatenate(pin(*corner), 0))
    up_partner_near, up_corner_near = near(up_partner), near(up_corner)
    down_unit = pin(jnp.concatenate([down_mine, down_got], 1))
    mid_near, up_partner_near, up_corner_near = pin(mid_near, up_partner_near, up_corner_near)
    upstream_other = run(lambda *blocks: assemble(pair_place, blocks), up_partner, up_corner, up_partner_near, up_corner_near)
    mid_far = pin(mid_far)
    mid_diagonal = near(mid_far)
    mid_partner = pin(mid_partner)
    corner = far(mid_partner[:half]), ring.to_partner(mid_far[half:])
    mid_partner_near = near(mid_partner)
    gate_up_all = pin(gate_up_all)
    down_all = pair_gather(ring, pin(down_unit))
    mid_diagonal = pin(mid_diagonal)

    def swish(blocks, gain, weights):
        return gather_swish(pair_place, blocks, gain, weights, EPS)

    normed, factor_two, gate, up, hidden = run(
        swish, [middle_low, mid_far, mid_near, mid_diagonal], gains[1], gate_up_all
    )
    mid_partner_near, *corner = pin(mid_partner_near, *corner)
    mid_corner = pin(jnp.concatenate(corner, 0))
    mid_corner_near = pin(near(mid_corner))
    normed_other, _, gate_other, up_other, hidden_other = run(
        swish, [mid_partner, mid_corner, mid_partner_near, mid_corner_near], gains[1], gate_up_all
    )
    down_grad = run(
        lambda *ops: weight_grad(ops[:2], ops[2:], pair_order, False), hidden, hidden_other, upstream_wide, upstream_other
    )
    down_grad = pair_sum(ring, down_grad)

    down_all = pin(down_all)

    def back_swish(wide, weights, gate_value, up_value):
        return swish_back(wide, [weights], gate_value, up_value)

    def spread_back(left, weights):
        return spread_product(pair_place, left, [weights], True)

    low_other, inner_other = run(back_swish, upstream_other, down_all, gate_other, up_other)
    own_other, far_other, near_other, diagonal_other = run(spread_back, low_other, gate_up_all)
    diagonal_other, near_other, inner_other = near(diagonal_other), near(near_other), ring.to_partner(pin(inner_other[:, 0]))
    low_mine, inner, diagonal_other, near_other, inner_other = run(
        back_swish, upstream_wide, down_all, gate, up, beside=(diagonal_other, near_other, inner_other)
    )
    corner = pin((pin(far_other).astype(f32) + diagonal_other).astype(low))
    from_far, from_partner = far(corner[:half]), ring.to_partner(corner[half:])
    inner = pin(inner[:, 0] + inner_other)
    inner_near = near(inner)
    own, to_far, to_near, to_diagonal, from_far, from_partner, inner_near = run(
        spread_back, low_mine, gate_up_all, beside=(from_far, from_partner, inner_near)
    )
    got_far, got_own = near(to_diagonal), near(to_near)
    inner = pin(inner + inner_near)
    inner_far = far(inner)
    to_partner = own_other.astype(f32) + near_other
    to_partner = jnp.concatenate([to_partner[:half] + from_far, to_partner[half:]], 0)
    to_far, got_far, to_partner = pin(to_far, got_far, to_partner.astype(low))
    to_partner = ring.to_partner(to_partner)
    to_far = to_far.astype(f32) + got_far
    to_far = jnp.concatenate([to_far[:half], to_far[half:] + from_partner], 0)
    own, got_own, to_far, inner_far = pin(own, got_own, to_far.astype(low), inner_far)
    from_far = far(to_far)
    gate_up_grad = run(
        lambda *ops: weight_grad(ops[:2], ops[2:], pair_order, True), normed, normed_other, low_mine, low_other
    )
    inner = (inner + inner_far)[:, None] / full_width
    own, got_own, from_partner, from_far, inner, down_grad, gate_up_grad = pin(
        own, got_own, to_partner, from_far, inner, down_grad, gate_up_grad
    )
    gate_up_grad = pair_sum(ring, gate_up_grad)

    def spread_down(left, weights):
        return spread_product(pair_place, left, [weights], False)

    grad_normed = own.astype(f32) + got_own + from_partner + from_far
    grad_middle = (
        cotangent.astype(f32)
        + factor_two * ffwd_norm * grad_normed
        - middle * (factor_two * factor_two * inner)
    )
    grad_middle, grad_low = pin(grad_middle, grad_middle.astype(low))
    grad_far, grad_near = far(grad_low), near(grad_low)
    down_got = ring.to_partner(pin(down_grad[:, down_grad.shape[1] // 2 :]))
    own_other, far_other, near_other, diagonal_other = run(spread_down, hidden_other, down_all)
    out_own, out_to_far, out_to_near, out_to_diagonal, grad_near, down_got = run(
        spread_down, hidden, down_all, beside=(grad_near, down_got)
    )
    near_other, diagonal_other = near(near_other), near(diagonal_other)
    grad_far = pin(grad_far)
    grad_diagonal = near(grad_far)
    near_other, diagonal_other, grad_diagonal, own_other, far_other = pin(
        near_other, diagonal_other, grad_diagonal, own_other, far_other
    )
    out_first, out_second = pin(
        (own_other.astype(f32) + near_other).astype(low), (far_other.astype(f32) + diagonal_other).astype(low)
    )
    out_first = ring.to_partner(out_first)
    out_got_own, out_got_far = near(out_to_near), near(out_to_diagonal)
    ffwd_gain = pin(jnp.sum(grad_normed * middle * factor_two, 0))

    middle_wide = run(lambda *blocks: assemble(place, blocks), grad_low, grad_far, grad_near, grad_diagonal)
    grad_mixed = run(lambda wide, weights: times_transposed(wide, [weights], behind_order), middle_wide, output_all)
    query_low, key_low, value_low, head_gains, out_first, out_got_own, out_got_far = run(
        lambda *ops: attend_back(*ops, *turning, MOST, EPS),
        qkv_raw,
        turned_q,
        turned_k,
        values,
        grad_mixed,
        beside=(out_first, out_got_own, out_got_far),
    )
    out_second = ring.to_partner(out_second)
    qkv_low = pin(jnp.concatenate([query_low, key_low, value_low], 1))

    def parts(*numbers, beside=()):
        order = jnp.array(numbers, jnp.int32)
        return run(
            lambda *ops: block_grads(ops[:2], ops[2:], order, ring.count), wide_one, middle_wide, qkv_low, mixed, beside=beside
        )

    def go(on, back, *beside):
        on, back, *beside = pin(on.astype(low), back.astype(low), *beside)
        return ring.send_on(on), ring.send_back(back), *beside

    first = parts(steps)
    cut = first.shape[1] // 2
    on, back = go(first[0, :cut], first[0, cut:])
    own_first, to_far, to_near, to_diagonal, inner, attn_gain = run(
        lambda left, weights, wide: spread_product(place, left, weights, True, wide, True), qkv_low, qkv_all, wide_one
    )
    got_far, got_own = near(to_diagonal), near(to_near)
    second = parts(steps + 1, steps - 1)
    own, on, back, out_second, gate_up_grad = parts(
        *(n for s in range(2, steps) for n in (steps + s, steps - s)), 0, beside=(on, back, out_second, gate_up_grad)
    )
    on = jnp.concatenate([second[0, :cut] + on.astype(f32), second[0, cut:].astype(f32)], 0)
    back = jnp.concatenate([second[1, :cut].astype(f32), second[1, cut:] + back.astype(f32)], 0)
    on, back, got_far, got_own, to_far = go(on, back, got_far, got_own, to_far)
    to_far = pin((to_far.astype(f32) + got_far).astype(low))
    gain_keep, gain_send = attn_gain[:1, : full_width // 2], attn_gain[:1, full_width // 2 :]
    head_gains = jnp.sum(head_gains.reshape(-1, 8, head_size), 0)[:2].reshape(-1)
    sums = pin(jnp.concatenate([gain_send[0], head_gains, inner[:, 0]]))
    sums_got = pin(near(sums))
    both_gain = gain_keep[0] + sums_got[: full_width // 2]
    sums = pin(jnp.concatenate([both_gain[part_width:], (sums + sums_got)[full_width // 2 :]]))
    sums_got = far(sums)
    grad_far = far(to_far)
    sums_got, out_to_far = pin(sums_got, out_to_far)
    attn_gain = (both_gain[:part_width] + sums_got[:part_width]) / attn_norm
    rest = (sums + sums_got)[part_width:]
    inner = rest[2 * head_size :][:, None] / full_width
    sums = jnp.concatenate([attn_gain, ffwd_gain, rest[: 2 * head_size]])
    sums, inner = pin(sums, inner)
    bits = [1 << n for n in range(lax.axis_size("row").bit_length() - 1)]
    sums_got = swap(sums, "row", bits[0])
    on, back, sums_got = pin(on, back, sums_got)
    on, back = go(own[0] + on.astype(f32), own[1] + back.astype(f32))
    sums = pin(sums + sums_got)
    sums_got = swap(sums, "row", bits[1])
    columns_here = gate_up_grad.shape[0] // 2
    gate_up_got = ring.to_partner(pin(gate_up_grad[columns_here:]))
    grad_far = pin(grad_far)
    to_far = (out_to_far.astype(f32) + out_got_far + out_second).astype(low)
    hidden_grad = (
        grad_middle
        + factor_one * attn_norm * (own_first.astype(f32) + got_own + grad_far)
        - residual * (factor_one * factor_one * inner)
    )
    hidden_grad, to_far = pin(hidden_grad, to_far)
    out_far = far(to_far)
    on, back, sums_got = pin(on, back, sums_got)
    on, back = go(own[2] + on.astype(f32), own[3] + back.astype(f32))
    sums = pin(sums + sums_got)
    for bit in bits[2:-1]:
        sums = pin(sums + pin(swap(sums, "row", bit)))
    sums_got = swap(sums, "row", bits[-1])
    out_far = pin(out_far)
    hidden_out = pin((middle + out_own + out_got_own + out_first + out_far).astype(low))
    gate_up_grad, gate_up_got, down_got = pin(gate_up_grad, gate_up_got, down_got)
    gate_grad, up_grad = (
        pair_join(ring, gate_up_grad[:columns_here, at], gate_up_got[:, at], 1)
        for at in (slice(0, gate_up_grad.shape[1] // 2), slice(gate_up_grad.shape[1] // 2, None))
    )
    down_out = pair_join(ring, down_grad[:, : down_grad.shape[1] // 2], down_got, 0)
    gate_grad, up_grad, down_out = pin(gate_grad, up_grad, down_out)
    on, back, sums_got = pin(on, back, sums_got)
    sums = sums + sums_got
    total = ring.inner_sum(own[4].astype(f32) + on + back, 0)
    attn_gain, ffwd_gain, query_gain, key_gain = jnp.split(
        sums, [part_width, 2 * part_width, 2 * part_width + head_size]
    )
    return (
        hidden_out,
        hidden_grad,
        attn_gain,
        total[:, :q_width],
        total[:, q_width : q_width + k_width],
        total[:, q_width + k_width : q_width + 2 * k_width],
        query_gain,
        key_gain,
        total[:, q_width + 2 * k_width :].T,
        ffwd_gain,
        gate_grad,
        up_grad,
        down_out,
    )


def solution(mesh):
    in_specs = (
        P("row", "col"),
        P("row", None),
        P("col"),
        P("row", "col"),
        P("row", "col"),
        P("row", "col"),
        P(),
        P(),
        P("col", "row"),
        P("col"),
        P("row", "col"),
        P("row", "col"),
        P("col", "row"),
        P("row", "col"),
    )
    out_specs = (
        P("row", "col"),
        P("row", "col"),
        P("col"),
        P("row", "col"),
        P("row", "col"),
        P("row", "col"),
        P(),
        P(),
        P("col", "row"),
        P("col"),
        P("row", "col"),
        P("row", "col"),
        P("col", "row"),
    )
    return jax.shard_map(local, mesh=mesh, in_specs=in_specs, out_specs=out_specs, check_vma=False)
```

```python
import math

import jax
import jax.numpy as jnp
from jax import lax
from jax.experimental import pallas as pl
from jax.experimental.pallas import tpu as pltpu
from jax.sharding import PartitionSpec as P

EPS = 1e-06
THETA = 1000000.0
NEGATIVE = -1e30
MOST = 512
COST_SCALE = 0.02


def tables(lengths_row, row_number_total):
    steps_idx = jnp.arange(row_number_total, dtype=jnp.int32)
    seq_ends = jnp.cumsum(lengths_row)
    seq_starts = seq_ends - lengths_row
    segment = jnp.sum((steps_idx[:, None] >= seq_ends[None, :]).astype(jnp.int32), 1)
    member = segment[:, None] == jnp.arange(lengths_row.shape[0], dtype=jnp.int32)[None, :]
    return steps_idx - jnp.sum(jnp.where(member, seq_starts[None, :], 0), 1)


def rotary(position, head_size):
    half_size = head_size // 2
    frequency = THETA ** (-(jnp.arange(half_size, dtype=jnp.float32) * 2.0 / head_size))
    angles = position.astype(jnp.float32)[:, None] * frequency[None, :]
    cosines, sines = jnp.cos(angles), jnp.sin(angles)
    return jnp.concatenate([cosines, cosines], 1), jnp.concatenate([-sines, sines], 1)


def ring_order(count):
    return list(range(0, count, 2)) + list(range(count - 1, 0, -2))


class Ring:
    def __init__(self):
        rows = lax.axis_size("row")
        self.count = count = min(8, rows)
        self.half = count // 2
        self.members = members = rows // count
        self.groups = [[g * members + m for m in range(members)] for g in range(count)]
        self.lanes = None if members == 1 else [[g * members + m for g in range(count)] for m in range(members)]
        order = ring_order(count)
        self.onward = self.spell([(order[i], order[(i + 1) % count]) for i in range(count)])
        self.backward = [(b, a) for a, b in self.onward]
        self.partner = self.spell([(g, g ^ 1) for g in range(count)])
        self.pairs = [[(2 * p + side) * members + m for p in range(count // 2)] for side in range(2) for m in range(members)]
        group = lax.axis_index("row") // members
        self.parity = group % 2
        self.place = self.places([[order[(order.index(g) - j) % count] for j in range(count)] for g in range(count)])
        self.behind = jnp.array([[order[(order.index(g) - j) % count] for j in range(count)] for g in range(count)])[group]
        self.plain_place = self.places([list(range(count))] * count)
        self.pair_place = self.places(
            [[j // 2 * 2 + (g % 2 ^ j % 2) for j in range(count)] for g in range(count)]
        )

    def spell(self, pairs):
        return [(a * self.members + m, b * self.members + m) for a, b in pairs for m in range(self.members)]

    def places(self, behind):
        cols = lax.axis_size("col")
        per_col = self.count // cols
        table = [
            [[COL_ORDER.index((b // per_col) ^ c) * per_col + b % per_col for b in row] for c in range(cols)]
            for row in behind
        ]
        return jnp.array(table, jnp.int32)[lax.axis_index("row") // self.members, lax.axis_index("col")]

    def send_on(self, value):
        return lax.ppermute(value, "row", self.onward)

    def send_back(self, value):
        return lax.ppermute(value, "row", self.backward)

    def to_partner(self, value):
        return lax.ppermute(value, "row", self.partner)

    def gather_stack(self, block):
        return lax.all_gather(block, "row", axis=0, axis_index_groups=self.lanes)

    def sum_stack(self, blocks):
        return lax.psum_scatter(blocks, "row", scatter_dimension=0, axis_index_groups=self.lanes)

    def inner_gather(self, block, axis):
        if self.members == 1:
            return block
        return lax.all_gather(block, "row", axis=axis, tiled=True, axis_index_groups=self.groups)

    def inner_sum(self, value, axis):
        if self.members == 1:
            return value
        value = value.astype(jnp.bfloat16)
        return lax.psum_scatter(
            value, "row", scatter_dimension=axis, tiled=True, axis_index_groups=self.groups
        ).astype(jnp.float32)


def side_of(blocks, axis, number):
    halves = [b.shape[axis] // 2 for b in blocks]
    cuts = [lax.dynamic_slice_in_dim(b, number * h, h, axis) for b, h in zip(blocks, halves, strict=True)]
    return jnp.concatenate(cuts, axis)


def pair_gather(ring, unit):
    return lax.all_gather(unit, "row", axis=0, axis_index_groups=ring.pairs)


def pair_sum(ring, units):
    return lax.psum_scatter(units, "row", scatter_dimension=0, axis_index_groups=ring.pairs)


def pair_join(ring, mine, got, axis):
    first = ring.parity == 0
    mine, got = mine.astype(jnp.float32), got.astype(jnp.float32)
    value = jnp.concatenate([jnp.where(first, mine, got), jnp.where(first, got, mine)], axis)
    return ring.inner_sum(value, 1 - axis)


class Chain:
    def __init__(self):
        self.token = lax.create_token()

    def pin(self, *values):
        self.token, *values = lax.optimization_barrier((self.token, *values))
        return values if len(values) > 1 else values[0]

    def run(self, kernel, *operands, beside=()):
        results = kernel(*self.pin(operands))
        results = tuple(results) if isinstance(results, (list, tuple)) else (results,)
        return self.pin(*results, *beside)


COL_ORDER = (0, 2, 1, 3)


def swap(value, axis, bit):
    return lax.ppermute(value, axis, [(i, i ^ bit) for i in range(lax.axis_size(axis))])


def dot_nt(left_side, right_side):
    return lax.dot_general(
        left_side, right_side, (((1,), (1,)), ((), ())), preferred_element_type=jnp.float32
    )


def dot_nn(left_side, right_side):
    return jnp.dot(left_side, right_side, preferred_element_type=jnp.float32)


def dot_tn(left_side, right_side):
    return lax.dot_general(
        left_side, right_side, (((0,), (0,)), ((), ())), preferred_element_type=jnp.float32
    )


def cost(flops):
    return pl.CostEstimate(flops=int(COST_SCALE * flops), bytes_accessed=1 << 16, transcendentals=0)


def kernel_call(body, places, operands, specs, outs, out_specs, grid, scratch, flops, mib):
    return pl.pallas_call(
        body,
        grid_spec=pltpu.PrefetchScalarGridSpec(
            num_scalar_prefetch=1,
            grid=grid,
            in_specs=specs,
            out_specs=out_specs,
            scratch_shapes=scratch,
        ),
        out_shape=outs,
        cost_estimate=cost(flops),
        compiler_params=pltpu.CompilerParams(vmem_limit_bytes=mib << 20),
    )(places, *operands)


def whole_spec(array, buffers=1):
    zeros = (0,) * len(array.shape)
    return pl.BlockSpec(array.shape, lambda *_: zeros, pipeline_mode=pl.Buffered(buffers))


def rows_spec(array, rows):
    return pl.BlockSpec((rows,) + tuple(array.shape[1:]), lambda i, *_: (i,) + (0,) * (len(array.shape) - 1))


def columns_spec(array, columns):
    return pl.BlockSpec((array.shape[0], columns), lambda i, *_: (0, i))


def shape_of(shape, dtype):
    return jax.ShapeDtypeStruct(shape, dtype)


def piece_at(place_ref, j, piece):
    return pl.ds(pl.multiple_of(place_ref[j] * piece, piece), piece)


def norm_rows(place_ref, x_refs, gain_ref, wide_ref, factor_ref, all_ref, piece, eps):
    tokens, full = wide_ref.shape
    width = x_refs[0].shape[1]
    total = jnp.zeros((tokens, 1), jnp.float32)
    for i, x_ref in enumerate(x_refs):
        value = x_ref[...]
        all_ref[:, i * width : (i + 1) * width] = value
        value = value.astype(jnp.float32)
        total = total + jnp.sum(value * value, 1, keepdims=True)
    factor = lax.rsqrt(total / full + eps)
    factor_ref[...] = factor
    for j in range(full // piece):
        at = piece_at(place_ref, j, piece)
        value = all_ref[:, at].astype(jnp.float32) * factor * gain_ref[:, at]
        wide_ref[:, j * piece : (j + 1) * piece] = value.astype(jnp.bfloat16)


def gather_norm_matmul(place, hidden_blocks, gain, weights, eps):
    tokens, width = hidden_blocks[0].shape
    full = width * len(hidden_blocks)
    count = len(weights)
    piece, columns = weights[0].shape
    tile = min(512, columns)
    many = len(hidden_blocks)

    def body(place_ref, *refs):
        x_refs, gain_ref = refs[:many], refs[many]
        w_refs = refs[many + 1 : many + 1 + count]
        wide_ref, factor_ref, out_ref, all_ref = refs[many + 1 + count :]

        @pl.when(pl.program_id(0) == 0)
        def _():
            norm_rows(place_ref, x_refs, gain_ref, wide_ref, factor_ref, all_ref, piece, eps)

        total = dot_nn(wide_ref[:, :piece], w_refs[0][...])
        for j in range(1, count):
            total = total + dot_nn(wide_ref[:, j * piece : (j + 1) * piece], w_refs[j][...])
        out_ref[...] = total

    outs = (
        shape_of((tokens, full), jnp.bfloat16),
        shape_of((tokens, 1), jnp.float32),
        shape_of((tokens, columns), jnp.float32),
    )
    operands = (*hidden_blocks, gain, *weights)
    specs = [whole_spec(b) for b in hidden_blocks] + [whole_spec(gain)] + [columns_spec(w, tile) for w in weights]
    out_specs = (whole_spec(outs[0]), whole_spec(outs[1]), columns_spec(outs[2], tile))
    scratch = [pltpu.VMEM((tokens, full), jnp.bfloat16)]
    return kernel_call(
        body, place, operands, specs, outs, out_specs, (columns // tile,), scratch, 2 * tokens * full * columns, 48
    )


def above(first, second):
    def body(_, first_ref, second_ref, out_ref):
        @pl.when(pl.program_id(0) == 0)
        def _():
            out_ref[...] = first_ref[...]

        @pl.when(pl.program_id(0) == 1)
        def _():
            out_ref[...] = second_ref[...]

    rows, columns = first.shape
    out = shape_of((2 * rows, columns), first.dtype)
    return kernel_call(
        body, jnp.zeros((1,), jnp.int32), (first, second), [whole_spec(first), whole_spec(second)], (out,),
        (rows_spec(out, rows),), (2,), [], 0, 32,
    )[0]


def units_of(refs):
    return [refs[0].at[j] for j in range(refs[0].shape[0])] if len(refs) == 1 else refs


def gather_swish(place, blocks, gain, weights, eps):
    tokens, width = blocks[0].shape
    count, unit, both = weights.shape
    columns = both // 2
    full, many = width * len(blocks), len(blocks)
    piece = full // place.shape[0]
    tile = min(256, columns)

    def body(place_ref, *refs):
        x_refs, gain_ref, g_ref, u_ref = refs[:many], refs[many], refs[many + 1], refs[many + 2]
        wide_ref, factor_ref, gate_ref, up_ref, hidden_ref, all_ref = refs[many + 3 :]

        @pl.when(pl.program_id(0) == 0)
        def _():
            norm_rows(place_ref, x_refs, gain_ref, wide_ref, factor_ref, all_ref, piece, eps)

        def product(w_ref):
            total = dot_nn(wide_ref[:, :unit], w_ref[0])
            for j in range(1, count):
                total = total + dot_nn(wide_ref[:, j * unit : (j + 1) * unit], w_ref[j])
            return total

        gate = product(g_ref)
        gate_ref[...] = gate
        up = product(u_ref)
        up_ref[...] = up
        hidden_ref[...] = (gate / (1.0 + jnp.exp(-gate)) * up).astype(jnp.bfloat16)

    outs = (
        shape_of((tokens, full), jnp.bfloat16),
        shape_of((tokens, 1), jnp.float32),
        shape_of((tokens, columns), jnp.float32),
        shape_of((tokens, columns), jnp.float32),
        shape_of((tokens, columns), jnp.bfloat16),
    )
    operands = (*blocks, gain, weights, weights)
    steps = columns // tile
    specs = [whole_spec(b) for b in (*blocks, gain)] + [
        pl.BlockSpec((count, unit, tile), lambda i, *_: (0, 0, i)),
        pl.BlockSpec((count, unit, tile), lambda i, *_: (0, 0, i + steps)),
    ]
    out_specs = (whole_spec(outs[0]), whole_spec(outs[1])) + tuple(columns_spec(o, tile) for o in outs[2:])
    scratch = [pltpu.VMEM((tokens, full), jnp.bfloat16)]
    return kernel_call(
        body, place, operands, specs, outs, out_specs, (steps,), scratch, 4 * tokens * full * columns, 48
    )


def spread_product(place, left, weights, transposed, normed=None, by_feature=False):
    tokens, inner = left.shape
    many = len(weights)
    count = many if many > 1 else weights[0].shape[0]
    unit = weights[0].shape[-2 if transposed else -1]
    full = unit * count
    piece = full // place.shape[0]
    per_unit = unit // piece
    tile = min(256, tokens)
    dot = dot_nt if transposed else dot_nn
    extras = () if normed is None else (normed,)

    def body(place_ref, *refs):
        y_ref, w_refs = refs[0], units_of(refs[1 : 1 + many])
        rest = refs[1 + many + len(extras) :]
        part_refs, all_ref = rest[:cols], rest[-1]
        rows = jnp.zeros((tile, 1), jnp.float32)
        if by_feature:

            @pl.when(pl.program_id(0) == 0)
            def _():
                rest[cols + 1][...] = jnp.zeros_like(rest[cols + 1])

        for j in range(count):
            total = dot(y_ref[...], w_refs[j][...])
            if extras:
                weighted = total * refs[1 + many][:, j * unit : (j + 1) * unit].astype(jnp.float32)
                rows = rows + jnp.sum(weighted, 1, keepdims=True)
                if by_feature:
                    sums = jnp.broadcast_to(jnp.sum(weighted, 0, keepdims=True), (8, unit))
                    for i in range(per_unit):
                        at = piece_at(place_ref, j * per_unit + i, piece)
                        rest[cols + 1][:, at] += sums[:, i * piece : (i + 1) * piece]
            total = total.astype(jnp.bfloat16)
            for i in range(per_unit):
                at = piece_at(place_ref, j * per_unit + i, piece)
                all_ref[:, at] = total[:, i * piece : (i + 1) * piece]
        for c, ref in enumerate(part_refs):
            ref[...] = all_ref[:, c * (full // cols) : (c + 1) * (full // cols)]
        if extras:
            rest[cols][...] = rows

    cols = len(COL_ORDER)
    outs = (shape_of((tokens, full // cols), jnp.bfloat16),) * cols
    if extras:
        outs += (shape_of((tokens, 1), jnp.float32),)
    operands = (left, *weights, *extras)
    specs = [rows_spec(left, tile)] + [whole_spec(w) for w in weights] + [rows_spec(e, tile) for e in extras]
    out_specs = tuple(rows_spec(o, tile) for o in outs)
    if by_feature:
        outs += (shape_of((8, full), jnp.float32),)
        out_specs += (whole_spec(outs[cols + 1]),)
    scratch = [pltpu.VMEM((tile, full), jnp.bfloat16)]
    return kernel_call(
        body, place, operands, specs, outs, out_specs, (tokens // tile,), scratch, 2 * tokens * full * inner, 48
    )


def assemble(place, blocks):
    tokens, width = blocks[0].shape
    many = len(blocks)
    full = width * many
    piece = full // place.shape[0]
    tile = min(256, tokens)

    def body(place_ref, *refs):
        x_refs, (wide_ref, all_ref) = refs[:many], refs[many:]
        for i in range(many):
            all_ref[:, i * width : (i + 1) * width] = x_refs[i][...]
        for j in range(full // piece):
            wide_ref[:, j * piece : (j + 1) * piece] = all_ref[:, piece_at(place_ref, j, piece)]

    outs = (shape_of((tokens, full), jnp.bfloat16),)
    specs = [rows_spec(b, tile) for b in blocks]
    scratch = [pltpu.VMEM((tile, full), jnp.bfloat16)]
    return kernel_call(
        body, place, blocks, specs, outs, (rows_spec(outs[0], tile),), (tokens // tile,), scratch, 1500 * tokens * 1024, 32
    )[0]


def times_transposed(wide, weights, order):
    return back_product(wide, weights, (), lambda total: (total,), order)[0]


def swish_back(wide, weights, gate, up):
    def gradients(total, gate_value, up_value):
        sigma = 1.0 / (1.0 + jnp.exp(-gate_value))
        grad_gate = total * up_value * sigma * (1.0 + gate_value * (1.0 - sigma))
        grad_up = total * gate_value * sigma
        return grad_gate, grad_up, jnp.sum(grad_gate * gate_value + grad_up * up_value, 1, keepdims=True)

    return back_product(wide, weights, (gate, up), gradients)


def back_product(wide, weights, extras, epilogue, order=None):
    tokens, full = wide.shape
    others, units = len(extras), len(weights)
    count = units if units > 1 else weights[0].shape[0]
    columns, unit = weights[0].shape[-2:]
    tile = min(256, tokens)
    parts = max(1, others)

    stacked = order is not None

    def body(order_ref, *refs):
        wide_ref, extra_refs = refs[0], refs[1 : 1 + others]
        w_refs, out_ref = refs[1 + others : 1 + others + units], refs[1 + others + units]
        if not stacked:
            w_refs = units_of(w_refs)
        else:
            w_refs = [w_refs[0].at[order_ref[j]] for j in range(count)]
        total = dot_nt(wide_ref[:, :unit], w_refs[0][...])
        for j in range(1, count):
            total = total + dot_nt(wide_ref[:, j * unit : (j + 1) * unit], w_refs[j][...])
        results = epilogue(total, *(e[...] for e in extra_refs))
        for i, part in enumerate(results[:parts]):
            out_ref[:, i * columns : (i + 1) * columns] = part.astype(jnp.bfloat16)
        for ref, value in zip(refs[2 + others + units :], results[parts:], strict=True):
            ref[...] = value

    outs = (shape_of((tokens, parts * columns), jnp.bfloat16),)
    if extras:
        outs += (shape_of((tokens, 1), jnp.float32),)
    operands = (wide, *extras, *weights)
    specs = [rows_spec(b, tile) for b in (wide, *extras)] + [whole_spec(w) for w in weights]
    order = order if stacked else jnp.zeros((1,), jnp.int32)
    return kernel_call(
        body, order, operands, specs, outs, tuple(rows_spec(o, tile) for o in outs), (tokens // tile,), [],
        2 * tokens * full * columns, 48,
    )


def weight_grad(lefts, rights, order, by_left):
    tokens, rows = lefts[0].shape
    columns = rights[0].shape[1]
    many = len(lefts)
    units = order.shape[0]
    rows, columns = (rows // units, columns) if by_left else (rows, columns // units)

    def body(_, *refs):
        out_ref = refs[-1]
        total = dot_tn(refs[0][...], refs[many][...])
        for c in range(1, many):
            total = total + dot_tn(refs[c][...], refs[many + c][...])
        out_ref[0] = total.astype(jnp.bfloat16)

    outs = (shape_of((units, rows, columns), jnp.bfloat16),)
    moving = pl.BlockSpec((tokens, rows if by_left else columns), lambda i, *_: (0, i))
    left_specs = [moving if by_left else whole_spec(a) for a in lefts]
    right_specs = [whole_spec(a) if by_left else moving for a in rights]
    out_specs = (pl.BlockSpec((1, rows, columns), lambda i, order_ref: (order_ref[i], 0, 0)),)
    flops = 2 * tokens * many * units * rows * columns
    operands = (*lefts, *rights)
    return kernel_call(
        body, order, operands, left_specs + right_specs, outs, out_specs, (units,), [], flops, 56
    )[0]


def block_grads(lefts, rights, order, count):
    tokens, full = lefts[0].shape
    rows = full // count
    widths = [right.shape[1] for right in rights]
    many, steps = len(lefts), order.shape[0]

    def body(_, *refs):
        start = 0
        for c, width in enumerate(widths):
            refs[-1][0, :, start : start + width] = dot_tn(refs[c][...], refs[many + c][...]).astype(jnp.bfloat16)
            start += width

    outs = (shape_of((steps, rows, sum(widths)), jnp.bfloat16),)
    operands = (*lefts, *rights)
    specs = [pl.BlockSpec((tokens, rows), lambda i, order_ref: (0, order_ref[i]))] * many
    specs += [whole_spec(a) for a in operands[many:]]
    return kernel_call(
        body, order, operands, specs, outs, (pl.BlockSpec((1, rows, sum(widths)), lambda i, *_: (i, 0, 0)),), (steps,), [],
        2 * tokens * steps * rows * sum(widths), 60,
    )[0]


def turn(values, cos_wide, sin_wide):
    return values * cos_wide + pltpu.roll(values, values.shape[1] // 2, 1) * sin_wide


def band(rows, cols, first_row, first_col, position):
    distance = (
        lax.broadcasted_iota(jnp.int32, (rows, cols), 0)
        + (first_row - first_col)
        - lax.broadcasted_iota(jnp.int32, (rows, cols), 1)
    )
    return (distance >= 0) & (distance <= position)


def attention_blocks(tokens, most):
    rows = min(256, tokens)
    reach = -(-(most - 1) // rows)
    return rows, [(i * rows, max(0, i - reach) * rows, (i + 1) * rows) for i in range(tokens // rows)]


def attend(raw, position, cos_wide, sin_wide, query_norm, key_norm, q_width, k_width, most, eps):
    tokens = raw.shape[0]
    size = query_norm.shape[1]
    kv_heads, per_group = k_width // size, q_width // k_width
    factor = 1.0 / math.sqrt(size)
    rows, plan = attention_blocks(tokens, most)

    def body(_, q_ref, k_ref, v_ref, pos_ref, cos_ref, sin_ref, qn_ref, kn_ref, qt_ref, kt_ref, vb_ref, mix_ref):
        def turned(value, gain):
            scale = lax.rsqrt(jnp.mean(value * value, 1, keepdims=True) + eps)
            return turn(value * scale * gain, cos_ref[...], sin_ref[...]).astype(jnp.bfloat16)

        kt_ref[...] = turned(k_ref[...], kn_ref[...])
        vb_ref[...] = v_ref[...].astype(jnp.bfloat16)
        for g in range(per_group):
            at = slice(g * size, (g + 1) * size)
            qt_ref[:, at] = turned(q_ref[:, at], qn_ref[...])
        for first, low, high in plan:
            span = slice(first, first + rows)
            allowed = band(rows, high - low, first, low, pos_ref[span, :])
            for g in range(per_group):
                at = slice(g * size, (g + 1) * size)
                scores = dot_nt(qt_ref[span, at], kt_ref[low:high, :]) * factor
                scores = jnp.where(allowed, scores, NEGATIVE)
                weights = jnp.exp(scores - jnp.max(scores, 1, keepdims=True))
                weights = (weights * (1.0 / jnp.sum(weights, 1, keepdims=True))).astype(jnp.bfloat16)
                mix_ref[span, at] = dot_nn(weights, vb_ref[low:high, :]).astype(jnp.bfloat16)

    group = per_group * size
    outs = tuple(shape_of((tokens, w), jnp.bfloat16) for w in (q_width, k_width, k_width, q_width))
    q_spec = pl.BlockSpec((tokens, group), lambda i, *_: (0, i))
    k_spec = pl.BlockSpec((tokens, size), lambda i, *_: (0, q_width // size + i))
    v_spec = pl.BlockSpec((tokens, size), lambda i, *_: (0, (q_width + k_width) // size + i))
    one = pl.BlockSpec((tokens, size), lambda i, *_: (0, i))
    operands = (raw, raw, raw, position, cos_wide, sin_wide, query_norm, key_norm)
    specs = [q_spec, k_spec, v_spec] + [whole_spec(a) for a in operands[3:]]
    flops = 20 * tokens * (high_sum(plan) * rows // tokens) * q_width
    return kernel_call(
        body, jnp.zeros((1,), jnp.int32), operands, specs, outs, (q_spec, one, one, q_spec), (kv_heads,), [], flops, 48
    )


def high_sum(plan):
    return sum(high - low for _, low, high in plan)


def attend_back(raw, turned_q, turned_k, values, grad_mixed, position, cos_wide, sin_wide, query_norm, key_norm, most, eps):
    tokens, q_width = turned_q.shape
    k_width = turned_k.shape[1]
    size = query_norm.shape[1]
    kv_heads, per_group = k_width // size, q_width // k_width
    factor = 1.0 / math.sqrt(size)
    rows, plan = attention_blocks(tokens, most)

    def body(_, q_ref, k_ref, qt_ref, kt_ref, v_ref, dm_ref, pos_ref, cos_ref, sin_ref, qn_ref, kn_ref,
             dq_ref, dk_ref, dv_ref, gain_ref, key_sum, value_sum):
        key_sum[...] = jnp.zeros_like(key_sum)
        value_sum[...] = jnp.zeros_like(value_sum)

        def back(raw_rows, gain, upstream, span):
            scale = lax.rsqrt(jnp.mean(raw_rows * raw_rows, 1, keepdims=True) + eps)
            turned_back = turn(upstream, cos_ref[span, :], -sin_ref[span, :])
            inner = jnp.mean(turned_back * gain * raw_rows, 1, keepdims=True)
            grad = scale * gain * turned_back - raw_rows * (scale * scale * scale * inner)
            return grad.astype(jnp.bfloat16), jnp.sum(turned_back * raw_rows * scale, 0, keepdims=True)

        query_gain = jnp.zeros((1, size), jnp.float32)
        for first, low, high in plan:
            span = slice(first, first + rows)
            allowed = band(rows, high - low, first, low, pos_ref[span, :])
            for g in range(per_group):
                at = slice(g * size, (g + 1) * size)
                queries, upstream = qt_ref[span, at], dm_ref[span, at]
                scores = dot_nt(queries, kt_ref[low:high, :]) * factor
                scores = jnp.where(allowed, scores, NEGATIVE)
                probs = jnp.exp(scores - jnp.max(scores, 1, keepdims=True))
                probs = probs * (1.0 / jnp.sum(probs, 1, keepdims=True))
                grads = dot_nt(upstream, v_ref[low:high, :])
                weighted = probs * grads
                total = jnp.sum(weighted, 1, keepdims=True)
                grads = (weighted - probs * total).astype(jnp.bfloat16)
                value_sum[low:high, :] += dot_tn(probs.astype(jnp.bfloat16), upstream)
                key_sum[low:high, :] += dot_tn(grads, queries)
                grad_turned = dot_nn(grads, kt_ref[low:high, :]) * factor
                grad, gain = back(q_ref[span, at], qn_ref[...], grad_turned, span)
                dq_ref[span, at] = grad
                query_gain = query_gain + gain
        grad, key_gain = back(k_ref[...], kn_ref[...], key_sum[...] * factor, slice(0, tokens))
        dk_ref[...] = grad
        dv_ref[...] = value_sum[...].astype(jnp.bfloat16)
        gain_ref[...] = jnp.concatenate([query_gain, key_gain, jnp.zeros((6, size), jnp.float32)], 0)

    group = per_group * size
    outs = (
        shape_of((tokens, q_width), jnp.bfloat16),
        shape_of((tokens, k_width), jnp.bfloat16),
        shape_of((tokens, k_width), jnp.bfloat16),
        shape_of((8 * kv_heads, size), jnp.float32),
    )
    q_spec = pl.BlockSpec((tokens, group), lambda i, *_: (0, i))
    k_spec = pl.BlockSpec((tokens, size), lambda i, *_: (0, q_width // size + i))
    one = pl.BlockSpec((tokens, size), lambda i, *_: (0, i))
    operands = (raw, raw, turned_q, turned_k, values, grad_mixed, position, cos_wide, sin_wide, query_norm, key_norm)
    specs = [q_spec, k_spec, q_spec, one, one, q_spec] + [whole_spec(a) for a in operands[6:]]
    out_specs = (q_spec, one, one, pl.BlockSpec((8, size), lambda i, *_: (i, 0)))
    scratch = [pltpu.VMEM((tokens, size), jnp.float32)] * 2
    flops = 28 * tokens * (high_sum(plan) * rows // tokens) * q_width
    return kernel_call(
        body, jnp.zeros((1,), jnp.int32), operands, specs, outs, out_specs, (kv_heads,), scratch, flops, 48
    )


def local(
    hidden_in,
    seq_lengths,
    attn_norm,
    w_query,
    key_weight,
    value_weight,
    query_norm,
    key_norm,
    w_output,
    ffwd_norm,
    w_gate,
    w_up,
    w_down,
    cotangent,
):
    low, f32 = jnp.bfloat16, jnp.float32
    tokens, part_width = hidden_in.shape
    full_width = part_width * lax.axis_size("col")
    head_size = query_norm.shape[0]
    q_width, k_width = w_query.shape[1], key_weight.shape[1]
    ring = Ring()
    place, plain_place, pair_place = ring.place, ring.plain_place, ring.pair_place
    steps, pairs, half = ring.half, ring.half, tokens // 2
    pair_order = jnp.arange(pairs, dtype=jnp.int32)
    chain = Chain()
    pin, run = chain.pin, chain.run

    def near(value):
        return swap(value, "col", 1)

    def far(value):
        return swap(value, "col", 2)

    qkv, hidden_in = pin(jnp.concatenate([w_query, key_weight, value_weight], 1), hidden_in)
    qkv = ring.inner_gather(qkv, 0)
    on, back = ring.send_on(qkv), ring.send_back(qkv)
    output_all = ring.gather_stack(ring.inner_gather(w_output, 1))
    hidden_far = far(hidden_in)
    gains = jnp.stack([attn_norm, ffwd_norm])
    gains_far = far(gains)
    behind, ahead = [], []
    on, back = pin(on, back)
    behind.append(on)
    ahead.append(back)
    on, back = ring.send_on(on), ring.send_back(back)
    hidden_far, gains_far = pin(hidden_far, gains_far)
    hidden_blocks = [hidden_in, hidden_far, near(hidden_in), near(hidden_far)]
    gains_near = near(gains)
    on, back, gains_near, gate, up = pin(on, back, gains_near, w_gate, w_up)
    behind.append(on)
    ahead.append(back)
    on, back = ring.send_on(on), ring.send_back(back)
    gate_up = [ring.inner_gather(w, 0) for w in (gate, up)]
    gate_up_mine = side_of(gate_up, 1, ring.parity)
    gate_up_got = ring.to_partner(side_of(gate_up, 1, 1 - ring.parity))
    gains_diagonal, gate_up_mine, *hidden_blocks = pin(near(gains_far), gate_up_mine, *hidden_blocks)
    position = tables(seq_lengths[0], tokens)[:, None]
    position, cos_wide, sin_wide, behind_order = pin(position, *rotary(position[:, 0], head_size), ring.behind)
    on, back = pin(on, back)
    behind.append(on)
    ahead.append(back)
    cut = on.shape[0] // 2
    on, back = ring.send_on(on[:cut]), ring.send_back(back[cut:])
    gate_up_got, output_all = pin(gate_up_got, output_all)
    gate_up_all = pair_gather(ring, run(above, gate_up_mine, gate_up_got))
    on, back = pin(on, back)
    qkv_all = [qkv, *behind, jnp.concatenate([on, back], 0), *ahead[::-1]]
    gains = jnp.stack([gains, gains_far, gains_near, gains_diagonal], 1).reshape(2, 1, full_width)

    down, upstream = pin(w_down, cotangent)
    down = [ring.inner_gather(down, 1)]
    down_mine = side_of(down, 0, ring.parity)
    down_got = ring.to_partner(side_of(down, 0, 1 - ring.parity))
    up_far, up_partner = far(upstream), ring.to_partner(upstream)
    turning = (position, cos_wide, sin_wide, query_norm[None, :], key_norm[None, :])
    residual = hidden_in.astype(f32)
    wide_one, factor_one, qkv_raw = run(
        lambda blocks, gain, weights: gather_norm_matmul(place, blocks, gain, weights, EPS), hidden_blocks, gains[0], qkv_all
    )
    turned_q, turned_k, values, mixed = run(
        lambda raw: attend(raw, *turning, q_width, k_width, MOST, EPS), qkv_raw
    )
    up_far, up_partner, down_got, down_mine = pin(up_far, up_partner, down_got, down_mine)
    own, to_far, to_near, to_diagonal = run(
        lambda left, weights: spread_product(plain_place, left, [weights], False), mixed, output_all
    )
    got_far, got_own = near(to_diagonal), near(to_near)
    up_near, up_diagonal = near(upstream), near(up_far)
    to_far, got_far = pin(to_far, got_far)
    attended = far(pin((to_far.astype(f32) + got_far).astype(low)))
    corner = far(pin(up_partner[:half])), ring.to_partner(up_far[half:])
    up_near, up_diagonal = pin(up_near, up_diagonal)
    upstream_wide = run(lambda *blocks: assemble(pair_place, blocks), upstream, up_far, up_near, up_diagonal)
    attended, own, got_own = pin(attended, own, got_own)

    middle = residual + own + got_own + attended
    middle, middle_low = pin(middle, middle.astype(low))
    mid_far, mid_partner = far(middle_low), ring.to_partner(middle_low)
    mid_near = near(middle_low)
    up_corner = pin(jnp.concatenate(pin(*corner), 0))
    up_partner_near, up_corner_near = near(up_partner), near(up_corner)
    down_unit = pin(jnp.concatenate([down_mine, down_got], 1))
    mid_near, up_partner_near, up_corner_near = pin(mid_near, up_partner_near, up_corner_near)
    upstream_other = run(lambda *blocks: assemble(pair_place, blocks), up_partner, up_corner, up_partner_near, up_corner_near)
    mid_far = pin(mid_far)
    mid_diagonal = near(mid_far)
    mid_diagonal, mid_partner = pin(mid_diagonal, mid_partner)
    corner = far(mid_partner[:half]), ring.to_partner(mid_far[half:])
    mid_partner_near = near(mid_partner)
    gate_up_all = pin(gate_up_all)
    down_all = pair_gather(ring, down_unit)

    def swish(blocks, gain, weights):
        return gather_swish(pair_place, blocks, gain, weights, EPS)

    normed, factor_two, gate, up, hidden = run(
        swish, [middle_low, mid_far, mid_near, mid_diagonal], gains[1], gate_up_all
    )
    mid_partner_near, *corner = pin(mid_partner_near, *corner)
    mid_corner = pin(jnp.concatenate(corner, 0))
    mid_corner_near = pin(near(mid_corner))
    normed_other, _, gate_other, up_other, hidden_other = run(
        swish, [mid_partner, mid_corner, mid_partner_near, mid_corner_near], gains[1], gate_up_all
    )
    down_grad = run(
        lambda *ops: weight_grad(ops[:2], ops[2:], pair_order, False), hidden, hidden_other, upstream_wide, upstream_other
    )
    down_grad = pair_sum(ring, down_grad)

    down_all = pin(down_all)

    def back_swish(wide, weights, gate_value, up_value):
        return swish_back(wide, [weights], gate_value, up_value)

    def spread_back(left, weights):
        return spread_product(pair_place, left, [weights], True)

    low_other, inner_other = run(back_swish, upstream_other, down_all, gate_other, up_other)
    own_other, far_other, near_other, diagonal_other = run(spread_back, low_other, gate_up_all)
    diagonal_other, near_other, inner_other = near(diagonal_other), near(near_other), ring.to_partner(pin(inner_other[:, 0]))
    low_mine, inner, diagonal_other, near_other, inner_other = run(
        back_swish, upstream_wide, down_all, gate, up, beside=(diagonal_other, near_other, inner_other)
    )
    corner = pin((pin(far_other).astype(f32) + diagonal_other).astype(low))
    from_far, from_partner = far(corner[:half]), ring.to_partner(corner[half:])
    inner = pin(inner[:, 0] + inner_other)
    inner_near = near(inner)
    own, to_far, to_near, to_diagonal, from_far, from_partner, inner_near = run(
        spread_back, low_mine, gate_up_all, beside=(from_far, from_partner, inner_near)
    )
    got_far, got_own = near(to_diagonal), near(to_near)
    inner = pin(inner + inner_near)
    inner_far = far(inner)
    to_partner = own_other.astype(f32) + near_other
    to_partner = jnp.concatenate([to_partner[:half] + from_far, to_partner[half:]], 0)
    to_far, got_far, to_partner = pin(to_far, got_far, to_partner.astype(low))
    to_partner = ring.to_partner(to_partner)
    to_far = to_far.astype(f32) + got_far
    to_far = jnp.concatenate([to_far[:half], to_far[half:] + from_partner], 0)
    own, got_own, to_far, inner_far = pin(own, got_own, to_far.astype(low), inner_far)
    from_far = far(to_far)
    gate_up_grad = run(
        lambda *ops: weight_grad(ops[:2], ops[2:], pair_order, True), normed, normed_other, low_mine, low_other
    )
    inner = (inner + inner_far)[:, None] / full_width
    own, got_own, from_partner, from_far, inner, down_grad, gate_up_grad = pin(
        own, got_own, to_partner, from_far, inner, down_grad, gate_up_grad
    )
    gate_up_grad = pair_sum(ring, gate_up_grad)

    def spread_down(left, weights):
        return spread_product(pair_place, left, [weights], False)

    grad_normed = own.astype(f32) + got_own + from_partner + from_far
    grad_middle = (
        cotangent.astype(f32)
        + factor_two * ffwd_norm * grad_normed
        - middle * (factor_two * factor_two * inner)
    )
    grad_middle, grad_low = pin(grad_middle, grad_middle.astype(low))
    grad_far, grad_near = far(grad_low), near(grad_low)
    down_got = ring.to_partner(pin(down_grad[:, down_grad.shape[1] // 2 :]))
    own_other, far_other, near_other, diagonal_other = run(spread_down, hidden_other, down_all)
    out_own, out_to_far, out_to_near, out_to_diagonal, grad_near, down_got = run(
        spread_down, hidden, down_all, beside=(grad_near, down_got)
    )
    near_other, diagonal_other = near(near_other), near(diagonal_other)
    grad_far = pin(grad_far)
    grad_diagonal = near(grad_far)
    near_other, diagonal_other, grad_diagonal, own_other, far_other = pin(
        near_other, diagonal_other, grad_diagonal, own_other, far_other
    )
    out_first, out_second = pin(
        (own_other.astype(f32) + near_other).astype(low), (far_other.astype(f32) + diagonal_other).astype(low)
    )
    out_first = ring.to_partner(out_first)
    out_got_own, out_got_far = near(out_to_near), near(out_to_diagonal)
    ffwd_gain = pin(jnp.sum(grad_normed * middle * factor_two, 0))

    middle_wide = run(lambda *blocks: assemble(place, blocks), grad_low, grad_far, grad_near, grad_diagonal)
    grad_mixed = run(lambda wide, weights: times_transposed(wide, [weights], behind_order), middle_wide, output_all)
    query_low, key_low, value_low, head_gains, out_first, out_got_own, out_got_far = run(
        lambda *ops: attend_back(*ops, *turning, MOST, EPS),
        qkv_raw,
        turned_q,
        turned_k,
        values,
        grad_mixed,
        beside=(out_first, out_got_own, out_got_far),
    )
    out_second = ring.to_partner(out_second)
    qkv_low = pin(jnp.concatenate([query_low, key_low, value_low], 1))

    def parts(*numbers, beside=()):
        order = jnp.array(numbers, jnp.int32)
        return run(
            lambda *ops: block_grads(ops[:2], ops[2:], order, ring.count), wide_one, middle_wide, qkv_low, mixed, beside=beside
        )

    def go(on, back, *beside):
        on, back, *beside = pin(on.astype(low), back.astype(low), *beside)
        return ring.send_on(on), ring.send_back(back), *beside

    first = parts(steps)
    cut = first.shape[1] // 2
    on, back = go(first[0, :cut], first[0, cut:])
    own_first, to_far, to_near, to_diagonal, inner, attn_gain = run(
        lambda left, weights, wide: spread_product(place, left, weights, True, wide, True), qkv_low, qkv_all, wide_one
    )
    got_far, got_own = near(to_diagonal), near(to_near)
    second = parts(steps + 1, steps - 1)
    own, on, back, out_second = parts(
        *(n for s in range(2, steps) for n in (steps + s, steps - s)), 0, beside=(on, back, out_second)
    )
    on = jnp.concatenate([second[0, :cut] + on.astype(f32), second[0, cut:].astype(f32)], 0)
    back = jnp.concatenate([second[1, :cut].astype(f32), second[1, cut:] + back.astype(f32)], 0)
    on, back, got_far, got_own, to_far = go(on, back, got_far, got_own, to_far)
    to_far = pin((to_far.astype(f32) + got_far).astype(low))
    gain_keep, gain_send = attn_gain[:1, : full_width // 2], attn_gain[:1, full_width // 2 :]
    head_gains = jnp.sum(head_gains.reshape(-1, 8, head_size), 0)[:2].reshape(-1)
    sums = pin(jnp.concatenate([gain_send[0], head_gains, inner[:, 0]]))
    sums_got = pin(near(sums))
    both_gain = gain_keep[0] + sums_got[: full_width // 2]
    sums = pin(jnp.concatenate([both_gain[part_width:], (sums + sums_got)[full_width // 2 :]]))
    sums_got = far(sums)
    grad_far = far(to_far)
    sums_got, out_to_far, gate_up_grad = pin(sums_got, out_to_far, gate_up_grad)
    columns_here = gate_up_grad.shape[0] // 2
    gate_up_got = ring.to_partner(pin(gate_up_grad[columns_here:]))
    attn_gain = (both_gain[:part_width] + sums_got[:part_width]) / attn_norm
    rest = (sums + sums_got)[part_width:]
    inner = rest[2 * head_size :][:, None] / full_width
    sums = jnp.concatenate([attn_gain, ffwd_gain, rest[: 2 * head_size]])
    sums, inner = pin(sums, inner)
    bits = [1 << n for n in range(lax.axis_size("row").bit_length() - 1)]
    sums_got = swap(sums, "row", bits[0])
    on, back, sums_got = pin(on, back, sums_got)
    on, back = go(own[0] + on.astype(f32), own[1] + back.astype(f32))
    sums = pin(sums + sums_got)
    sums_got = swap(sums, "row", bits[1])
    grad_far = pin(grad_far)
    to_far = (out_to_far.astype(f32) + out_got_far + out_second).astype(low)
    hidden_grad = (
        grad_middle
        + factor_one * attn_norm * (own_first.astype(f32) + got_own + grad_far)
        - residual * (factor_one * factor_one * inner)
    )
    hidden_grad, to_far = pin(hidden_grad, to_far)
    out_far = far(to_far)
    on, back, sums_got = pin(on, back, sums_got)
    gate_up_got = pin(gate_up_got)
    on, back = go(own[2] + on.astype(f32), own[3] + back.astype(f32))
    sums = pin(sums + sums_got)
    for bit in bits[2:-1]:
        sums = pin(sums + pin(swap(sums, "row", bit)))
    sums_got = swap(sums, "row", bits[-1])
    gate_up_grad, gate_up_got, down_got = pin(gate_up_grad, gate_up_got, down_got)
    gate_grad, up_grad = (
        pair_join(ring, gate_up_grad[:columns_here, at], gate_up_got[:, at], 1)
        for at in (slice(0, gate_up_grad.shape[1] // 2), slice(gate_up_grad.shape[1] // 2, None))
    )
    down_out = pair_join(ring, down_grad[:, : down_grad.shape[1] // 2], down_got, 0)
    gate_grad, up_grad, down_out = pin(gate_grad, up_grad, down_out)
    out_far = pin(out_far)
    hidden_out = pin((middle + out_own + out_got_own + out_first + out_far).astype(low))
    on, back, sums_got = pin(on, back, sums_got)
    sums = sums + sums_got
    total = ring.inner_sum(own[4].astype(f32) + on + back, 0)
    attn_gain, ffwd_gain, query_gain, key_gain = jnp.split(
        sums, [part_width, 2 * part_width, 2 * part_width + head_size]
    )
    return (
        hidden_out,
        hidden_grad,
        attn_gain,
        total[:, :q_width],
        total[:, q_width : q_width + k_width],
        total[:, q_width + k_width : q_width + 2 * k_width],
        query_gain,
        key_gain,
        total[:, q_width + 2 * k_width :].T,
        ffwd_gain,
        gate_grad,
        up_grad,
        down_out,
    )


def solution(mesh):
    in_specs = (
        P("row", "col"),
        P("row", None),
        P("col"),
        P("row", "col"),
        P("row", "col"),
        P("row", "col"),
        P(),
        P(),
        P("col", "row"),
        P("col"),
        P("row", "col"),
        P("row", "col"),
        P("col", "row"),
        P("row", "col"),
    )
    out_specs = (
        P("row", "col"),
        P("row", "col"),
        P("col"),
        P("row", "col"),
        P("row", "col"),
        P("row", "col"),
        P(),
        P(),
        P("col", "row"),
        P("col"),
        P("row", "col"),
        P("row", "col"),
        P("col", "row"),
    )
    return jax.shard_map(local, mesh=mesh, in_specs=in_specs, out_specs=out_specs, check_vma=False)
```

```python
import math

import jax
import jax.numpy as jnp
from jax import lax
from jax.experimental import pallas as pl
from jax.experimental.pallas import tpu as pltpu
from jax.sharding import PartitionSpec as P

EPS = 1e-06
THETA = 1000000.0
NEGATIVE = -1e30
MOST = 512
COST_SCALE = 0.02


def tables(lengths_row, row_number_total):
    steps_idx = jnp.arange(row_number_total, dtype=jnp.int32)
    seq_ends = jnp.cumsum(lengths_row)
    seq_starts = seq_ends - lengths_row
    segment = jnp.sum((steps_idx[:, None] >= seq_ends[None, :]).astype(jnp.int32), 1)
    member = segment[:, None] == jnp.arange(lengths_row.shape[0], dtype=jnp.int32)[None, :]
    return steps_idx - jnp.sum(jnp.where(member, seq_starts[None, :], 0), 1)


def rotary(position, head_size):
    half_size = head_size // 2
    frequency = THETA ** (-(jnp.arange(half_size, dtype=jnp.float32) * 2.0 / head_size))
    angles = position.astype(jnp.float32)[:, None] * frequency[None, :]
    cosines, sines = jnp.cos(angles), jnp.sin(angles)
    return jnp.concatenate([cosines, cosines], 1), jnp.concatenate([-sines, sines], 1)


def ring_order(count):
    return list(range(0, count, 2)) + list(range(count - 1, 0, -2))


class Ring:
    def __init__(self):
        rows = lax.axis_size("row")
        self.count = count = min(8, rows)
        self.half = count // 2
        self.members = members = rows // count
        self.groups = [[g * members + m for m in range(members)] for g in range(count)]
        self.lanes = None if members == 1 else [[g * members + m for g in range(count)] for m in range(members)]
        order = ring_order(count)
        self.onward = self.spell([(order[i], order[(i + 1) % count]) for i in range(count)])
        self.backward = [(b, a) for a, b in self.onward]
        self.partner = self.spell([(g, g ^ 1) for g in range(count)])
        self.pairs = [[(2 * p + side) * members + m for p in range(count // 2)] for side in range(2) for m in range(members)]
        group = lax.axis_index("row") // members
        self.parity = group % 2
        self.place = self.places([[order[(order.index(g) - j) % count] for j in range(count)] for g in range(count)])
        self.behind = jnp.array([[order[(order.index(g) - j) % count] for j in range(count)] for g in range(count)])[group]
        self.plain_place = self.places([list(range(count))] * count)
        self.pair_place = self.places(
            [[j // 2 * 2 + (g % 2 ^ j % 2) for j in range(count)] for g in range(count)]
        )

    def spell(self, pairs):
        return [(a * self.members + m, b * self.members + m) for a, b in pairs for m in range(self.members)]

    def places(self, behind):
        cols = lax.axis_size("col")
        per_col = self.count // cols
        table = [
            [[COL_ORDER.index((b // per_col) ^ c) * per_col + b % per_col for b in row] for c in range(cols)]
            for row in behind
        ]
        return jnp.array(table, jnp.int32)[lax.axis_index("row") // self.members, lax.axis_index("col")]

    def send_on(self, value):
        return lax.ppermute(value, "row", self.onward)

    def send_back(self, value):
        return lax.ppermute(value, "row", self.backward)

    def to_partner(self, value):
        return lax.ppermute(value, "row", self.partner)

    def gather_stack(self, block):
        return lax.all_gather(block, "row", axis=0, axis_index_groups=self.lanes)

    def sum_stack(self, blocks):
        return lax.psum_scatter(blocks, "row", scatter_dimension=0, axis_index_groups=self.lanes)

    def inner_gather(self, block, axis):
        if self.members == 1:
            return block
        return lax.all_gather(block, "row", axis=axis, tiled=True, axis_index_groups=self.groups)

    def inner_sum(self, value, axis):
        if self.members == 1:
            return value
        value = value.astype(jnp.bfloat16)
        return lax.psum_scatter(
            value, "row", scatter_dimension=axis, tiled=True, axis_index_groups=self.groups
        ).astype(jnp.float32)


def side_of(blocks, axis, number):
    halves = [b.shape[axis] // 2 for b in blocks]
    cuts = [lax.dynamic_slice_in_dim(b, number * h, h, axis) for b, h in zip(blocks, halves, strict=True)]
    return jnp.concatenate(cuts, axis)


def pair_gather(ring, unit):
    return lax.all_gather(unit, "row", axis=0, axis_index_groups=ring.pairs)


def pair_sum(ring, units):
    return lax.psum_scatter(units, "row", scatter_dimension=0, axis_index_groups=ring.pairs)


def pair_join(ring, mine, got, axis):
    first = ring.parity == 0
    mine, got = mine.astype(jnp.float32), got.astype(jnp.float32)
    value = jnp.concatenate([jnp.where(first, mine, got), jnp.where(first, got, mine)], axis)
    return ring.inner_sum(value, 1 - axis)


class Chain:
    def __init__(self):
        self.token = lax.create_token()

    def pin(self, *values):
        self.token, *values = lax.optimization_barrier((self.token, *values))
        return values if len(values) > 1 else values[0]

    def run(self, kernel, *operands, beside=()):
        results = kernel(*self.pin(operands))
        results = tuple(results) if isinstance(results, (list, tuple)) else (results,)
        return self.pin(*results, *beside)


COL_ORDER = (0, 2, 1, 3)


def swap(value, axis, bit):
    return lax.ppermute(value, axis, [(i, i ^ bit) for i in range(lax.axis_size(axis))])


def dot_nt(left_side, right_side):
    return lax.dot_general(
        left_side, right_side, (((1,), (1,)), ((), ())), preferred_element_type=jnp.float32
    )


def dot_nn(left_side, right_side):
    return jnp.dot(left_side, right_side, preferred_element_type=jnp.float32)


def dot_tn(left_side, right_side):
    return lax.dot_general(
        left_side, right_side, (((0,), (0,)), ((), ())), preferred_element_type=jnp.float32
    )


def cost(flops):
    return pl.CostEstimate(flops=int(COST_SCALE * flops), bytes_accessed=1 << 16, transcendentals=0)


def kernel_call(body, places, operands, specs, outs, out_specs, grid, scratch, flops, mib):
    return pl.pallas_call(
        body,
        grid_spec=pltpu.PrefetchScalarGridSpec(
            num_scalar_prefetch=1,
            grid=grid,
            in_specs=specs,
            out_specs=out_specs,
            scratch_shapes=scratch,
        ),
        out_shape=outs,
        cost_estimate=cost(flops),
        compiler_params=pltpu.CompilerParams(vmem_limit_bytes=mib << 20),
    )(places, *operands)


def whole_spec(array, buffers=1):
    zeros = (0,) * len(array.shape)
    return pl.BlockSpec(array.shape, lambda *_: zeros, pipeline_mode=pl.Buffered(buffers))


def rows_spec(array, rows):
    return pl.BlockSpec((rows,) + tuple(array.shape[1:]), lambda i, *_: (i,) + (0,) * (len(array.shape) - 1))


def columns_spec(array, columns):
    return pl.BlockSpec((array.shape[0], columns), lambda i, *_: (0, i))


def shape_of(shape, dtype):
    return jax.ShapeDtypeStruct(shape, dtype)


def piece_at(place_ref, j, piece):
    return pl.ds(pl.multiple_of(place_ref[j] * piece, piece), piece)


def norm_rows(place_ref, x_refs, gain_ref, wide_ref, factor_ref, all_ref, piece, eps):
    tokens, full = wide_ref.shape
    width = x_refs[0].shape[1]
    total = jnp.zeros((tokens, 1), jnp.float32)
    for i, x_ref in enumerate(x_refs):
        value = x_ref[...]
        all_ref[:, i * width : (i + 1) * width] = value
        value = value.astype(jnp.float32)
        total = total + jnp.sum(value * value, 1, keepdims=True)
    factor = lax.rsqrt(total / full + eps)
    factor_ref[...] = factor
    for j in range(full // piece):
        at = piece_at(place_ref, j, piece)
        value = all_ref[:, at].astype(jnp.float32) * factor * gain_ref[:, at]
        wide_ref[:, j * piece : (j + 1) * piece] = value.astype(jnp.bfloat16)


def gather_norm_matmul(place, hidden_blocks, gain, weights, eps):
    tokens, width = hidden_blocks[0].shape
    full = width * len(hidden_blocks)
    count = len(weights)
    piece, columns = weights[0].shape
    tile = min(512, columns)
    many = len(hidden_blocks)

    def body(place_ref, *refs):
        x_refs, gain_ref = refs[:many], refs[many]
        w_refs = refs[many + 1 : many + 1 + count]
        wide_ref, factor_ref, out_ref, all_ref = refs[many + 1 + count :]

        @pl.when(pl.program_id(0) == 0)
        def _():
            norm_rows(place_ref, x_refs, gain_ref, wide_ref, factor_ref, all_ref, piece, eps)

        total = dot_nn(wide_ref[:, :piece], w_refs[0][...])
        for j in range(1, count):
            total = total + dot_nn(wide_ref[:, j * piece : (j + 1) * piece], w_refs[j][...])
        out_ref[...] = total

    outs = (
        shape_of((tokens, full), jnp.bfloat16),
        shape_of((tokens, 1), jnp.float32),
        shape_of((tokens, columns), jnp.float32),
    )
    operands = (*hidden_blocks, gain, *weights)
    specs = [whole_spec(b) for b in hidden_blocks] + [whole_spec(gain)] + [columns_spec(w, tile) for w in weights]
    out_specs = (whole_spec(outs[0]), whole_spec(outs[1]), columns_spec(outs[2], tile))
    scratch = [pltpu.VMEM((tokens, full), jnp.bfloat16)]
    return kernel_call(
        body, place, operands, specs, outs, out_specs, (columns // tile,), scratch, 2 * tokens * full * columns, 48
    )


def above(first, second):
    def body(_, first_ref, second_ref, out_ref):
        @pl.when(pl.program_id(0) == 0)
        def _():
            out_ref[...] = first_ref[...]

        @pl.when(pl.program_id(0) == 1)
        def _():
            out_ref[...] = second_ref[...]

    rows, columns = first.shape
    out = shape_of((2 * rows, columns), first.dtype)
    return kernel_call(
        body, jnp.zeros((1,), jnp.int32), (first, second), [whole_spec(first), whole_spec(second)], (out,),
        (rows_spec(out, rows),), (2,), [], 0, 32,
    )[0]


def units_of(refs):
    return [refs[0].at[j] for j in range(refs[0].shape[0])] if len(refs) == 1 else refs


def gather_swish(place, blocks, gain, weights, eps):
    tokens, width = blocks[0].shape
    count, unit, both = weights.shape
    columns = both // 2
    full, many = width * len(blocks), len(blocks)
    piece = full // place.shape[0]
    tile = min(256, columns)

    def body(place_ref, *refs):
        x_refs, gain_ref, g_ref, u_ref = refs[:many], refs[many], refs[many + 1], refs[many + 2]
        wide_ref, factor_ref, gate_ref, up_ref, hidden_ref, all_ref = refs[many + 3 :]

        @pl.when(pl.program_id(0) == 0)
        def _():
            norm_rows(place_ref, x_refs, gain_ref, wide_ref, factor_ref, all_ref, piece, eps)

        def product(w_ref):
            total = dot_nn(wide_ref[:, :unit], w_ref[0])
            for j in range(1, count):
                total = total + dot_nn(wide_ref[:, j * unit : (j + 1) * unit], w_ref[j])
            return total

        gate = product(g_ref)
        gate_ref[...] = gate
        up = product(u_ref)
        up_ref[...] = up
        hidden_ref[...] = (gate / (1.0 + jnp.exp(-gate)) * up).astype(jnp.bfloat16)

    outs = (
        shape_of((tokens, full), jnp.bfloat16),
        shape_of((tokens, 1), jnp.float32),
        shape_of((tokens, columns), jnp.float32),
        shape_of((tokens, columns), jnp.float32),
        shape_of((tokens, columns), jnp.bfloat16),
    )
    operands = (*blocks, gain, weights, weights)
    steps = columns // tile
    specs = [whole_spec(b) for b in (*blocks, gain)] + [
        pl.BlockSpec((count, unit, tile), lambda i, *_: (0, 0, i)),
        pl.BlockSpec((count, unit, tile), lambda i, *_: (0, 0, i + steps)),
    ]
    out_specs = (whole_spec(outs[0]), whole_spec(outs[1])) + tuple(columns_spec(o, tile) for o in outs[2:])
    scratch = [pltpu.VMEM((tokens, full), jnp.bfloat16)]
    return kernel_call(
        body, place, operands, specs, outs, out_specs, (steps,), scratch, 4 * tokens * full * columns, 48
    )


def spread_product(place, left, weights, transposed, normed=None, by_feature=False):
    tokens, inner = left.shape
    many = len(weights)
    count = many if many > 1 else weights[0].shape[0]
    unit = weights[0].shape[-2 if transposed else -1]
    full = unit * count
    piece = full // place.shape[0]
    per_unit = unit // piece
    tile = min(256, tokens)
    dot = dot_nt if transposed else dot_nn
    extras = () if normed is None else (normed,)

    def body(place_ref, *refs):
        y_ref, w_refs = refs[0], units_of(refs[1 : 1 + many])
        rest = refs[1 + many + len(extras) :]
        part_refs, all_ref = rest[:cols], rest[-1]
        rows = jnp.zeros((tile, 1), jnp.float32)
        if by_feature:

            @pl.when(pl.program_id(0) == 0)
            def _():
                rest[cols + 1][...] = jnp.zeros_like(rest[cols + 1])

        for j in range(count):
            total = dot(y_ref[...], w_refs[j][...])
            if extras:
                weighted = total * refs[1 + many][:, j * unit : (j + 1) * unit].astype(jnp.float32)
                rows = rows + jnp.sum(weighted, 1, keepdims=True)
                if by_feature:
                    sums = jnp.broadcast_to(jnp.sum(weighted, 0, keepdims=True), (8, unit))
                    for i in range(per_unit):
                        at = piece_at(place_ref, j * per_unit + i, piece)
                        rest[cols + 1][:, at] += sums[:, i * piece : (i + 1) * piece]
            total = total.astype(jnp.bfloat16)
            for i in range(per_unit):
                at = piece_at(place_ref, j * per_unit + i, piece)
                all_ref[:, at] = total[:, i * piece : (i + 1) * piece]
        for c, ref in enumerate(part_refs):
            ref[...] = all_ref[:, c * (full // cols) : (c + 1) * (full // cols)]
        if extras:
            rest[cols][...] = rows

    cols = len(COL_ORDER)
    outs = (shape_of((tokens, full // cols), jnp.bfloat16),) * cols
    if extras:
        outs += (shape_of((tokens, 1), jnp.float32),)
    operands = (left, *weights, *extras)
    specs = [rows_spec(left, tile)] + [whole_spec(w) for w in weights] + [rows_spec(e, tile) for e in extras]
    out_specs = tuple(rows_spec(o, tile) for o in outs)
    if by_feature:
        outs += (shape_of((8, full), jnp.float32),)
        out_specs += (whole_spec(outs[cols + 1]),)
    scratch = [pltpu.VMEM((tile, full), jnp.bfloat16)]
    return kernel_call(
        body, place, operands, specs, outs, out_specs, (tokens // tile,), scratch, 2 * tokens * full * inner, 48
    )


def assemble(place, blocks):
    tokens, width = blocks[0].shape
    many = len(blocks)
    full = width * many
    piece = full // place.shape[0]
    tile = min(256, tokens)

    def body(place_ref, *refs):
        x_refs, (wide_ref, all_ref) = refs[:many], refs[many:]
        for i in range(many):
            all_ref[:, i * width : (i + 1) * width] = x_refs[i][...]
        for j in range(full // piece):
            wide_ref[:, j * piece : (j + 1) * piece] = all_ref[:, piece_at(place_ref, j, piece)]

    outs = (shape_of((tokens, full), jnp.bfloat16),)
    specs = [rows_spec(b, tile) for b in blocks]
    scratch = [pltpu.VMEM((tile, full), jnp.bfloat16)]
    return kernel_call(
        body, place, blocks, specs, outs, (rows_spec(outs[0], tile),), (tokens // tile,), scratch, 1500 * tokens * 1024, 32
    )[0]


def times_transposed(wide, weights, order):
    return back_product(wide, weights, (), lambda total: (total,), order)[0]


def swish_back(wide, weights, gate, up):
    def gradients(total, gate_value, up_value):
        sigma = 1.0 / (1.0 + jnp.exp(-gate_value))
        grad_gate = total * up_value * sigma * (1.0 + gate_value * (1.0 - sigma))
        grad_up = total * gate_value * sigma
        return grad_gate, grad_up, jnp.sum(grad_gate * gate_value + grad_up * up_value, 1, keepdims=True)

    return back_product(wide, weights, (gate, up), gradients)


def back_product(wide, weights, extras, epilogue, order=None):
    tokens, full = wide.shape
    others, units = len(extras), len(weights)
    count = units if units > 1 else weights[0].shape[0]
    columns, unit = weights[0].shape[-2:]
    tile = min(256, tokens)
    parts = max(1, others)

    stacked = order is not None

    def body(order_ref, *refs):
        wide_ref, extra_refs = refs[0], refs[1 : 1 + others]
        w_refs, out_ref = refs[1 + others : 1 + others + units], refs[1 + others + units]
        if not stacked:
            w_refs = units_of(w_refs)
        else:
            w_refs = [w_refs[0].at[order_ref[j]] for j in range(count)]
        total = dot_nt(wide_ref[:, :unit], w_refs[0][...])
        for j in range(1, count):
            total = total + dot_nt(wide_ref[:, j * unit : (j + 1) * unit], w_refs[j][...])
        results = epilogue(total, *(e[...] for e in extra_refs))
        for i, part in enumerate(results[:parts]):
            out_ref[:, i * columns : (i + 1) * columns] = part.astype(jnp.bfloat16)
        for ref, value in zip(refs[2 + others + units :], results[parts:], strict=True):
            ref[...] = value

    outs = (shape_of((tokens, parts * columns), jnp.bfloat16),)
    if extras:
        outs += (shape_of((tokens, 1), jnp.float32),)
    operands = (wide, *extras, *weights)
    specs = [rows_spec(b, tile) for b in (wide, *extras)] + [whole_spec(w) for w in weights]
    order = order if stacked else jnp.zeros((1,), jnp.int32)
    return kernel_call(
        body, order, operands, specs, outs, tuple(rows_spec(o, tile) for o in outs), (tokens // tile,), [],
        2 * tokens * full * columns, 48,
    )


def weight_grad(lefts, rights, order, by_left):
    tokens, rows = lefts[0].shape
    columns = rights[0].shape[1]
    many = len(lefts)
    units = order.shape[0]
    rows, columns = (rows // units, columns) if by_left else (rows, columns // units)

    def body(_, *refs):
        out_ref = refs[-1]
        total = dot_tn(refs[0][...], refs[many][...])
        for c in range(1, many):
            total = total + dot_tn(refs[c][...], refs[many + c][...])
        out_ref[0] = total.astype(jnp.bfloat16)

    outs = (shape_of((units, rows, columns), jnp.bfloat16),)
    moving = pl.BlockSpec((tokens, rows if by_left else columns), lambda i, *_: (0, i))
    left_specs = [moving if by_left else whole_spec(a) for a in lefts]
    right_specs = [whole_spec(a) if by_left else moving for a in rights]
    out_specs = (pl.BlockSpec((1, rows, columns), lambda i, order_ref: (order_ref[i], 0, 0)),)
    flops = 2 * tokens * many * units * rows * columns
    operands = (*lefts, *rights)
    return kernel_call(
        body, order, operands, left_specs + right_specs, outs, out_specs, (units,), [], flops, 56
    )[0]


def block_grads(lefts, rights, order, count):
    tokens, full = lefts[0].shape
    rows = full // count
    widths = [right.shape[1] for right in rights]
    many, steps = len(lefts), order.shape[0]

    def body(_, *refs):
        start = 0
        for c, width in enumerate(widths):
            refs[-1][0, :, start : start + width] = dot_tn(refs[c][...], refs[many + c][...]).astype(jnp.bfloat16)
            start += width

    outs = (shape_of((steps, rows, sum(widths)), jnp.bfloat16),)
    operands = (*lefts, *rights)
    specs = [pl.BlockSpec((tokens, rows), lambda i, order_ref: (0, order_ref[i]))] * many
    specs += [whole_spec(a) for a in operands[many:]]
    return kernel_call(
        body, order, operands, specs, outs, (pl.BlockSpec((1, rows, sum(widths)), lambda i, *_: (i, 0, 0)),), (steps,), [],
        2 * tokens * steps * rows * sum(widths), 60,
    )[0]


def turn(values, cos_wide, sin_wide):
    return values * cos_wide + pltpu.roll(values, values.shape[1] // 2, 1) * sin_wide


def band(rows, cols, first_row, first_col, position):
    distance = (
        lax.broadcasted_iota(jnp.int32, (rows, cols), 0)
        + (first_row - first_col)
        - lax.broadcasted_iota(jnp.int32, (rows, cols), 1)
    )
    return (distance >= 0) & (distance <= position)


def attention_blocks(tokens, most):
    rows = min(256, tokens)
    reach = -(-(most - 1) // rows)
    return rows, [(i * rows, max(0, i - reach) * rows, (i + 1) * rows) for i in range(tokens // rows)]


def attend(raw, position, cos_wide, sin_wide, query_norm, key_norm, q_width, k_width, most, eps):
    tokens = raw.shape[0]
    size = query_norm.shape[1]
    kv_heads, per_group = k_width // size, q_width // k_width
    factor = 1.0 / math.sqrt(size)
    rows, plan = attention_blocks(tokens, most)

    def body(_, q_ref, k_ref, v_ref, pos_ref, cos_ref, sin_ref, qn_ref, kn_ref, qt_ref, kt_ref, vb_ref, mix_ref):
        def turned(value, gain):
            scale = lax.rsqrt(jnp.mean(value * value, 1, keepdims=True) + eps)
            return turn(value * scale * gain, cos_ref[...], sin_ref[...]).astype(jnp.bfloat16)

        kt_ref[...] = turned(k_ref[...], kn_ref[...])
        vb_ref[...] = v_ref[...].astype(jnp.bfloat16)
        for g in range(per_group):
            at = slice(g * size, (g + 1) * size)
            qt_ref[:, at] = turned(q_ref[:, at], qn_ref[...])
        for first, low, high in plan:
            span = slice(first, first + rows)
            allowed = band(rows, high - low, first, low, pos_ref[span, :])
            for g in range(per_group):
                at = slice(g * size, (g + 1) * size)
                scores = dot_nt(qt_ref[span, at], kt_ref[low:high, :]) * factor
                scores = jnp.where(allowed, scores, NEGATIVE)
                weights = jnp.exp(scores - jnp.max(scores, 1, keepdims=True))
                weights = (weights * (1.0 / jnp.sum(weights, 1, keepdims=True))).astype(jnp.bfloat16)
                mix_ref[span, at] = dot_nn(weights, vb_ref[low:high, :]).astype(jnp.bfloat16)

    group = per_group * size
    outs = tuple(shape_of((tokens, w), jnp.bfloat16) for w in (q_width, k_width, k_width, q_width))
    q_spec = pl.BlockSpec((tokens, group), lambda i, *_: (0, i))
    k_spec = pl.BlockSpec((tokens, size), lambda i, *_: (0, q_width // size + i))
    v_spec = pl.BlockSpec((tokens, size), lambda i, *_: (0, (q_width + k_width) // size + i))
    one = pl.BlockSpec((tokens, size), lambda i, *_: (0, i))
    operands = (raw, raw, raw, position, cos_wide, sin_wide, query_norm, key_norm)
    specs = [q_spec, k_spec, v_spec] + [whole_spec(a) for a in operands[3:]]
    flops = 20 * tokens * (high_sum(plan) * rows // tokens) * q_width
    return kernel_call(
        body, jnp.zeros((1,), jnp.int32), operands, specs, outs, (q_spec, one, one, q_spec), (kv_heads,), [], flops, 48
    )


def high_sum(plan):
    return sum(high - low for _, low, high in plan)


def attend_back(raw, turned_q, turned_k, values, grad_mixed, position, cos_wide, sin_wide, query_norm, key_norm, most, eps):
    tokens, q_width = turned_q.shape
    k_width = turned_k.shape[1]
    size = query_norm.shape[1]
    kv_heads, per_group = k_width // size, q_width // k_width
    factor = 1.0 / math.sqrt(size)
    rows, plan = attention_blocks(tokens, most)

    def body(_, q_ref, k_ref, qt_ref, kt_ref, v_ref, dm_ref, pos_ref, cos_ref, sin_ref, qn_ref, kn_ref,
             dq_ref, dk_ref, dv_ref, gain_ref, key_sum, value_sum):
        key_sum[...] = jnp.zeros_like(key_sum)
        value_sum[...] = jnp.zeros_like(value_sum)

        def back(raw_rows, gain, upstream, span):
            scale = lax.rsqrt(jnp.mean(raw_rows * raw_rows, 1, keepdims=True) + eps)
            turned_back = turn(upstream, cos_ref[span, :], -sin_ref[span, :])
            inner = jnp.mean(turned_back * gain * raw_rows, 1, keepdims=True)
            grad = scale * gain * turned_back - raw_rows * (scale * scale * scale * inner)
            return grad.astype(jnp.bfloat16), jnp.sum(turned_back * raw_rows * scale, 0, keepdims=True)

        query_gain = jnp.zeros((1, size), jnp.float32)
        for first, low, high in plan:
            span = slice(first, first + rows)
            allowed = band(rows, high - low, first, low, pos_ref[span, :])
            for g in range(per_group):
                at = slice(g * size, (g + 1) * size)
                queries, upstream = qt_ref[span, at], dm_ref[span, at]
                scores = dot_nt(queries, kt_ref[low:high, :]) * factor
                scores = jnp.where(allowed, scores, NEGATIVE)
                probs = jnp.exp(scores - jnp.max(scores, 1, keepdims=True))
                probs = probs * (1.0 / jnp.sum(probs, 1, keepdims=True))
                grads = dot_nt(upstream, v_ref[low:high, :])
                weighted = probs * grads
                total = jnp.sum(weighted, 1, keepdims=True)
                grads = (weighted - probs * total).astype(jnp.bfloat16)
                value_sum[low:high, :] += dot_tn(probs.astype(jnp.bfloat16), upstream)
                key_sum[low:high, :] += dot_tn(grads, queries)
                grad_turned = dot_nn(grads, kt_ref[low:high, :]) * factor
                grad, gain = back(q_ref[span, at], qn_ref[...], grad_turned, span)
                dq_ref[span, at] = grad
                query_gain = query_gain + gain
        grad, key_gain = back(k_ref[...], kn_ref[...], key_sum[...] * factor, slice(0, tokens))
        dk_ref[...] = grad
        dv_ref[...] = value_sum[...].astype(jnp.bfloat16)
        gain_ref[...] = jnp.concatenate([query_gain, key_gain, jnp.zeros((6, size), jnp.float32)], 0)

    group = per_group * size
    outs = (
        shape_of((tokens, q_width), jnp.bfloat16),
        shape_of((tokens, k_width), jnp.bfloat16),
        shape_of((tokens, k_width), jnp.bfloat16),
        shape_of((8 * kv_heads, size), jnp.float32),
    )
    q_spec = pl.BlockSpec((tokens, group), lambda i, *_: (0, i))
    k_spec = pl.BlockSpec((tokens, size), lambda i, *_: (0, q_width // size + i))
    one = pl.BlockSpec((tokens, size), lambda i, *_: (0, i))
    operands = (raw, raw, turned_q, turned_k, values, grad_mixed, position, cos_wide, sin_wide, query_norm, key_norm)
    specs = [q_spec, k_spec, q_spec, one, one, q_spec] + [whole_spec(a) for a in operands[6:]]
    out_specs = (q_spec, one, one, pl.BlockSpec((8, size), lambda i, *_: (i, 0)))
    scratch = [pltpu.VMEM((tokens, size), jnp.float32)] * 2
    flops = 28 * tokens * (high_sum(plan) * rows // tokens) * q_width
    return kernel_call(
        body, jnp.zeros((1,), jnp.int32), operands, specs, outs, out_specs, (kv_heads,), scratch, flops, 48
    )


def local(
    hidden_in,
    seq_lengths,
    attn_norm,
    w_query,
    key_weight,
    value_weight,
    query_norm,
    key_norm,
    w_output,
    ffwd_norm,
    w_gate,
    w_up,
    w_down,
    cotangent,
):
    low, f32 = jnp.bfloat16, jnp.float32
    tokens, part_width = hidden_in.shape
    full_width = part_width * lax.axis_size("col")
    head_size = query_norm.shape[0]
    q_width, k_width = w_query.shape[1], key_weight.shape[1]
    ring = Ring()
    place, plain_place, pair_place = ring.place, ring.plain_place, ring.pair_place
    steps, pairs, half = ring.half, ring.half, tokens // 2
    pair_order = jnp.arange(pairs, dtype=jnp.int32)
    chain = Chain()
    pin, run = chain.pin, chain.run

    def near(value):
        return swap(value, "col", 1)

    def far(value):
        return swap(value, "col", 2)

    qkv, hidden_in = pin(jnp.concatenate([w_query, key_weight, value_weight], 1), hidden_in)
    qkv = ring.inner_gather(qkv, 0)
    on, back = ring.send_on(qkv), ring.send_back(qkv)
    output_all = ring.gather_stack(ring.inner_gather(w_output, 1))
    hidden_far = far(hidden_in)
    gains = jnp.stack([attn_norm, ffwd_norm])
    gains_far = far(gains)
    behind, ahead = [], []
    on, back = pin(on, back)
    behind.append(on)
    ahead.append(back)
    on, back = ring.send_on(on), ring.send_back(back)
    hidden_far, gains_far = pin(hidden_far, gains_far)
    hidden_blocks = [hidden_in, hidden_far, near(hidden_in), near(hidden_far)]
    gains_near = near(gains)
    on, back, gains_near, gate, up = pin(on, back, gains_near, w_gate, w_up)
    behind.append(on)
    ahead.append(back)
    on, back = ring.send_on(on), ring.send_back(back)
    gate_up = [ring.inner_gather(w, 0) for w in (gate, up)]
    gate_up_mine = side_of(gate_up, 1, ring.parity)
    gate_up_got = ring.to_partner(side_of(gate_up, 1, 1 - ring.parity))
    gains_diagonal, gate_up_mine, *hidden_blocks = pin(near(gains_far), gate_up_mine, *hidden_blocks)
    position = tables(seq_lengths[0], tokens)[:, None]
    position, cos_wide, sin_wide, behind_order = pin(position, *rotary(position[:, 0], head_size), ring.behind)
    on, back = pin(on, back)
    behind.append(on)
    ahead.append(back)
    cut = on.shape[0] // 2
    on, back = ring.send_on(on[:cut]), ring.send_back(back[cut:])
    gate_up_got, output_all = pin(gate_up_got, output_all)
    gate_up_all = pair_gather(ring, run(above, gate_up_mine, gate_up_got))
    on, back = pin(on, back)
    qkv_all = [qkv, *behind, jnp.concatenate([on, back], 0), *ahead[::-1]]
    gains = jnp.stack([gains, gains_far, gains_near, gains_diagonal], 1).reshape(2, 1, full_width)

    down, upstream = pin(w_down, cotangent)
    down = [ring.inner_gather(down, 1)]
    down_mine = side_of(down, 0, ring.parity)
    down_got = ring.to_partner(side_of(down, 0, 1 - ring.parity))
    up_far, up_partner = far(upstream), ring.to_partner(upstream)
    turning = (position, cos_wide, sin_wide, query_norm[None, :], key_norm[None, :])
    residual = hidden_in.astype(f32)
    wide_one, factor_one, qkv_raw = run(
        lambda blocks, gain, weights: gather_norm_matmul(place, blocks, gain, weights, EPS), hidden_blocks, gains[0], qkv_all
    )
    turned_q, turned_k, values, mixed = run(
        lambda raw: attend(raw, *turning, q_width, k_width, MOST, EPS), qkv_raw
    )
    up_far, up_partner, down_got, down_mine = pin(up_far, up_partner, down_got, down_mine)
    own, to_far, to_near, to_diagonal = run(
        lambda left, weights: spread_product(plain_place, left, [weights], False), mixed, output_all
    )
    got_far, got_own = near(to_diagonal), near(to_near)
    up_near, up_diagonal = near(upstream), near(up_far)
    to_far, got_far = pin(to_far, got_far)
    attended = far(pin((to_far.astype(f32) + got_far).astype(low)))
    corner = far(pin(up_partner[:half])), ring.to_partner(up_far[half:])
    up_near, up_diagonal = pin(up_near, up_diagonal)
    upstream_wide = run(lambda *blocks: assemble(pair_place, blocks), upstream, up_far, up_near, up_diagonal)
    attended, own, got_own = pin(attended, own, got_own)

    middle = residual + own + got_own + attended
    middle, middle_low = pin(middle, middle.astype(low))
    mid_far, mid_partner = far(middle_low), ring.to_partner(middle_low)
    mid_near = near(middle_low)
    up_corner = pin(jnp.concatenate(pin(*corner), 0))
    up_partner_near, up_corner_near = near(up_partner), near(up_corner)
    down_unit = pin(jnp.concatenate([down_mine, down_got], 1))
    mid_near, up_partner_near, up_corner_near = pin(mid_near, up_partner_near, up_corner_near)
    upstream_other = run(lambda *blocks: assemble(pair_place, blocks), up_partner, up_corner, up_partner_near, up_corner_near)
    mid_far = pin(mid_far)
    mid_diagonal = near(mid_far)
    mid_diagonal, mid_partner = pin(mid_diagonal, mid_partner)
    corner = far(mid_partner[:half]), ring.to_partner(mid_far[half:])
    mid_partner_near = near(mid_partner)
    gate_up_all = pin(gate_up_all)
    down_all = pair_gather(ring, down_unit)

    def swish(blocks, gain, weights):
        return gather_swish(pair_place, blocks, gain, weights, EPS)

    normed, factor_two, gate, up, hidden = run(
        swish, [middle_low, mid_far, mid_near, mid_diagonal], gains[1], gate_up_all
    )
    mid_partner_near, *corner = pin(mid_partner_near, *corner)
    mid_corner = pin(jnp.concatenate(corner, 0))
    mid_corner_near = pin(near(mid_corner))
    normed_other, _, gate_other, up_other, hidden_other = run(
        swish, [mid_partner, mid_corner, mid_partner_near, mid_corner_near], gains[1], gate_up_all
    )
    down_grad = run(
        lambda *ops: weight_grad(ops[:2], ops[2:], pair_order, False), hidden, hidden_other, upstream_wide, upstream_other
    )
    down_grad = pair_sum(ring, down_grad)

    down_all = pin(down_all)

    def back_swish(wide, weights, gate_value, up_value):
        return swish_back(wide, [weights], gate_value, up_value)

    def spread_back(left, weights):
        return spread_product(pair_place, left, [weights], True)

    low_other, inner_other = run(back_swish, upstream_other, down_all, gate_other, up_other)
    own_other, far_other, near_other, diagonal_other = run(spread_back, low_other, gate_up_all)
    diagonal_other, near_other, inner_other = near(diagonal_other), near(near_other), ring.to_partner(pin(inner_other[:, 0]))
    low_mine, inner, diagonal_other, near_other, inner_other = run(
        back_swish, upstream_wide, down_all, gate, up, beside=(diagonal_other, near_other, inner_other)
    )
    corner = pin((pin(far_other).astype(f32) + diagonal_other).astype(low))
    from_far, from_partner = far(corner[:half]), ring.to_partner(corner[half:])
    inner = pin(inner[:, 0] + inner_other)
    inner_near = near(inner)
    own, to_far, to_near, to_diagonal, from_far, from_partner, inner_near = run(
        spread_back, low_mine, gate_up_all, beside=(from_far, from_partner, inner_near)
    )
    got_far, got_own = near(to_diagonal), near(to_near)
    inner = pin(inner + inner_near)
    inner_far = far(inner)
    to_partner = own_other.astype(f32) + near_other
    to_partner = jnp.concatenate([to_partner[:half] + from_far, to_partner[half:]], 0)
    to_far, got_far, to_partner = pin(to_far, got_far, to_partner.astype(low))
    to_partner = ring.to_partner(to_partner)
    to_far = to_far.astype(f32) + got_far
    to_far = jnp.concatenate([to_far[:half], to_far[half:] + from_partner], 0)
    own, got_own, to_far, inner_far = pin(own, got_own, to_far.astype(low), inner_far)
    from_far = far(to_far)
    gate_up_grad = run(
        lambda *ops: weight_grad(ops[:2], ops[2:], pair_order, True), normed, normed_other, low_mine, low_other
    )
    inner = (inner + inner_far)[:, None] / full_width
    own, got_own, from_partner, from_far, inner, down_grad, gate_up_grad = pin(
        own, got_own, to_partner, from_far, inner, down_grad, gate_up_grad
    )
    gate_up_grad = pair_sum(ring, gate_up_grad)

    def spread_down(left, weights):
        return spread_product(pair_place, left, [weights], False)

    grad_normed = own.astype(f32) + got_own + from_partner + from_far
    grad_middle = (
        cotangent.astype(f32)
        + factor_two * ffwd_norm * grad_normed
        - middle * (factor_two * factor_two * inner)
    )
    grad_middle, grad_low = pin(grad_middle, grad_middle.astype(low))
    grad_far, grad_near = far(grad_low), near(grad_low)
    down_got = ring.to_partner(pin(down_grad[:, down_grad.shape[1] // 2 :]))
    own_other, far_other, near_other, diagonal_other = run(spread_down, hidden_other, down_all)
    out_own, out_to_far, out_to_near, out_to_diagonal, grad_near, down_got = run(
        spread_down, hidden, down_all, beside=(grad_near, down_got)
    )
    near_other, diagonal_other = near(near_other), near(diagonal_other)
    grad_far = pin(grad_far)
    grad_diagonal = near(grad_far)
    near_other, diagonal_other, grad_diagonal, own_other, far_other = pin(
        near_other, diagonal_other, grad_diagonal, own_other, far_other
    )
    out_first, out_second = pin(
        (own_other.astype(f32) + near_other).astype(low), (far_other.astype(f32) + diagonal_other).astype(low)
    )
    out_first = ring.to_partner(out_first)
    out_got_own, out_got_far = near(out_to_near), near(out_to_diagonal)
    ffwd_gain = pin(jnp.sum(grad_normed * middle * factor_two, 0))

    middle_wide = run(lambda *blocks: assemble(place, blocks), grad_low, grad_far, grad_near, grad_diagonal)
    grad_mixed = run(lambda wide, weights: times_transposed(wide, [weights], behind_order), middle_wide, output_all)
    query_low, key_low, value_low, head_gains, out_first, out_got_own, out_got_far = run(
        lambda *ops: attend_back(*ops, *turning, MOST, EPS),
        qkv_raw,
        turned_q,
        turned_k,
        values,
        grad_mixed,
        beside=(out_first, out_got_own, out_got_far),
    )
    out_second = ring.to_partner(out_second)
    qkv_low = pin(jnp.concatenate([query_low, key_low, value_low], 1))

    def parts(*numbers, beside=()):
        order = jnp.array(numbers, jnp.int32)
        return run(
            lambda *ops: block_grads(ops[:2], ops[2:], order, ring.count), wide_one, middle_wide, qkv_low, mixed, beside=beside
        )

    def go(on, back, *beside):
        on, back, *beside = pin(on.astype(low), back.astype(low), *beside)
        return ring.send_on(on), ring.send_back(back), *beside

    first = parts(steps)
    cut = first.shape[1] // 2
    on, back = go(first[0, :cut], first[0, cut:])
    own_first, to_far, to_near, to_diagonal, inner, attn_gain = run(
        lambda left, weights, wide: spread_product(place, left, weights, True, wide, True), qkv_low, qkv_all, wide_one
    )
    got_far, got_own = near(to_diagonal), near(to_near)
    second, on, back = parts(steps + 1, steps - 1, beside=(on, back))
    on = jnp.concatenate([second[0, :cut] + on.astype(f32), second[0, cut:].astype(f32)], 0)
    back = jnp.concatenate([second[1, :cut].astype(f32), second[1, cut:] + back.astype(f32)], 0)
    on, back, got_far, got_own, to_far = go(on, back, got_far, got_own, to_far)
    to_far = pin((to_far.astype(f32) + got_far).astype(low))
    gain_keep, gain_send = attn_gain[:1, : full_width // 2], attn_gain[:1, full_width // 2 :]
    head_gains = jnp.sum(head_gains.reshape(-1, 8, head_size), 0)[:2].reshape(-1)
    sums = pin(jnp.concatenate([gain_send[0], head_gains, inner[:, 0]]))
    sums_got = pin(near(sums))
    both_gain = gain_keep[0] + sums_got[: full_width // 2]
    sums = pin(jnp.concatenate([both_gain[part_width:], (sums + sums_got)[full_width // 2 :]]))
    sums_got = far(sums)
    grad_far = far(to_far)
    sums_got, out_to_far, gate_up_grad = pin(sums_got, out_to_far, gate_up_grad)
    columns_here = gate_up_grad.shape[0] // 2
    gate_up_got = ring.to_partner(pin(gate_up_grad[columns_here:]))
    attn_gain = (both_gain[:part_width] + sums_got[:part_width]) / attn_norm
    rest = (sums + sums_got)[part_width:]
    inner = rest[2 * head_size :][:, None] / full_width
    sums = jnp.concatenate([attn_gain, ffwd_gain, rest[: 2 * head_size]])
    sums, inner = pin(sums, inner)
    bits = [1 << n for n in range(lax.axis_size("row").bit_length() - 1)]
    sums_got = swap(sums, "row", bits[0])
    own, out_second = parts(*(n for s in range(2, steps) for n in (steps + s, steps - s)), 0, beside=(out_second,))
    on, back, sums_got = pin(on, back, sums_got)
    on, back = go(own[0] + on.astype(f32), own[1] + back.astype(f32))
    sums = pin(sums + sums_got)
    sums_got = swap(sums, "row", bits[1])
    grad_far = pin(grad_far)
    to_far = (out_to_far.astype(f32) + out_got_far + out_second).astype(low)
    hidden_grad = (
        grad_middle
        + factor_one * attn_norm * (own_first.astype(f32) + got_own + grad_far)
        - residual * (factor_one * factor_one * inner)
    )
    hidden_grad, to_far = pin(hidden_grad, to_far)
    out_far = far(to_far)
    on, back, sums_got = pin(on, back, sums_got)
    gate_up_got = pin(gate_up_got)
    on, back = go(own[2] + on.astype(f32), own[3] + back.astype(f32))
    sums = pin(sums + sums_got)
    for bit in bits[2:-1]:
        sums = pin(sums + pin(swap(sums, "row", bit)))
    sums_got = swap(sums, "row", bits[-1])
    gate_up_grad, gate_up_got, down_got = pin(gate_up_grad, gate_up_got, down_got)
    gate_grad, up_grad = (
        pair_join(ring, gate_up_grad[:columns_here, at], gate_up_got[:, at], 1)
        for at in (slice(0, gate_up_grad.shape[1] // 2), slice(gate_up_grad.shape[1] // 2, None))
    )
    down_out = pair_join(ring, down_grad[:, : down_grad.shape[1] // 2], down_got, 0)
    gate_grad, up_grad, down_out = pin(gate_grad, up_grad, down_out)
    out_far = pin(out_far)
    hidden_out = pin((middle + out_own + out_got_own + out_first + out_far).astype(low))
    on, back, sums_got = pin(on, back, sums_got)
    sums = sums + sums_got
    total = ring.inner_sum(own[4].astype(f32) + on + back, 0)
    attn_gain, ffwd_gain, query_gain, key_gain = jnp.split(
        sums, [part_width, 2 * part_width, 2 * part_width + head_size]
    )
    return (
        hidden_out,
        hidden_grad,
        attn_gain,
        total[:, :q_width],
        total[:, q_width : q_width + k_width],
        total[:, q_width + k_width : q_width + 2 * k_width],
        query_gain,
        key_gain,
        total[:, q_width + 2 * k_width :].T,
        ffwd_gain,
        gate_grad,
        up_grad,
        down_out,
    )


def solution(mesh):
    in_specs = (
        P("row", "col"),
        P("row", None),
        P("col"),
        P("row", "col"),
        P("row", "col"),
        P("row", "col"),
        P(),
        P(),
        P("col", "row"),
        P("col"),
        P("row", "col"),
        P("row", "col"),
        P("col", "row"),
        P("row", "col"),
    )
    out_specs = (
        P("row", "col"),
        P("row", "col"),
        P("col"),
        P("row", "col"),
        P("row", "col"),
        P("row", "col"),
        P(),
        P(),
        P("col", "row"),
        P("col"),
        P("row", "col"),
        P("row", "col"),
        P("col", "row"),
    )
    return jax.shard_map(local, mesh=mesh, in_specs=in_specs, out_specs=out_specs, check_vma=False)
```
